256 devices in a mesh: patch: 32 (over z, y), lev: 8 (over x, core).
Axes of the slice: x: 4, y: 4, z: 8, core: 2. Of those that a mesh axis runs over, the one named last changes fastest.
Arguments:
- node_state: bfloat16 [8192, 16, 192], P('patch', 'lev'), may hold values from -6 to 6
- edge_attr: bfloat16 [65536, 192], P('patch'), may hold values from -6 to 6
- edge_sender: int32 [65536], P('patch'), may hold values from 0 to 1791, as said below
- edge_receiver: int32 [65536], P('patch'), may hold values from -1 to 127, as said below
- tile_block: int32 [512], P('patch'), may hold values from 0 to 1
- halo_rows: int32 [1024, 48], P('patch'), may hold values from 0 to 255
- valid_levels: int32 [8192], P('patch'), may hold values from 12 to 16
- edge_w_in: bfloat16 [576, 192], replicated, may hold values from -0.25 to 0.25
- edge_bias: float32 [192], replicated, may hold values from -3 to 3
- edge_w_out: bfloat16 [192, 192], replicated, may hold values from -0.4375 to 0.4375
- node_w_in: bfloat16 [384, 192], replicated, may hold values from -0.3125 to 0.3125
- node_bias: float32 [192], replicated, may hold values from -3 to 3
- node_w_out: bfloat16 [192, 192], replicated, may hold values from -0.4375 to 0.4375
- node_gain: float32 [192], replicated, may hold values from 0.1 to 1.9
- attention_gain: float32 [192], replicated, may hold values from 0.1 to 1.9
- query_weight: bfloat16 [192, 192], replicated, may hold values from -12.268693 to 12.268693
- key_weight: bfloat16 [192, 192], replicated, may hold values from -0.28867513 to 0.28867513
- value_weight: bfloat16 [192, 192], replicated, may hold values from -0.4375 to 0.4375
- output_weight: bfloat16 [192, 192], replicated, may hold values from -0.4375 to 0.4375
Outputs:
- column_state: bfloat16 [8192, 16, 192], P('patch', 'lev')
The draws below stay inside these ranges and needn't reach their ends.
Inputs may be any that keep to these rules, and one draw needn't show every extreme that they name: `edge_sender`: rows of a table below 256 are the patch's own nodes; row 256 + q * 48 + s is slot s of what patch q sends it. Empty edge slots hold 0. Slots of a send list that no edge reads may name any row. `edge_receiver`: empty slots fill whole tiles at the end of a patch's tiles; patches have from half of their 16 tiles to all of them in use, and some patch uses all.
All inputs are finite; a program needn't handle non-finite values.
Results may differ from the reference program's by a relative error of at most 0.008.
Values may be sent and summed in bfloat16 or wider, within the bound.
No kernel may reach another device: no remote copies, remote signals or barrier semaphores. Data moves between devices by JAX's collectives and lax.ppermute only.
A program may use at most 64 MiB of HBM per device.

```python
import math
import jax
import jax.numpy as jnp
from jax import lax

D = 192
HEADS = 4
NODE_DEV = 256
SLOT = 48
TILE_DEV = 16
EDGE_DEV = 2048
LEVELS = 16
NODES = 8192
EDGES = 65536
N_PATCH = 32


def graph_tables(key):
    patch_total = NODES // NODE_DEV
    block_total = NODE_DEV // 128
    key_list = jax.random.split(key, 11)
    patch_ids = jnp.arange(patch_total, dtype=jnp.int32)
    counts = jax.random.randint(key_list[0], (patch_total, patch_total), SLOT // 4, SLOT + 1)
    full_source = (patch_ids + jax.random.randint(key_list[1], (patch_total,), 1, patch_total)) % patch_total
    counts = counts.at[full_source, patch_ids].set(SLOT)
    counts = counts.at[patch_ids, patch_ids].set(0)
    counts = counts.at[patch_total - 1, 0].set(SLOT)
    halo_table = jax.random.randint(key_list[2], (patch_total, patch_total, SLOT), 0, NODE_DEV)
    halo_table = halo_table.at[patch_total - 1, 0, SLOT - 1].set(NODE_DEV - 1).at[patch_total - 1, 0, 0].set(0)
    used_tiles = jax.random.randint(key_list[3], (patch_total,), TILE_DEV // 2, TILE_DEV + 1)
    busiest = jax.random.randint(key_list[4], (), 0, patch_total)
    used_tiles = used_tiles.at[busiest].set(TILE_DEV).at[(busiest + 1) % patch_total].set(TILE_DEV // 2)
    live_tiles = jnp.arange(TILE_DEV, dtype=jnp.int32)[None, :] < used_tiles[:, None]
    block_ids = jax.random.randint(key_list[5], (patch_total, TILE_DEV), 0, block_total)
    edge_shape = (patch_total, TILE_DEV, 128)
    receivers = jax.random.randint(key_list[6], edge_shape, 0, 128)
    receivers = jnp.where(live_tiles[:, :, None], receivers, -1)
    receivers = receivers.at[0, 0, 0].set(127)
    local_rows = jax.random.randint(key_list[7], edge_shape, 0, NODE_DEV)
    source = (patch_ids[:, None, None] + jax.random.randint(key_list[8], edge_shape, 1, patch_total)) % patch_total
    slot_limit = counts[source, jnp.broadcast_to(patch_ids[:, None, None], edge_shape)]
    slot_pick = jax.random.randint(key_list[9], edge_shape, 0, slot_limit)
    remote_rows = NODE_DEV + source * SLOT + slot_pick
    local_pick = jax.random.randint(key_list[10], edge_shape, 0, 10) < 7
    senders = jnp.where(local_pick, local_rows, remote_rows)
    senders = jnp.where(live_tiles[:, :, None], senders, 0)
    senders = senders.at[0, 0, 0].set(NODE_DEV + (patch_total - 1) * SLOT + SLOT - 1)
    return (senders.reshape(-1), receivers.reshape(-1), block_ids.reshape(-1), halo_table.reshape(patch_total * patch_total, SLOT))


def draw_edge_sender(key, part):
    tables = graph_tables(key)
    return tables[0].astype(jnp.int32)


def draw_edge_receiver(key, part):
    tables = graph_tables(key)
    return tables[1].astype(jnp.int32)


def draw_tile_block(key, part):
    tables = graph_tables(key)
    return tables[2].astype(jnp.int32)


def draw_halo_rows(key, part):
    tables = graph_tables(key)
    return tables[3].astype(jnp.int32)


def attention_base(key):
    return jnp.clip(jax.random.normal(key, (D, D), jnp.float32), -3.98, 3.98) / math.sqrt(D)


def draw_key_weight(key, part):
    base_matrix = attention_base(key)
    return base_matrix.astype(jnp.bfloat16)


def draw_query_weight(key, part):
    key = jax.random.fold_in(key, 6)
    first_key = jax.random.fold_in(key, 0)
    fresh_matrix = jnp.clip(jax.random.normal(first_key, (D, D), jnp.float32), -3.98, 3.98) / math.sqrt(D)
    return fresh_matrix.astype(jnp.bfloat16)


def with_ends(entries, own_key, low, top_value):
    shape = entries.shape
    spot = [jax.random.randint(jax.random.fold_in(own_key, axis), (), 0, shape[axis]) for axis in range(len(shape))]
    entries = entries.at[tuple(spot)].set(low)
    longest = shape.index(max(shape))
    spot[longest] = (spot[longest] + 1) % shape[longest]
    return entries.at[tuple(spot)].set(top_value)


def level_of(stream_key, shape, cuts, smallest, high):
    loudness = 1.0
    for position, shards_of in cuts:
        steps = jax.random.uniform(jax.random.fold_in(jax.random.fold_in(stream_key, 6), position), (shards_of,), jnp.float32, smallest / len(cuts), high / len(cuts))
        loudness = loudness * jnp.repeat(jnp.exp(steps), shape[position] // shards_of).reshape((-1,) + (1,) * (len(shape) - 1 - position))
    return loudness


def gaussian(own_key, shape, scale, most, cuts=(), held_as=jnp.bfloat16):
    entries = jax.random.normal(own_key, shape, jnp.float32) * scale
    if len(cuts) > 0:
        entries = level_of(own_key, shape, cuts, -0.22, 0.18) * entries
    return jnp.clip(entries, min=-most, max=most).astype(held_as)


def setup_inputs(seed: int = 0) -> dict:
    keys = jax.random.split(jax.random.key(seed), 20)
    return {
        "node_state": gaussian(keys[0], (NODES, LEVELS, D), 1.0, 6.0, ((0, 32), (1, 8))),
        "edge_attr": gaussian(keys[1], (EDGES, D), 1.0, 6.0, ((0, 32),)),
        "edge_sender": draw_edge_sender(jax.random.fold_in(keys[19], 71), 0),
        "edge_receiver": draw_edge_receiver(jax.random.fold_in(keys[19], 71), 0),
        "tile_block": draw_tile_block(jax.random.fold_in(keys[19], 71), 0),
        "halo_rows": draw_halo_rows(jax.random.fold_in(keys[19], 71), 0),
        "valid_levels": with_ends(jax.random.randint(keys[6], (NODES,), LEVELS - LEVELS // 4, LEVELS + 1), jax.random.fold_in(keys[6], 1), LEVELS - LEVELS // 4, LEVELS).astype(jnp.int32),
        "edge_w_in": gaussian(keys[7], (3 * D, D), (3 * D) ** -0.5, 0.25),
        "edge_bias": gaussian(keys[8], (D,), 0.5, 3.0, (), jnp.float32),
        "edge_w_out": gaussian(keys[9], (D, D), D ** -0.5, 0.4375),
        "node_w_in": gaussian(keys[10], (2 * D, D), (2 * D) ** -0.5, 0.3125),
        "node_bias": gaussian(keys[11], (D,), 0.5, 3.0, (), jnp.float32),
        "node_w_out": gaussian(keys[12], (D, D), D ** -0.5, 0.4375),
        "node_gain": jnp.clip(1.0 + 0.18 * jax.random.normal(keys[13], (D,), jnp.float32), 0.1, 1.9),
        "attention_gain": jnp.clip(1.0 + 0.18 * jax.random.normal(keys[14], (D,), jnp.float32), 0.1, 1.9),
        "query_weight": draw_query_weight(jax.random.fold_in(keys[19], 71), 0),
        "key_weight": draw_key_weight(jax.random.fold_in(keys[19], 71), 0),
        "value_weight": gaussian(keys[17], (D, D), D ** -0.5, 0.4375),
        "output_weight": gaussian(keys[18], (D, D), D ** -0.5, 0.4375),
    }


def normalize(values):
    centered = values - lax.optimization_barrier(jnp.mean(values, axis=-1, keepdims=True))
    spread = lax.optimization_barrier(jnp.mean(centered * centered, axis=-1, keepdims=True))
    return centered * lax.rsqrt(spread + 1e-05)

def column_attention(queries, key_rows, value_rows, key_live):
    node_count, query_levels, model_width = queries.shape
    key_levels = key_rows.shape[1]
    head_width = model_width // HEADS
    query_heads = queries.astype(jnp.float32).reshape(node_count, query_levels, HEADS, head_width)
    key_heads = key_rows.astype(jnp.float32).reshape(node_count, key_levels, HEADS, head_width)
    value_heads = value_rows.astype(jnp.float32).reshape(node_count, key_levels, HEADS, head_width)
    scores = jnp.einsum('nlhd,nmhd->nhlm', query_heads, key_heads) * (1.0 / math.sqrt(head_width))
    scores = jnp.where(key_live[:, None, None, :], scores, -1e+30)
    weights = jax.nn.softmax(scores, axis=-1).astype(jnp.bfloat16)
    attended = jnp.einsum('nhlm,nmhd->nlhd', weights.astype(jnp.float32), value_heads)
    return attended.astype(jnp.bfloat16).reshape(node_count, query_levels, model_width)

def reference(node_state, edge_attr, edge_sender, edge_receiver, tile_block, halo_rows, valid_levels, edge_w_in, edge_bias, edge_w_out, node_w_in, node_bias, node_w_out, node_gain, attention_gain, query_weight, key_weight, value_weight, output_weight):
    patch_states = node_state.reshape(N_PATCH, NODE_DEV, LEVELS, D)
    send_lists = halo_rows.reshape(N_PATCH, N_PATCH, SLOT)
    patch_ids = jnp.arange(N_PATCH, dtype=jnp.int32)

    def patch_levels(inputs):
        patch_index, senders, in_block, block_ids, attributes = inputs
        own_rows = patch_states[patch_index]
        remote_rows = patch_states[patch_ids[:, None], send_lists[:, patch_index, :]].reshape(N_PATCH * SLOT, LEVELS, D)
        node_table = jnp.concatenate([own_rows, remote_rows], axis=0)
        live_edge = in_block >= 0
        receiver = block_ids[:, None] * 128 + in_block
        receiver_index = jnp.where(live_edge, receiver, 0).reshape(-1)
        segment_index = jnp.where(live_edge, receiver, NODE_DEV).reshape(-1)
        edge_base = jnp.dot(attributes, edge_w_in[2 * D:], preferred_element_type=jnp.float32) + edge_bias

        def one_level(level_pair):
            table_level, own_level = level_pair
            sender_proj = jnp.dot(table_level, edge_w_in[:D], preferred_element_type=jnp.float32)
            receiver_proj = jnp.dot(own_level, edge_w_in[D:2 * D], preferred_element_type=jnp.float32)
            edge_pre = sender_proj[senders] + receiver_proj[receiver_index] + edge_base
            edge_hidden = jax.nn.silu(edge_pre).astype(jnp.bfloat16)
            message = jnp.dot(edge_hidden, edge_w_out, preferred_element_type=jnp.float32).astype(jnp.bfloat16)
            summed = jax.ops.segment_sum(message.astype(jnp.float32), segment_index, num_segments=NODE_DEV + 1)[:NODE_DEV]
            summed = summed.astype(jnp.bfloat16)
            node_pre = jnp.dot(own_level, node_w_in[:D], preferred_element_type=jnp.float32) + jnp.dot(summed, node_w_in[D:], preferred_element_type=jnp.float32) + node_bias
            node_hidden = jax.nn.silu(node_pre).astype(jnp.bfloat16)
            update = jnp.dot(node_hidden, node_w_out, preferred_element_type=jnp.float32)
            return (own_level.astype(jnp.float32) + node_gain * normalize(update)).astype(jnp.bfloat16)
        per_level = lax.map(one_level, (jnp.swapaxes(node_table, 0, 1), jnp.swapaxes(own_rows, 0, 1)))
        return jnp.swapaxes(per_level, 0, 1)
    level_state = lax.map(patch_levels, (patch_ids, edge_sender.reshape(N_PATCH, EDGE_DEV), edge_receiver.reshape(N_PATCH, TILE_DEV, 128), tile_block.reshape(N_PATCH, TILE_DEV), edge_attr.reshape(N_PATCH, EDGE_DEV, D)))

    def patch_columns(inputs):
        states_now, counts = inputs
        normed = (attention_gain * normalize(states_now.astype(jnp.float32))).astype(jnp.bfloat16)
        flat_rows = normed.reshape(NODE_DEV * LEVELS, D)
        queries = jnp.dot(flat_rows, query_weight, preferred_element_type=jnp.float32).astype(jnp.bfloat16).reshape(NODE_DEV, LEVELS, D)
        key_rows = jnp.dot(flat_rows, key_weight, preferred_element_type=jnp.float32).astype(jnp.bfloat16).reshape(NODE_DEV, LEVELS, D)
        value_rows = jnp.dot(flat_rows, value_weight, preferred_element_type=jnp.float32).astype(jnp.bfloat16).reshape(NODE_DEV, LEVELS, D)
        level_live = jnp.arange(LEVELS, dtype=jnp.int32)[None, :] < counts[:, None]
        attended = column_attention(queries, key_rows, value_rows, level_live)
        mixed_rows = jnp.dot(attended.reshape(NODE_DEV * LEVELS, D), output_weight, preferred_element_type=jnp.float32).reshape(NODE_DEV, LEVELS, D)
        return (states_now.astype(jnp.float32) + jnp.where(level_live[:, :, None], mixed_rows, 0.0)).astype(jnp.bfloat16)
    result = lax.map(patch_columns, (level_state, valid_levels.reshape(N_PATCH, NODE_DEV)))
    return result.reshape(NODES, LEVELS, D)
```

```python
import math

import jax
import jax.numpy as jnp
from jax import lax
from jax.experimental import pallas as pl
from jax.experimental.pallas import tpu as pltpu
from jax.sharding import PartitionSpec as P

HEADS = 4
BF16 = jnp.bfloat16
F32 = jnp.float32
VMEM_BYTES = 48 * 1024 * 1024


def dot(a, b):
    return jnp.dot(a, b, preferred_element_type=F32)


def silu(v):
    return v / (1.0 + jnp.exp(-v))


def normalize(values):
    centered = values - jnp.mean(values, axis=-1, keepdims=True)
    spread = jnp.mean(centered * centered, axis=-1, keepdims=True)
    return centered * lax.rsqrt(spread + 1e-05)


def onehot(column, width):
    lanes = lax.broadcasted_iota(jnp.int32, (column.shape[0], width), 1).astype(F32)
    return jnp.where(column == lanes, 1.0, 0.0).astype(BF16)


def level_pair(merged, weight):
    depth, width = weight.shape
    half = merged.shape[1] // 2
    cut = half // 128 * 128
    filler = jnp.zeros((half - cut, width), weight.dtype)
    first = jnp.concatenate([weight, filler], axis=0)
    second = jnp.concatenate([filler, weight], axis=0)
    return (
        dot(merged[:, : half + half - cut], first),
        dot(merged[:, cut:], second),
    )


def merge_levels(first, second):
    return jnp.concatenate([first, second], axis=1)


def halo_kernel(halo_ref, own_ref, out_ref, pick_ref):
    patch_count, slot_count = halo_ref.shape
    columns = halo_ref[...].astype(F32).T
    for patch in range(patch_count):
        pick_ref[patch * slot_count : (patch + 1) * slot_count, :] = onehot(
            columns[:, patch : patch + 1], own_ref.shape[0]
        )
    out_ref[...] = dot(pick_ref[...], own_ref[...]).astype(BF16)


def local_kernel(
    sender_ref, receiver_ref, attr_ref, own_ref, w_in_ref, bias_ref, pre0_ref, pre1_ref, deliver_ref
):
    tile_count, tile = sender_ref.shape
    width = attr_ref.shape[1]
    node_dev = own_ref.shape[0]
    own = own_ref[...]
    sender_columns = sender_ref[...].astype(F32).T
    receiver_columns = receiver_ref[...].astype(F32).T
    w_send = w_in_ref[0:width, :]
    w_recv = w_in_ref[width : 2 * width, :]
    w_attr = w_in_ref[2 * width : 3 * width, :]
    for index in range(tile_count):
        rows = slice(index * tile, (index + 1) * tile)
        base = dot(attr_ref[rows, :], w_attr) + bias_ref[...]
        send_rows = dot(onehot(sender_columns[:, index : index + 1], node_dev), own).astype(BF16)
        recv_rows = dot(onehot(receiver_columns[:, index : index + 1], node_dev), own).astype(BF16)
        send0, send1 = level_pair(send_rows, w_send)
        recv0, recv1 = level_pair(recv_rows, w_recv)
        pre0_ref[rows, :] = base + send0 + recv0
        pre1_ref[rows, :] = base + send1 + recv1
        nodes = lax.broadcasted_iota(jnp.int32, (node_dev, tile), 0)
        deliver_ref[:, rows] = jnp.where(
            nodes == receiver_ref[index : index + 1, :], 1.0, 0.0
        ).astype(BF16)


def edge_kernel(
    sender_ref,
    pre0_ref,
    pre1_ref,
    deliver_ref,
    remote_ref,
    own_ref,
    w_in_ref,
    w_out_ref,
    node_w_in_ref,
    node_bias_ref,
    node_w_out_ref,
    node_gain_ref,
    attention_gain_ref,
    state_ref,
    normed_ref,
    message0_ref,
    message1_ref,
):
    tile_count, tile = sender_ref.shape
    node_dev = own_ref.shape[0]
    width = w_out_ref.shape[0]
    remote = remote_ref[...]
    w_send = w_in_ref[0:width, :]
    w_out = w_out_ref[...]
    columns = (sender_ref[...] - node_dev).astype(F32).T
    for index in range(tile_count):
        rows = slice(index * tile, (index + 1) * tile)
        send_rows = dot(
            onehot(columns[:, index : index + 1], remote.shape[0]), remote
        ).astype(BF16)
        send0, send1 = level_pair(send_rows, w_send)
        hidden0 = silu(pre0_ref[rows, :] + send0).astype(BF16)
        hidden1 = silu(pre1_ref[rows, :] + send1).astype(BF16)
        message0_ref[rows, :] = dot(hidden0, w_out).astype(BF16)
        message1_ref[rows, :] = dot(hidden1, w_out).astype(BF16)
    deliver = deliver_ref[...]
    own = own_ref[...]
    own_pair = level_pair(own, node_w_in_ref[0:width, :])
    own_values = (own[:, :width], own[:, width:])
    states = []
    normed = []
    for level, message_ref in enumerate((message0_ref, message1_ref)):
        summed = dot(deliver, message_ref[...]).astype(BF16)
        node_pre = (
            own_pair[level] + dot(summed, node_w_in_ref[width : 2 * width, :]) + node_bias_ref[...]
        )
        update = dot(silu(node_pre).astype(BF16), node_w_out_ref[...])
        state = (
            own_values[level].astype(F32) + node_gain_ref[...] * normalize(update)
        ).astype(BF16)
        states.append(state)
        normed.append(
            (attention_gain_ref[...] * normalize(state.astype(F32))).astype(BF16)
        )
    state_ref[...] = merge_levels(*states)
    normed_ref[...] = merge_levels(*normed)


def attention_kernel(
    rows_ref, bias_ref, query_ref, key_ref, value_ref, out_ref
):
    group_count, item_count, merged = rows_ref.shape
    width = merged // 2
    head_width = width // HEADS
    scale = 1.0 / math.sqrt(head_width)
    chunk = 16
    half = group_count * chunk
    total = 2 * half
    head_of = lax.broadcasted_iota(jnp.int32, (1, width), 1) // head_width
    row_node = lax.broadcasted_iota(jnp.int32, (total, total), 0) % chunk
    col_node = lax.broadcasted_iota(jnp.int32, (total, total), 1) % chunk
    same_node = row_node == col_node
    for part in range(item_count // chunk):
        items = slice(part * chunk, (part + 1) * chunk)
        merged_rows = rows_ref[:, items, :].reshape(half, merged)

        def project(weight_ref):
            pair = level_pair(merged_rows, weight_ref[...])
            return jnp.concatenate([p.astype(BF16) for p in pair], axis=0)

        queries, keys, values = project(query_ref), project(key_ref), project(value_ref)
        bias = jnp.where(same_node, bias_ref[part], -1e30)
        attended = jnp.zeros((total, width), F32)
        for head in range(HEADS):
            in_head = head_of == head
            head_keys = jnp.where(in_head, keys, 0.0).astype(BF16)
            head_values = jnp.where(in_head, values, 0.0).astype(BF16)
            scores = lax.dot_general(
                queries, head_keys, (((1,), (1,)), ((), ())), preferred_element_type=F32
            )
            scores = scores * scale + bias
            powers = jnp.exp(scores - jnp.max(scores, axis=-1, keepdims=True))
            weights = powers / jnp.sum(powers, axis=-1, keepdims=True)
            attended = attended + dot(weights.astype(BF16), head_values)
        attended = attended.astype(BF16)
        out_ref[:, items, :] = merge_levels(attended[:half], attended[half:]).reshape(
            group_count, chunk, merged
        )


def output_kernel(state_ref, attended_ref, live_ref, weight_ref, out_ref):
    width = weight_ref.shape[0]
    mixed = level_pair(attended_ref[...], weight_ref[...])
    state = state_ref[...].astype(F32)
    for level in range(2):
        kept = mixed[level] * live_ref[:, level : level + 1]
        out_ref[level] = (state[:, level * width : (level + 1) * width] + kept).astype(BF16)


def call(kernel, out_shape, *operands, scratch=()):
    return pl.pallas_call(
        kernel,
        out_shape=out_shape,
        scratch_shapes=list(scratch),
        compiler_params=pltpu.CompilerParams(vmem_limit_bytes=VMEM_BYTES),
    )(*operands)


def shape(dims, dtype=BF16):
    return jax.ShapeDtypeStruct(dims, dtype)


def per_device(
    node_state,
    edge_attr,
    edge_sender,
    edge_receiver,
    tile_block,
    halo_rows,
    valid_levels,
    edge_w_in,
    edge_bias,
    edge_w_out,
    node_w_in,
    node_bias,
    node_w_out,
    node_gain,
    attention_gain,
    query_weight,
    key_weight,
    value_weight,
    output_weight,
):
    group_count = lax.axis_size("lev")
    node_dev, lev_dev, width = node_state.shape
    tile_count = tile_block.shape[0]
    patch_count, slot_count = halo_rows.shape
    merged = lev_dev * width
    own = node_state.reshape(node_dev, merged)
    outgoing = call(
        halo_kernel,
        shape((patch_count * slot_count, merged)),
        halo_rows,
        own,
        scratch=[pltpu.VMEM((patch_count * slot_count, node_dev), BF16)],
    )
    incoming = lax.all_to_all(
        outgoing.reshape(patch_count, slot_count, merged),
        "patch",
        split_axis=0,
        concat_axis=0,
        tiled=True,
    ).reshape(patch_count * slot_count, merged)

    senders = edge_sender.reshape(tile_count, 128)
    in_block = edge_receiver.reshape(tile_count, 128)
    receivers = jnp.where(in_block >= 0, tile_block[:, None] * 128 + in_block, -1)
    edge_count = edge_attr.shape[0]
    pre0, pre1, deliver = call(
        local_kernel,
        (
            shape((edge_count, width), F32),
            shape((edge_count, width), F32),
            shape((node_dev, edge_count)),
        ),
        senders,
        receivers,
        edge_attr,
        own,
        edge_w_in,
        edge_bias[None, :],
    )
    state, normed = call(
        edge_kernel,
        (shape((node_dev, merged)), shape((node_dev, merged))),
        senders,
        pre0,
        pre1,
        deliver,
        incoming,
        own,
        edge_w_in,
        edge_w_out,
        node_w_in,
        node_bias[None, :],
        node_w_out,
        node_gain[None, :],
        attention_gain[None, :],
        scratch=[
            pltpu.VMEM((edge_count, width), BF16),
            pltpu.VMEM((edge_count, width), BF16),
        ],
    )
    per_group = node_dev // group_count
    chunk = 16
    me = lax.axis_index("lev")
    mine = lax.dynamic_slice_in_dim(valid_levels, me * per_group, per_group)
    level_of = (
        jnp.arange(group_count, dtype=jnp.int32)[None, :, None] * lev_dev
        + jnp.arange(lev_dev, dtype=jnp.int32)[:, None, None]
    )
    key_bias = jnp.where(
        level_of[None] < mine.reshape(per_group // chunk, 1, 1, chunk), 0.0, -1e30
    ).reshape(per_group // chunk, 1, lev_dev * group_count * chunk)
    columns = lax.all_to_all(
        normed.reshape(group_count, per_group, merged),
        "lev",
        split_axis=0,
        concat_axis=0,
        tiled=True,
    )
    attended = call(
        attention_kernel,
        shape((group_count, per_group, merged)),
        columns,
        key_bias,
        query_weight,
        key_weight,
        value_weight,
    )
    returned = lax.all_to_all(
        attended, "lev", split_axis=0, concat_axis=0, tiled=True
    ).reshape(node_dev, merged)
    levels = me * lev_dev + jnp.arange(lev_dev, dtype=jnp.int32)
    live = (levels[None, :] < valid_levels[:, None]).astype(F32)
    out = call(
        output_kernel,
        shape((lev_dev, node_dev, width)),
        state,
        returned,
        live,
        output_weight,
    )
    return out.transpose(1, 0, 2)


def solution(mesh):
    in_specs = (
        P("patch", "lev", None),
        P("patch", None),
        P("patch"),
        P("patch"),
        P("patch"),
        P("patch", None),
        P("patch"),
    ) + (P(),) * 12
    out_specs = P("patch", "lev", None)
    return jax.shard_map(
        per_device, mesh=mesh, in_specs=in_specs, out_specs=out_specs, check_vma=False
    )
```

```python
import math

import jax
import jax.numpy as jnp
from jax import lax
from jax.experimental import pallas as pl
from jax.experimental.pallas import tpu as pltpu
from jax.sharding import PartitionSpec as P

HEADS = 4
BF16 = jnp.bfloat16
F32 = jnp.float32
VMEM_BYTES = 60 * 1024 * 1024
LATE_TILES = 6
LATE_STEP = 2


def dot(a, b):
    return jnp.dot(a, b, preferred_element_type=F32)


def dot_lanes(a, b):
    return lax.dot_general(a, b, (((1,), (1,)), ((), ())), preferred_element_type=F32)


def silu(v):
    return v / (1.0 + jnp.exp(-v))


def normalize(values):
    centered = values - jnp.mean(values, axis=-1, keepdims=True)
    spread = jnp.mean(centered * centered, axis=-1, keepdims=True)
    return centered * lax.rsqrt(spread + 1e-05)


def onehot(column, width):
    lanes = lax.broadcasted_iota(jnp.int32, (column.shape[0], width), 1).astype(F32)
    return jnp.where(column == lanes, 1.0, 0.0).astype(BF16)


def level_pair(merged, weight):
    depth, width = weight.shape
    half = merged.shape[1] // 2
    cut = half // 128 * 128
    filler = jnp.zeros((half - cut, width), weight.dtype)
    first = jnp.concatenate([weight, filler], axis=0)
    second = jnp.concatenate([filler, weight], axis=0)
    return (
        dot(merged[:, : half + half - cut], first),
        dot(merged[:, cut:], second),
    )


def merge_levels(first, second):
    return jnp.concatenate([first, second], axis=1)


def halo_kernel(halo_ref, own_ref, out_ref, pick_ref):
    patch_count, slot_count = halo_ref.shape
    columns = halo_ref[...].astype(F32).T
    for patch in range(patch_count):
        pick_ref[patch * slot_count : (patch + 1) * slot_count, :] = onehot(
            columns[:, patch : patch + 1], own_ref.shape[1]
        )
    out_ref[...] = dot_lanes(pick_ref[...], own_ref[...]).astype(BF16)


def running_count(flags):
    tile_count, tile = flags.shape
    flags = flags.astype(BF16)
    before = lax.broadcasted_iota(jnp.int32, (tile, tile), 0) < lax.broadcasted_iota(
        jnp.int32, (tile, tile), 1
    )
    above = lax.broadcasted_iota(jnp.int32, (tile_count, tile_count), 1) < lax.broadcasted_iota(
        jnp.int32, (tile_count, tile_count), 0
    )
    inside = dot(flags, jnp.where(before, 1.0, 0.0).astype(BF16))
    totals = dot(flags, jnp.ones((tile, tile), BF16)).astype(BF16)
    return (
        inside + dot(jnp.where(above, 1.0, 0.0).astype(BF16), totals),
        dot(jnp.ones((tile_count, tile_count), BF16), totals),
    )


def local_kernel(
    sender_ref,
    receiver_ref,
    attr_ref,
    own_ref,
    w_in_ref,
    bias_ref,
    w_out_ref,
    tiles_ref,
    pre0_ref,
    pre1_ref,
    wanted_ref,
    deliver_ref,
    sum0_ref,
    sum1_ref,
    own_rows_ref,
    position_ref,
    table_ref,
):
    tile_count, tile = sender_ref.shape
    width, edge_count = attr_ref.shape
    node_dev = own_ref.shape[1]
    eye = jnp.where(
        lax.broadcasted_iota(jnp.int32, (node_dev, node_dev), 0)
        == lax.broadcasted_iota(jnp.int32, (node_dev, node_dev), 1),
        1.0,
        0.0,
    ).astype(BF16)
    own_rows_ref[...] = dot_lanes(eye, own_ref[...]).astype(BF16)
    senders = sender_ref[...]
    receivers = receiver_ref[...]
    used = receivers >= 0
    is_remote = jnp.where(used & (senders >= node_dev), 1.0, 0.0)
    is_local = jnp.where(used & (senders < node_dev), 1.0, 0.0)
    is_empty = jnp.where(used, 0.0, 1.0)
    remote_rank, remote_total = running_count(is_remote)
    local_rank, local_total = running_count(is_local)
    empty_rank, _ = running_count(is_empty)
    position_ref[...] = jnp.where(
        is_remote > 0.0,
        remote_rank,
        jnp.where(
            is_local > 0.0, remote_total + local_rank, remote_total + local_total + empty_rank
        ),
    )
    remote_tiles = (jnp.sum(is_remote).astype(jnp.int32) + tile - 1) // tile
    used_tiles = (jnp.sum(1.0 - is_empty).astype(jnp.int32) + tile - 1) // tile
    late_tiles = jnp.maximum(remote_tiles, LATE_TILES)
    tiles_ref[0] = late_tiles
    table_ref[0:width, :] = attr_ref[...]
    table_ref[width:, :] = jnp.zeros((table_ref.shape[0] - width, edge_count), BF16)
    for index in range(tile_count):
        lanes = slice(index * tile, (index + 1) * tile)
        row = senders[index : index + 1, :]
        table_ref[width : width + 16, lanes] = jnp.concatenate(
            [
                (row // tile).astype(F32),
                (row % tile).astype(F32),
                receivers[index : index + 1, :].astype(F32),
                jnp.zeros((13, tile), F32),
            ],
            axis=0,
        ).astype(BF16)
    w_send = w_in_ref[0:width, :]
    w_recv = w_in_ref[width : 2 * width, :]
    w_attr = w_in_ref[2 * width : 3 * width, :]
    sum0_ref[...] = jnp.zeros_like(sum0_ref)
    sum1_ref[...] = jnp.zeros_like(sum1_ref)

    def arrange(index):
        wanted = lax.broadcasted_iota(jnp.int32, (tile, tile), 0).astype(F32) + (
            index * tile
        ).astype(F32)
        order = jnp.concatenate(
            [
                jnp.where(position_ref[t : t + 1, :] == wanted, 1.0, 0.0).astype(BF16)
                for t in range(tile_count)
            ],
            axis=1,
        )
        table = table_ref[...]
        moved = dot_lanes(order, table)
        receiver_row = dot_lanes(table[width : width + 16, :], order)[2:3, :]
        sender_column = moved[:, width : width + 1] * tile + moved[:, width + 1 : width + 2]
        receiver_column = moved[:, width + 2 : width + 3]
        own = own_rows_ref[...]
        send_rows = dot(onehot(sender_column, node_dev), own).astype(BF16)
        recv_rows = dot(onehot(receiver_column, node_dev), own).astype(BF16)
        base = dot(moved[:, :width].astype(BF16), w_attr) + bias_ref[...]
        send0, send1 = level_pair(send_rows, w_send)
        recv0, recv1 = level_pair(recv_rows, w_recv)
        nodes = lax.broadcasted_iota(jnp.int32, (node_dev, tile), 0).astype(F32)
        deliver = jnp.where(nodes == receiver_row, 1.0, 0.0).astype(BF16)
        return base + send0 + recv0, base + send1 + recv1, deliver, sender_column

    @pl.loop(0, late_tiles)
    def _(index):
        pre0, pre1, deliver, sender_column = arrange(index)
        rows = pl.ds(pl.multiple_of(index * tile, tile), tile)
        pre0_ref[rows, :] = pre0
        pre1_ref[rows, :] = pre1
        deliver_ref[index] = deliver
        wanted_ref[rows, :] = jnp.broadcast_to(sender_column - node_dev, (tile, 128))

    @pl.loop(late_tiles, jnp.maximum(used_tiles, late_tiles))
    def _(index):
        pre0, pre1, deliver, _ = arrange(index)
        w_out = w_out_ref[...]
        sum0_ref[...] += dot(deliver, dot(silu(pre0).astype(BF16), w_out).astype(BF16))
        sum1_ref[...] += dot(deliver, dot(silu(pre1).astype(BF16), w_out).astype(BF16))


def edge_kernel(
    tiles_ref,
    pre0_hbm,
    pre1_hbm,
    wanted_hbm,
    deliver_hbm,
    sum0_hbm,
    sum1_hbm,
    remote_hbm,
    own_hbm,
    w_in_hbm,
    w_out_hbm,
    node_w_in_hbm,
    node_bias_ref,
    node_w_out_hbm,
    node_gain_ref,
    attention_gain_ref,
    state_ref,
    normed_ref,
    pre0_ref,
    pre1_ref,
    wanted_ref,
    deliver_ref,
    total0_ref,
    total1_ref,
    remote_ref,
    own_ref,
    w_send_ref,
    w_out_ref,
    node_w_in_ref,
    node_w_out_ref,
    arrived,
):
    tile = deliver_ref.shape[2]
    width = w_out_ref.shape[0]
    late = LATE_TILES * tile
    fetches = [
        pltpu.make_async_copy(source, target, arrived.at[index])
        for index, (source, target) in enumerate(
            (
                (wanted_hbm.at[0:late], wanted_ref),
                (remote_hbm, remote_ref),
                (w_in_hbm.at[0:width], w_send_ref),
                (pre0_hbm.at[0:late], pre0_ref),
                (pre1_hbm.at[0:late], pre1_ref),
                (w_out_hbm, w_out_ref),
                (deliver_hbm.at[0:LATE_TILES], deliver_ref),
                (sum0_hbm, total0_ref),
                (sum1_hbm, total1_ref),
                (own_hbm, own_ref),
                (node_w_in_hbm, node_w_in_ref),
                (node_w_out_hbm, node_w_out_ref),
            )
        )
    ]
    for fetch in fetches:
        fetch.start()

    def messages(wanted, pre0, pre1):
        rows = wanted.shape[0]
        lanes = lax.broadcasted_iota(jnp.int32, (rows, 128), 1).astype(F32)
        pick = jnp.concatenate(
            [
                jnp.where(wanted == lanes + float(first), 1.0, 0.0).astype(BF16)
                for first in range(0, remote_ref.shape[0], 128)
            ],
            axis=1,
        )
        send_rows = dot(pick, remote_ref[...]).astype(BF16)
        send0, send1 = level_pair(send_rows, w_send_ref[...])
        hidden0 = silu(pre0 + send0).astype(BF16)
        hidden1 = silu(pre1 + send1).astype(BF16)
        w_out = w_out_ref[...]
        return dot(hidden0, w_out).astype(BF16), dot(hidden1, w_out).astype(BF16)

    for fetch in fetches[:9]:
        fetch.wait()
    total0, total1 = total0_ref[...], total1_ref[...]
    step = LATE_STEP
    for start in range(0, LATE_TILES, step):
        rows = slice(start * tile, (start + step) * tile)
        message0, message1 = messages(wanted_ref[rows, :], pre0_ref[rows, :], pre1_ref[rows, :])
        deliver = jnp.concatenate([deliver_ref[start + i] for i in range(step)], axis=1)
        total0 += dot(deliver, message0)
        total1 += dot(deliver, message1)
    total0_ref[...] = total0
    total1_ref[...] = total1

    @pl.loop(LATE_TILES, tiles_ref[0])
    def _(index):
        rows = pl.ds(pl.multiple_of(index * tile, tile), tile)
        tail = [
            pltpu.make_async_copy(source, target, arrived.at[slot])
            for slot, (source, target) in enumerate(
                (
                    (wanted_hbm.at[rows], wanted_ref.at[0:tile]),
                    (pre0_hbm.at[rows], pre0_ref.at[0:tile]),
                    (pre1_hbm.at[rows], pre1_ref.at[0:tile]),
                    (deliver_hbm.at[pl.ds(index, 1)], deliver_ref.at[0:1]),
                )
            )
        ]
        for fetch in tail:
            fetch.start()
        for fetch in tail:
            fetch.wait()
        message0, message1 = messages(
            wanted_ref[0:tile, :], pre0_ref[0:tile, :], pre1_ref[0:tile, :]
        )
        deliver = deliver_ref[0]
        total0_ref[...] += dot(deliver, message0)
        total1_ref[...] += dot(deliver, message1)

    for fetch in fetches[9:]:
        fetch.wait()
    own = own_ref[...]
    own_pair = level_pair(own, node_w_in_ref[0:width, :])
    own_values = (own[:, :width], own[:, width:])
    states = []
    normed = []
    for level, total_ref in enumerate((total0_ref, total1_ref)):
        summed = total_ref[...].astype(BF16)
        node_pre = (
            own_pair[level] + dot(summed, node_w_in_ref[width : 2 * width, :]) + node_bias_ref[...]
        )
        update = dot(silu(node_pre).astype(BF16), node_w_out_ref[...])
        state = (
            own_values[level].astype(F32) + node_gain_ref[...] * normalize(update)
        ).astype(BF16)
        states.append(state)
        normed.append(
            (attention_gain_ref[...] * normalize(state.astype(F32))).astype(BF16)
        )
    state_ref[...] = merge_levels(*states)
    normed_ref[...] = merge_levels(*normed)


def attention_kernel(rows_ref, bias_ref, query_ref, key_ref, value_ref, out_ref, mix_ref):
    group_count, item_count, merged = rows_ref.shape
    width = merged // 2
    head_width = width // HEADS
    scale = 1.0 / math.sqrt(head_width)
    chunk = 8
    half = group_count * chunk
    total = 2 * half
    head_of = lax.broadcasted_iota(jnp.int32, (1, width), 1) // head_width
    row_node = lax.broadcasted_iota(jnp.int32, (total, total), 0) % chunk
    col_node = lax.broadcasted_iota(jnp.int32, (total, total), 1) % chunk
    same_node = row_node == col_node
    merged_rows = rows_ref[...].reshape(group_count * item_count, merged)

    def project(weight_ref):
        return [
            p.reshape(group_count, item_count, width)
            for p in level_pair(merged_rows, weight_ref[...])
        ]

    def rows_of(pair, part):
        items = slice(part * chunk, (part + 1) * chunk)
        return jnp.concatenate([p[:, items, :].reshape(half, width) for p in pair], axis=0)

    queries, keys, values = project(query_ref), project(key_ref), project(value_ref)
    ones = jnp.concatenate(
        [
            jnp.broadcast_to(jnp.where(head_of == head, 1.0, 0.0), (total, width))
            for head in range(HEADS)
        ],
        axis=0,
    ).astype(BF16)
    for part in range(item_count // chunk):
        part_queries = rows_of(queries, part).astype(BF16)
        part_keys = rows_of(keys, part)
        part_values = rows_of(values, part)
        bias = jnp.where(same_node, bias_ref[part], -1e30)
        stacked_keys = jnp.concatenate(
            [jnp.where(head_of == head, part_keys, 0.0).astype(BF16) for head in range(HEADS)],
            axis=0,
        )
        stacked_values = jnp.concatenate(
            [jnp.where(head_of == head, part_values, 0.0).astype(BF16) for head in range(HEADS)],
            axis=0,
        )
        scores = dot_lanes(part_queries, stacked_keys)
        powers = []
        for head in range(HEADS):
            own_scores = scores[:, head * total : (head + 1) * total] * scale + bias
            top = jnp.max(own_scores, axis=-1, keepdims=True)
            powers.append(jnp.exp(own_scores - top).astype(BF16))
        powers = jnp.concatenate(powers, axis=1)
        attended = dot(powers, stacked_values) / dot(powers, ones)
        items = slice(part * chunk, (part + 1) * chunk)
        for level in range(2):
            mix_ref[level, :, items, :] = attended[level * half : (level + 1) * half].reshape(
                group_count, chunk, width
            )
    mixed = [
        mix_ref[level].reshape(group_count * item_count, width).astype(BF16) for level in range(2)
    ]
    out_ref[...] = merge_levels(*mixed).reshape(group_count, item_count, merged)


def output_kernel(state_ref, attended_ref, live_ref, weight_ref, out_ref):
    width = weight_ref.shape[0]
    mixed = level_pair(attended_ref[...], weight_ref[...])
    state = state_ref[...].astype(F32)
    for level in range(2):
        kept = mixed[level] * live_ref[:, level : level + 1]
        result = state[:, level * width : (level + 1) * width] + kept
        out_ref[level] = result.T.astype(BF16)


def call(kernel, out_shape, *operands, scratch=(), **specs):
    return pl.pallas_call(
        kernel,
        out_shape=out_shape,
        **specs,
        scratch_shapes=list(scratch),
        compiler_params=pltpu.CompilerParams(vmem_limit_bytes=VMEM_BYTES),
    )(*operands)


def shape(dims, dtype=BF16):
    return jax.ShapeDtypeStruct(dims, dtype)


def per_device(
    node_state,
    edge_attr,
    edge_sender,
    edge_receiver,
    tile_block,
    halo_rows,
    valid_levels,
    edge_w_in,
    edge_bias,
    edge_w_out,
    node_w_in,
    node_bias,
    node_w_out,
    node_gain,
    attention_gain,
    query_weight,
    key_weight,
    value_weight,
    output_weight,
):
    group_count = lax.axis_size("lev")
    node_dev, lev_dev, width = node_state.shape
    tile_count = tile_block.shape[0]
    patch_count, slot_count = halo_rows.shape
    merged = lev_dev * width
    own = node_state.transpose(1, 2, 0).reshape(merged, node_dev)
    outgoing = call(
        halo_kernel,
        shape((patch_count * slot_count, merged)),
        halo_rows,
        own,
        scratch=[pltpu.VMEM((patch_count * slot_count, node_dev), BF16)],
    )
    incoming = lax.all_to_all(
        outgoing.reshape(patch_count, slot_count, merged),
        "patch",
        split_axis=0,
        concat_axis=0,
        tiled=True,
    ).reshape(patch_count * slot_count, merged)

    senders = edge_sender.reshape(tile_count, 128)
    in_block = edge_receiver.reshape(tile_count, 128)
    receivers = jnp.where(in_block >= 0, tile_block[:, None] * 128 + in_block, -1)
    edge_count = edge_attr.shape[0]
    sums = [shape((node_dev, width), F32)] * 2
    tiles, pre0, pre1, wanted, deliver, sum0, sum1, own_rows = call(
        local_kernel,
        (
            shape((1,), jnp.int32),
            shape((edge_count, width), F32),
            shape((edge_count, width), F32),
            shape((edge_count, 128), F32),
            shape((tile_count, node_dev, 128)),
            *sums,
            shape((node_dev, merged)),
        ),
        senders,
        receivers,
        edge_attr.T,
        own,
        edge_w_in,
        edge_bias[None, :],
        edge_w_out,
        scratch=[
            pltpu.VMEM((tile_count, 128), F32),
            pltpu.VMEM((width + 16, edge_count), BF16),
        ],
        out_specs=[pl.BlockSpec(memory_space=pltpu.SMEM)]
        + [pl.BlockSpec(memory_space=pltpu.VMEM)] * 7,
    )
    late = LATE_TILES * 128
    state, normed = call(
        edge_kernel,
        (shape((node_dev, merged)), shape((node_dev, merged))),
        tiles,
        pre0,
        pre1,
        wanted,
        deliver,
        sum0,
        sum1,
        incoming,
        own_rows,
        edge_w_in,
        edge_w_out,
        node_w_in,
        node_bias[None, :],
        node_w_out,
        node_gain[None, :],
        attention_gain[None, :],
        scratch=[
            pltpu.VMEM((late, width), F32),
            pltpu.VMEM((late, width), F32),
            pltpu.VMEM((late, 128), F32),
            pltpu.VMEM((LATE_TILES, node_dev, 128), BF16),
            pltpu.VMEM((node_dev, width), F32),
            pltpu.VMEM((node_dev, width), F32),
            pltpu.VMEM((patch_count * slot_count, merged), BF16),
            pltpu.VMEM((node_dev, merged), BF16),
            pltpu.VMEM((width, width), BF16),
            pltpu.VMEM((width, width), BF16),
            pltpu.VMEM((2 * width, width), BF16),
            pltpu.VMEM((width, width), BF16),
            pltpu.SemaphoreType.DMA((12,)),
        ],
        in_specs=[pl.BlockSpec(memory_space=pltpu.SMEM)]
        + [pl.BlockSpec(memory_space=pl.ANY)] * 11
        + [pl.BlockSpec(memory_space=pltpu.VMEM)]
        + [pl.BlockSpec(memory_space=pl.ANY)]
        + [pl.BlockSpec(memory_space=pltpu.VMEM)] * 2,
    )
    per_group = node_dev // group_count
    chunk = 8
    me = lax.axis_index("lev")
    mine = lax.dynamic_slice_in_dim(valid_levels, me * per_group, per_group)
    level_of = (
        jnp.arange(group_count, dtype=jnp.int32)[None, :, None] * lev_dev
        + jnp.arange(lev_dev, dtype=jnp.int32)[:, None, None]
    )
    key_bias = jnp.where(
        level_of[None] < mine.reshape(per_group // chunk, 1, 1, chunk), 0.0, -1e30
    ).reshape(per_group // chunk, 1, lev_dev * group_count * chunk)
    columns = lax.all_to_all(
        normed.reshape(group_count, per_group, merged),
        "lev",
        split_axis=0,
        concat_axis=0,
        tiled=True,
    )
    attended = call(
        attention_kernel,
        shape((group_count, per_group, merged)),
        columns,
        key_bias,
        query_weight,
        key_weight,
        value_weight,
        scratch=[pltpu.VMEM((lev_dev, group_count, per_group, width), F32)],
    )
    returned = lax.all_to_all(
        attended, "lev", split_axis=0, concat_axis=0, tiled=True
    ).reshape(node_dev, merged)
    levels = me * lev_dev + jnp.arange(lev_dev, dtype=jnp.int32)
    live = (levels[None, :] < valid_levels[:, None]).astype(F32)
    out = call(
        output_kernel,
        shape((lev_dev, width, node_dev)),
        state,
        returned,
        live,
        output_weight,
    )
    return out.transpose(2, 0, 1)


def solution(mesh):
    in_specs = (
        P("patch", "lev", None),
        P("patch", None),
        P("patch"),
        P("patch"),
        P("patch"),
        P("patch", None),
        P("patch"),
    ) + (P(),) * 12
    out_specs = P("patch", "lev", None)
    return jax.shard_map(
        per_device, mesh=mesh, in_specs=in_specs, out_specs=out_specs, check_vma=False
    )
```

```python
import math

import jax
import jax.numpy as jnp
from jax import lax
from jax.experimental import pallas as pl
from jax.experimental.pallas import tpu as pltpu
from jax.sharding import PartitionSpec as P

HEADS = 4
BF16 = jnp.bfloat16
F32 = jnp.float32
VMEM_BYTES = 20 * 1024 * 1024
WIDE = 256
LATE_TILES = 3
CHUNK = 8


def dot(a, b):
    return jnp.dot(a, b, preferred_element_type=F32)


def dot_lanes(a, b):
    return lax.dot_general(a, b, (((1,), (1,)), ((), ())), preferred_element_type=F32)


def silu(v):
    return v / (1.0 + jnp.exp(-v))


def normalize(values):
    centered = values - jnp.mean(values, axis=-1, keepdims=True)
    spread = jnp.mean(centered * centered, axis=-1, keepdims=True)
    return centered * lax.rsqrt(spread + 1e-05)


def onehot(column, width):
    lanes = lax.broadcasted_iota(jnp.int32, (column.shape[0], width), 1).astype(F32)
    return jnp.where(column == lanes, 1.0, 0.0).astype(BF16)


def level_pair(merged, weight):
    depth, width = weight.shape
    half = merged.shape[1] // 2
    cut = half // 128 * 128
    filler = jnp.zeros((half - cut, width), weight.dtype)
    first = jnp.concatenate([weight, filler], axis=0)
    second = jnp.concatenate([filler, weight], axis=0)
    return (
        dot(merged[:, : half + half - cut], first),
        dot(merged[:, cut:], second),
    )


def merge_levels(first, second):
    return jnp.concatenate([first, second], axis=1)


def halo_kernel(halo_hbm, own_hbm, out_hbm, halo_ref, own_ref, rows_ref, arrived, sent):
    patch_count, slot_count = halo_ref.shape
    fetches = [
        pltpu.make_async_copy(halo_hbm, halo_ref, arrived.at[0]),
        pltpu.make_async_copy(own_hbm, own_ref, arrived.at[1]),
    ]
    for fetch in fetches:
        fetch.start()
    fetches[0].wait()
    columns = halo_ref[...].astype(F32).T
    sends = []
    step = patch_count // 4
    for part in range(4):
        pick = jnp.concatenate(
            [
                onehot(columns[:, patch : patch + 1], own_ref.shape[1])
                for patch in range(part * step, (part + 1) * step)
            ],
            axis=0,
        )
        if part == 0:
            fetches[1].wait()
        rows = slice(part * step * slot_count, (part + 1) * step * slot_count)
        rows_ref[rows, :] = dot_lanes(pick, own_ref[...]).astype(BF16)
        sends.append(
            pltpu.make_async_copy(rows_ref.at[rows], out_hbm.at[rows], sent.at[part])
        )
        sends[-1].start()
    for send in sends:
        send.wait()


def running_count(flags):
    tile_count, tile = flags.shape
    flags = flags.astype(BF16)
    before = lax.broadcasted_iota(jnp.int32, (tile, tile), 0) < lax.broadcasted_iota(
        jnp.int32, (tile, tile), 1
    )
    above = lax.broadcasted_iota(jnp.int32, (tile_count, tile_count), 1) < lax.broadcasted_iota(
        jnp.int32, (tile_count, tile_count), 0
    )
    inside = dot(flags, jnp.where(before, 1.0, 0.0).astype(BF16))
    totals = dot(flags, jnp.ones((tile, tile), BF16)).astype(BF16)
    return (
        inside + dot(jnp.where(above, 1.0, 0.0).astype(BF16), totals),
        dot(jnp.ones((tile_count, tile_count), BF16), totals),
    )


def local_kernel(
    sender_ref,
    receiver_ref,
    attr_hbm,
    own_hbm,
    w_in_ref,
    bias_ref,
    w_out_ref,
    tiles_ref,
    late_wanted_ref,
    pre0_ref,
    pre1_ref,
    late_deliver_ref,
    own_rows_ref,
    sum0_ref,
    sum1_ref,
    pre0_hbm,
    pre1_hbm,
    wanted_hbm,
    deliver_hbm,
    own_ref,
    position_ref,
    table_ref,
    rest0_ref,
    rest1_ref,
    rest2_ref,
    rest3_ref,
    sent,
    arrived,
):
    fetches = [
        pltpu.make_async_copy(own_hbm, own_ref, arrived.at[0]),
        pltpu.make_async_copy(attr_hbm, table_ref.at[0 : attr_hbm.shape[0]], arrived.at[1]),
    ]
    for fetch in fetches:
        fetch.start()
    tile_count, tile = sender_ref.shape
    width, edge_count = attr_hbm.shape
    merged, node_dev = own_ref.shape
    eye = jnp.where(
        lax.broadcasted_iota(jnp.int32, (node_dev, node_dev), 0)
        == lax.broadcasted_iota(jnp.int32, (node_dev, node_dev), 1),
        1.0,
        0.0,
    ).astype(BF16)
    senders = sender_ref[...]
    receivers = receiver_ref[...]
    used = receivers >= 0
    is_remote = jnp.where(used & (senders >= node_dev), 1.0, 0.0)
    is_local = jnp.where(used & (senders < node_dev), 1.0, 0.0)
    is_empty = jnp.where(used, 0.0, 1.0)
    remote_rank, remote_total = running_count(is_remote)
    local_rank, local_total = running_count(is_local)
    empty_rank, _ = running_count(is_empty)
    position_ref[...] = jnp.where(
        is_remote > 0.0,
        remote_rank,
        jnp.where(
            is_local > 0.0, remote_total + local_rank, remote_total + local_total + empty_rank
        ),
    )
    remote_tiles = (jnp.sum(is_remote).astype(jnp.int32) + WIDE - 1) // WIDE
    used_tiles = (jnp.sum(1.0 - is_empty).astype(jnp.int32) + WIDE - 1) // WIDE
    late_tiles = jnp.maximum(remote_tiles, LATE_TILES)
    tiles_ref[0] = late_tiles
    for fetch in fetches:
        fetch.wait()
    own_rows_ref[...] = dot_lanes(eye, own_ref[...]).astype(BF16)
    table_ref[width:, :] = jnp.zeros((table_ref.shape[0] - width, edge_count), BF16)
    for index in range(tile_count):
        lanes = slice(index * tile, (index + 1) * tile)
        row = senders[index : index + 1, :]
        table_ref[width : width + 16, lanes] = jnp.concatenate(
            [
                (row // tile).astype(F32),
                (row % tile).astype(F32),
                receivers[index : index + 1, :].astype(F32),
                jnp.zeros((13, tile), F32),
            ],
            axis=0,
        ).astype(BF16)
    w_send = w_in_ref[0:width, :]
    w_recv = w_in_ref[width : 2 * width, :]
    w_attr = w_in_ref[2 * width : 3 * width, :]
    sum0_ref[...] = jnp.zeros_like(sum0_ref)
    sum1_ref[...] = jnp.zeros_like(sum1_ref)

    def arrange(index):
        wanted = lax.broadcasted_iota(jnp.int32, (WIDE, tile), 0).astype(F32) + (
            index * WIDE
        ).astype(F32)
        order = jnp.concatenate(
            [
                jnp.where(position_ref[t : t + 1, :] == wanted, 1.0, 0.0).astype(BF16)
                for t in range(tile_count)
            ],
            axis=1,
        )
        moved = dot_lanes(order, table_ref[...])
        receiver_row = dot_lanes(table_ref[width : width + 16, :], order)[2:3, :]
        sender_column = moved[:, width : width + 1] * tile + moved[:, width + 1 : width + 2]
        receiver_column = moved[:, width + 2 : width + 3]
        own = own_rows_ref[...]
        send_rows = dot(onehot(sender_column, node_dev), own).astype(BF16)
        recv_rows = dot(onehot(receiver_column, node_dev), own).astype(BF16)
        base = dot(moved[:, :width].astype(BF16), w_attr) + bias_ref[...]
        send0, send1 = level_pair(send_rows, w_send)
        recv0, recv1 = level_pair(recv_rows, w_recv)
        nodes = lax.broadcasted_iota(jnp.int32, (node_dev, WIDE), 0).astype(F32)
        deliver = jnp.where(nodes == receiver_row, 1.0, 0.0).astype(BF16)
        return base + send0 + recv0, base + send1 + recv1, deliver, sender_column - node_dev

    @pl.loop(0, LATE_TILES)
    def _(index):
        pre0, pre1, deliver, wanted = arrange(index)
        rows = pl.ds(pl.multiple_of(index * WIDE, WIDE), WIDE)
        pre0_ref[rows, :] = pre0
        pre1_ref[rows, :] = pre1
        late_deliver_ref[index] = deliver
        late_wanted_ref[rows, :] = jnp.broadcast_to(wanted, (WIDE, 128))

    @pl.loop(LATE_TILES, late_tiles)
    def _(index):
        rest0_ref[...], rest1_ref[...], rest3_ref[0], wanted = arrange(index)
        rest2_ref[...] = jnp.broadcast_to(wanted, rest2_ref.shape)
        sends = [
            pltpu.make_async_copy(source, target.at[index - LATE_TILES], sent.at[slot])
            for slot, (source, target) in enumerate(
                (
                    (rest0_ref, pre0_hbm),
                    (rest1_ref, pre1_hbm),
                    (rest2_ref, wanted_hbm),
                    (rest3_ref.at[0], deliver_hbm),
                )
            )
        ]
        for send in sends:
            send.start()
        for send in sends:
            send.wait()

    @pl.loop(late_tiles, jnp.maximum(used_tiles, late_tiles))
    def _(index):
        pre0, pre1, deliver, _ = arrange(index)
        w_out = w_out_ref[...]
        sum0_ref[...] += dot(deliver, dot(silu(pre0).astype(BF16), w_out).astype(BF16))
        sum1_ref[...] += dot(deliver, dot(silu(pre1).astype(BF16), w_out).astype(BF16))


def edge_kernel(
    tiles_ref,
    late_wanted_ref,
    late_pre0_hbm,
    late_pre1_hbm,
    late_deliver_hbm,
    own_hbm,
    sum0_hbm,
    sum1_hbm,
    pre0_hbm,
    pre1_hbm,
    wanted_hbm,
    deliver_hbm,
    w_in_ref,
    w_out_ref,
    node_w_in_ref,
    node_bias_ref,
    node_w_out_ref,
    node_gain_ref,
    attention_gain_ref,
    remote_ref,
    state_ref,
    normed_ref,
    pre0_ref,
    pre1_ref,
    late_deliver_ref,
    own_ref,
    total0_ref,
    total1_ref,
    rest0_ref,
    rest1_ref,
    rest2_ref,
    rest3_ref,
    early_arrived,
    arrived,
):
    width = w_out_ref.shape[0]
    early = [
        pltpu.make_async_copy(source, target, early_arrived.at[slot])
        for slot, (source, target) in enumerate(
            (
                (late_pre0_hbm, pre0_ref),
                (late_pre1_hbm, pre1_ref),
                (late_deliver_hbm, late_deliver_ref),
                (sum0_hbm, total0_ref),
                (sum1_hbm, total1_ref),
                (own_hbm, own_ref),
            )
        )
    ]
    for fetch in early:
        fetch.start()
    w_send = w_in_ref[0:width, :]

    def gather(wanted):
        lanes = lax.broadcasted_iota(jnp.int32, wanted.shape, 1).astype(F32)
        pick = jnp.concatenate(
            [
                jnp.where(wanted == lanes + float(first), 1.0, 0.0).astype(BF16)
                for first in range(0, remote_ref.shape[0], 128)
            ],
            axis=1,
        )
        return level_pair(dot(pick, remote_ref[...]).astype(BF16), w_send)

    def messages(pre, sent):
        return dot(silu(pre + sent).astype(BF16), w_out_ref[...]).astype(BF16)

    sent0, sent1 = gather(late_wanted_ref[...])
    early[0].wait()
    message0 = messages(pre0_ref[...], sent0)
    early[1].wait()
    message1 = messages(pre1_ref[...], sent1)
    for fetch in early[2:]:
        fetch.wait()
    deliver = jnp.concatenate([late_deliver_ref[i] for i in range(LATE_TILES)], axis=1)
    total0_ref[...] += dot(deliver, message0)
    total1_ref[...] += dot(deliver, message1)

    @pl.loop(LATE_TILES, tiles_ref[0])
    def _(index):
        fetches = [
            pltpu.make_async_copy(source.at[index - LATE_TILES], target, arrived.at[slot])
            for slot, (source, target) in enumerate(
                (
                    (pre0_hbm, rest0_ref),
                    (pre1_hbm, rest1_ref),
                    (wanted_hbm, rest2_ref),
                    (deliver_hbm, rest3_ref.at[0]),
                )
            )
        ]
        for fetch in fetches:
            fetch.start()
        for fetch in fetches:
            fetch.wait()
        sent0, sent1 = gather(rest2_ref[...])
        total0_ref[...] += dot(rest3_ref[0], messages(rest0_ref[...], sent0))
        total1_ref[...] += dot(rest3_ref[0], messages(rest1_ref[...], sent1))

    own = own_ref[...]
    own_pair = level_pair(own, node_w_in_ref[0:width, :])
    own_values = (own[:, :width], own[:, width:])
    states = []
    normed = []
    for level, total_ref in enumerate((total0_ref, total1_ref)):
        summed = total_ref[...].astype(BF16)
        node_pre = (
            own_pair[level] + dot(summed, node_w_in_ref[width : 2 * width, :]) + node_bias_ref[...]
        )
        update = dot(silu(node_pre).astype(BF16), node_w_out_ref[...])
        state = (
            own_values[level].astype(F32) + node_gain_ref[...] * normalize(update)
        ).astype(BF16)
        states.append(state)
        normed.append(
            (attention_gain_ref[...] * normalize(state.astype(F32))).astype(BF16)
        )
    state_ref[...] = merge_levels(*states)
    normed_ref[...] = merge_levels(*normed)


def attention_kernel(rows_ref, bias_ref, query_ref, key_ref, value_ref, out_ref, mix_ref):
    group_count, item_count, merged = rows_ref.shape
    width = merged // 2
    head_width = width // HEADS
    scale = 1.0 / math.sqrt(head_width)
    chunk = CHUNK
    half = group_count * chunk
    total = 2 * half
    head_of = lax.broadcasted_iota(jnp.int32, (1, width), 1) // head_width
    row_node = lax.broadcasted_iota(jnp.int32, (total, total), 0) % chunk
    col_node = lax.broadcasted_iota(jnp.int32, (total, total), 1) % chunk
    same_node = row_node == col_node
    merged_rows = rows_ref[...].reshape(group_count * item_count, merged)

    def project(weight_ref):
        return [
            p.reshape(group_count, item_count, width)
            for p in level_pair(merged_rows, weight_ref[...])
        ]

    def rows_of(pair, part):
        items = slice(part * chunk, (part + 1) * chunk)
        return jnp.concatenate([p[:, items, :].reshape(half, width) for p in pair], axis=0)

    queries, keys, values = project(query_ref), project(key_ref), project(value_ref)
    ones = jnp.concatenate(
        [
            jnp.broadcast_to(jnp.where(head_of == head, 1.0, 0.0), (total, width))
            for head in range(HEADS)
        ],
        axis=0,
    ).astype(BF16)
    for part in range(item_count // chunk):
        part_queries = rows_of(queries, part).astype(BF16)
        part_keys = rows_of(keys, part)
        part_values = rows_of(values, part)
        bias = jnp.where(same_node, bias_ref[part], -1e30)
        stacked_keys = jnp.concatenate(
            [jnp.where(head_of == head, part_keys, 0.0).astype(BF16) for head in range(HEADS)],
            axis=0,
        )
        stacked_values = jnp.concatenate(
            [jnp.where(head_of == head, part_values, 0.0).astype(BF16) for head in range(HEADS)],
            axis=0,
        )
        scores = dot_lanes(part_queries, stacked_keys)
        powers = []
        for head in range(HEADS):
            own_scores = scores[:, head * total : (head + 1) * total] * scale + bias
            top = jnp.max(own_scores, axis=-1, keepdims=True)
            powers.append(jnp.exp(own_scores - top).astype(BF16))
        powers = jnp.concatenate(powers, axis=1)
        attended = dot(powers, stacked_values) / dot(powers, ones)
        items = slice(part * chunk, (part + 1) * chunk)
        for level in range(2):
            mix_ref[level, :, items, :] = attended[level * half : (level + 1) * half].reshape(
                group_count, chunk, width
            )
    mixed = [
        mix_ref[level].reshape(group_count * item_count, width).astype(BF16) for level in range(2)
    ]
    out_ref[...] = merge_levels(*mixed).reshape(group_count, item_count, merged)


def output_kernel(state_ref, attended_ref, live_ref, weight_ref, out_ref):
    width = weight_ref.shape[0]
    mixed = level_pair(attended_ref[...], weight_ref[...])
    state = state_ref[...].astype(F32)
    for level in range(2):
        kept = mixed[level] * live_ref[:, level : level + 1]
        result = state[:, level * width : (level + 1) * width] + kept
        out_ref[level] = result.T.astype(BF16)


def call(kernel, out_shape, *operands, scratch=(), **specs):
    return pl.pallas_call(
        kernel,
        out_shape=out_shape,
        **specs,
        scratch_shapes=list(scratch),
        compiler_params=pltpu.CompilerParams(vmem_limit_bytes=VMEM_BYTES),
    )(*operands)


def shape(dims, dtype=BF16):
    return jax.ShapeDtypeStruct(dims, dtype)


def kept(array):
    return pltpu.with_memory_space_constraint(array, pltpu.VMEM)


def in_hbm(array):
    return pltpu.with_memory_space_constraint(array, pltpu.HBM)


IN_SMEM = pl.BlockSpec(memory_space=pltpu.SMEM)
IN_VMEM = pl.BlockSpec(memory_space=pltpu.VMEM)
ANYWHERE = pl.BlockSpec(memory_space=pl.ANY)


def per_device(
    node_state,
    edge_attr,
    edge_sender,
    edge_receiver,
    tile_block,
    halo_rows,
    valid_levels,
    edge_w_in,
    edge_bias,
    edge_w_out,
    node_w_in,
    node_bias,
    node_w_out,
    node_gain,
    attention_gain,
    query_weight,
    key_weight,
    value_weight,
    output_weight,
):
    group_count = lax.axis_size("lev")
    node_dev, lev_dev, width = node_state.shape
    tile_count = tile_block.shape[0]
    patch_count, slot_count = halo_rows.shape
    merged = lev_dev * width
    remote_count = patch_count * slot_count
    edge_count = edge_attr.shape[0]
    own = node_state.transpose(1, 2, 0).reshape(merged, node_dev)
    outgoing = call(
        halo_kernel,
        shape((remote_count, merged)),
        in_hbm(halo_rows),
        in_hbm(own),
        in_specs=[ANYWHERE] * 2,
        out_specs=ANYWHERE,
        scratch=[
            pltpu.VMEM((patch_count, slot_count), jnp.int32),
            pltpu.VMEM((merged, node_dev), BF16),
            pltpu.VMEM((remote_count, merged), BF16),
            pltpu.SemaphoreType.DMA((2,)),
            pltpu.SemaphoreType.DMA((4,)),
        ],
    )
    incoming = lax.all_to_all(
        outgoing.reshape(patch_count, slot_count, merged),
        "patch",
        split_axis=0,
        concat_axis=0,
        tiled=True,
    ).reshape(remote_count, merged)

    senders = edge_sender.reshape(tile_count, 128)
    in_block = edge_receiver.reshape(tile_count, 128)
    receivers = jnp.where(in_block >= 0, tile_block[:, None] * 128 + in_block, -1)
    per_group = node_dev // group_count
    me = lax.axis_index("lev")
    mine = lax.dynamic_slice_in_dim(valid_levels, me * per_group, per_group)
    level_of = (
        jnp.arange(group_count, dtype=jnp.int32)[None, :, None] * lev_dev
        + jnp.arange(lev_dev, dtype=jnp.int32)[:, None, None]
    )
    key_bias = jnp.where(
        level_of[None] < mine.reshape(per_group // CHUNK, 1, 1, CHUNK), 0.0, -1e30
    ).reshape(per_group // CHUNK, 1, lev_dev * group_count * CHUNK)
    levels = me * lev_dev + jnp.arange(lev_dev, dtype=jnp.int32)
    live = (levels[None, :] < valid_levels[:, None]).astype(F32)

    rest = edge_count // WIDE - LATE_TILES
    late = LATE_TILES * WIDE
    rest_shapes = [
        ((WIDE, width), F32),
        ((WIDE, width), F32),
        ((WIDE, 128), F32),
        ((1, node_dev, WIDE), BF16),
    ]
    tiles, wanted, *tail = call(
        local_kernel,
        (
            shape((1,), jnp.int32),
            pltpu.VMEM((late, 128), F32),
            pltpu.HBM((late, width), F32),
            pltpu.HBM((late, width), F32),
            pltpu.HBM((LATE_TILES, node_dev, WIDE), BF16),
            pltpu.HBM((node_dev, merged), BF16),
            pltpu.HBM((node_dev, width), F32),
            pltpu.HBM((node_dev, width), F32),
            pltpu.HBM((rest, WIDE, width), F32),
            pltpu.HBM((rest, WIDE, width), F32),
            pltpu.HBM((rest, WIDE, 128), F32),
            pltpu.HBM((rest, node_dev, WIDE), BF16),
        ),
        senders,
        receivers,
        in_hbm(edge_attr.T),
        in_hbm(own),
        edge_w_in,
        edge_bias[None, :],
        edge_w_out,
        scratch=[
            pltpu.VMEM((merged, node_dev), BF16),
            pltpu.VMEM((tile_count, 128), F32),
            pltpu.VMEM((width + 16, edge_count), BF16),
            *(pltpu.VMEM(*entry) for entry in rest_shapes),
            pltpu.SemaphoreType.DMA((4,)),
            pltpu.SemaphoreType.DMA((2,)),
        ],
        in_specs=[IN_VMEM] * 2 + [ANYWHERE] * 2 + [IN_VMEM] * 3,
        out_specs=[IN_SMEM] + [IN_VMEM] * 7 + [ANYWHERE] * 4,
    )
    state, normed = call(
        edge_kernel,
        (pltpu.VMEM((node_dev, merged), BF16), shape((node_dev, merged))),
        tiles,
        kept(wanted),
        *(in_hbm(array) for array in tail),
        edge_w_in,
        edge_w_out,
        node_w_in,
        node_bias[None, :],
        node_w_out,
        node_gain[None, :],
        attention_gain[None, :],
        incoming,
        scratch=[
            pltpu.VMEM((late, width), F32),
            pltpu.VMEM((late, width), F32),
            pltpu.VMEM((LATE_TILES, node_dev, WIDE), BF16),
            pltpu.VMEM((node_dev, merged), BF16),
            pltpu.VMEM((node_dev, width), F32),
            pltpu.VMEM((node_dev, width), F32),
            *(pltpu.VMEM(*entry) for entry in rest_shapes),
            pltpu.SemaphoreType.DMA((6,)),
            pltpu.SemaphoreType.DMA((4,)),
        ],
        in_specs=[IN_SMEM, IN_VMEM] + [ANYWHERE] * 10 + [IN_VMEM] * 8,
    )
    columns = lax.all_to_all(
        normed.reshape(group_count, per_group, merged),
        "lev",
        split_axis=0,
        concat_axis=0,
        tiled=True,
    )
    attended = call(
        attention_kernel,
        shape((group_count, per_group, merged)),
        columns,
        key_bias,
        query_weight,
        key_weight,
        value_weight,
        scratch=[pltpu.VMEM((lev_dev, group_count, per_group, width), F32)],
    )
    returned = lax.all_to_all(
        attended, "lev", split_axis=0, concat_axis=0, tiled=True
    ).reshape(node_dev, merged)
    out = call(
        output_kernel,
        shape((lev_dev, width, node_dev)),
        kept(state),
        returned,
        live,
        output_weight,
    )
    return out.transpose(2, 0, 1)


def solution(mesh):
    in_specs = (
        P("patch", "lev", None),
        P("patch", None),
        P("patch"),
        P("patch"),
        P("patch"),
        P("patch", None),
        P("patch"),
    ) + (P(),) * 12
    out_specs = P("patch", "lev", None)
    return jax.shard_map(
        per_device, mesh=mesh, in_specs=in_specs, out_specs=out_specs, check_vma=False
    )
```

```python
import math

import jax
import jax.numpy as jnp
from jax import lax
from jax.experimental import pallas as pl
from jax.experimental.pallas import tpu as pltpu
from jax.sharding import PartitionSpec as P

HEADS = 4
BF16 = jnp.bfloat16
F32 = jnp.float32
VMEM_BYTES = 20 * 1024 * 1024
WIDE = 256
LATE_TILES = 3
CHUNK = 8
CHIPS = 4
CORES = 2


def dot(a, b):
    return jnp.dot(a, b, preferred_element_type=F32)


def dot_lanes(a, b):
    return lax.dot_general(a, b, (((1,), (1,)), ((), ())), preferred_element_type=F32)


def silu(v):
    return v / (1.0 + jnp.exp(-v))


def normalize(values):
    centered = values - jnp.mean(values, axis=-1, keepdims=True)
    spread = jnp.mean(centered * centered, axis=-1, keepdims=True)
    return centered * lax.rsqrt(spread + 1e-05)


def onehot(column, width):
    lanes = lax.broadcasted_iota(jnp.int32, (column.shape[0], width), 1).astype(F32)
    return jnp.where(column == lanes, 1.0, 0.0).astype(BF16)


def level_pair(merged, weight):
    depth, width = weight.shape
    half = merged.shape[1] // 2
    cut = half // 128 * 128
    filler = jnp.zeros((half - cut, width), weight.dtype)
    first = jnp.concatenate([weight, filler], axis=0)
    second = jnp.concatenate([filler, weight], axis=0)
    return (
        dot(merged[:, : half + half - cut], first),
        dot(merged[:, cut:], second),
    )


def merge_levels(first, second):
    return jnp.concatenate([first, second], axis=1)


def halo_kernel(halo_hbm, own_hbm, out_hbm, halo_ref, own_ref, rows_ref, arrived, sent):
    patch_count, slot_count = halo_ref.shape
    fetches = [
        pltpu.make_async_copy(halo_hbm, halo_ref, arrived.at[0]),
        pltpu.make_async_copy(own_hbm, own_ref, arrived.at[1]),
    ]
    for fetch in fetches:
        fetch.start()
    fetches[0].wait()
    columns = halo_ref[...].astype(F32).T
    sends = []
    step = patch_count // 4
    for part in range(4):
        pick = jnp.concatenate(
            [
                onehot(columns[:, patch : patch + 1], own_ref.shape[1])
                for patch in range(part * step, (part + 1) * step)
            ],
            axis=0,
        )
        if part == 0:
            fetches[1].wait()
        rows = slice(part * step * slot_count, (part + 1) * step * slot_count)
        rows_ref[rows, :] = dot_lanes(pick, own_ref[...]).astype(BF16)
        sends.append(
            pltpu.make_async_copy(rows_ref.at[rows], out_hbm.at[rows], sent.at[part])
        )
        sends[-1].start()
    for send in sends:
        send.wait()


def running_count(flags):
    tile_count, tile = flags.shape
    flags = flags.astype(BF16)
    before = lax.broadcasted_iota(jnp.int32, (tile, tile), 0) < lax.broadcasted_iota(
        jnp.int32, (tile, tile), 1
    )
    above = lax.broadcasted_iota(jnp.int32, (tile_count, tile_count), 1) < lax.broadcasted_iota(
        jnp.int32, (tile_count, tile_count), 0
    )
    inside = dot(flags, jnp.where(before, 1.0, 0.0).astype(BF16))
    totals = dot(flags, jnp.ones((tile, tile), BF16)).astype(BF16)
    return (
        inside + dot(jnp.where(above, 1.0, 0.0).astype(BF16), totals),
        dot(jnp.ones((tile_count, tile_count), BF16), totals),
    )


def local_kernel(
    place_ref,
    sender_ref,
    receiver_ref,
    attr_hbm,
    own_hbm,
    w_in_ref,
    bias_ref,
    w_out_ref,
    tiles_ref,
    late_wanted_ref,
    pre0_ref,
    pre1_ref,
    late_deliver_ref,
    own_rows_ref,
    sum0_ref,
    sum1_ref,
    pre0_hbm,
    pre1_hbm,
    wanted_hbm,
    deliver_hbm,
    own_ref,
    position_ref,
    table_ref,
    rest0_ref,
    rest1_ref,
    rest2_ref,
    rest3_ref,
    sent,
    arrived,
):
    fetches = [
        pltpu.make_async_copy(own_hbm, own_ref, arrived.at[0]),
        pltpu.make_async_copy(attr_hbm, table_ref.at[0 : attr_hbm.shape[0]], arrived.at[1]),
    ]
    for fetch in fetches:
        fetch.start()
    tile_count, tile = sender_ref.shape
    width, edge_count = attr_hbm.shape
    merged, node_dev = own_ref.shape
    eye = jnp.where(
        lax.broadcasted_iota(jnp.int32, (node_dev, node_dev), 0)
        == lax.broadcasted_iota(jnp.int32, (node_dev, node_dev), 1),
        1.0,
        0.0,
    ).astype(BF16)
    senders = sender_ref[...]
    receivers = receiver_ref[...]
    used = receivers >= 0
    is_remote = jnp.where(used & (senders >= node_dev), 1.0, 0.0)
    is_local = jnp.where(used & (senders < node_dev), 1.0, 0.0)
    is_empty = jnp.where(used, 0.0, 1.0)
    remote_rank, remote_total = running_count(is_remote)
    local_rank, local_total = running_count(is_local)
    empty_rank, _ = running_count(is_empty)
    position_ref[...] = jnp.where(
        is_remote > 0.0,
        remote_rank,
        jnp.where(
            is_local > 0.0, remote_total + local_rank, remote_total + local_total + empty_rank
        ),
    )
    remote_tiles = (jnp.sum(is_remote).astype(jnp.int32) + WIDE - 1) // WIDE
    used_tiles = (jnp.sum(1.0 - is_empty).astype(jnp.int32) + WIDE - 1) // WIDE
    late_tiles = jnp.maximum(remote_tiles, LATE_TILES)
    tiles_ref[0] = late_tiles
    tiles_ref[1] = place_ref[0]
    for fetch in fetches:
        fetch.wait()
    own_rows_ref[...] = dot_lanes(eye, own_ref[...]).astype(BF16)
    table_ref[width:, :] = jnp.zeros((table_ref.shape[0] - width, edge_count), BF16)
    for index in range(tile_count):
        lanes = slice(index * tile, (index + 1) * tile)
        row = senders[index : index + 1, :]
        table_ref[width : width + 16, lanes] = jnp.concatenate(
            [
                (row // tile).astype(F32),
                (row % tile).astype(F32),
                receivers[index : index + 1, :].astype(F32),
                jnp.zeros((13, tile), F32),
            ],
            axis=0,
        ).astype(BF16)
    w_send = w_in_ref[0:width, :]
    w_recv = w_in_ref[width : 2 * width, :]
    w_attr = w_in_ref[2 * width : 3 * width, :]
    sum0_ref[...] = jnp.zeros_like(sum0_ref)
    sum1_ref[...] = jnp.zeros_like(sum1_ref)

    def arrange(index):
        wanted = lax.broadcasted_iota(jnp.int32, (WIDE, tile), 0).astype(F32) + (
            index * WIDE
        ).astype(F32)
        order = jnp.concatenate(
            [
                jnp.where(position_ref[t : t + 1, :] == wanted, 1.0, 0.0).astype(BF16)
                for t in range(tile_count)
            ],
            axis=1,
        )
        moved = dot_lanes(order, table_ref[...])
        receiver_row = dot_lanes(table_ref[width : width + 16, :], order)[2:3, :]
        sender_column = moved[:, width : width + 1] * tile + moved[:, width + 1 : width + 2]
        receiver_column = moved[:, width + 2 : width + 3]
        own = own_rows_ref[...]
        send_rows = dot(onehot(sender_column, node_dev), own).astype(BF16)
        recv_rows = dot(onehot(receiver_column, node_dev), own).astype(BF16)
        base = dot(moved[:, :width].astype(BF16), w_attr) + bias_ref[...]
        send0, send1 = level_pair(send_rows, w_send)
        recv0, recv1 = level_pair(recv_rows, w_recv)
        nodes = lax.broadcasted_iota(jnp.int32, (node_dev, WIDE), 0).astype(F32)
        deliver = jnp.where(nodes == receiver_row, 1.0, 0.0).astype(BF16)
        return base + send0 + recv0, base + send1 + recv1, deliver, sender_column - node_dev

    @pl.loop(0, LATE_TILES)
    def _(index):
        pre0, pre1, deliver, wanted = arrange(index)
        rows = pl.ds(pl.multiple_of(index * WIDE, WIDE), WIDE)
        pre0_ref[rows, :] = pre0
        pre1_ref[rows, :] = pre1
        late_deliver_ref[index] = deliver
        late_wanted_ref[rows, :] = jnp.broadcast_to(wanted, (WIDE, 128))

    @pl.loop(LATE_TILES, late_tiles)
    def _(index):
        rest0_ref[...], rest1_ref[...], rest3_ref[0], wanted = arrange(index)
        rest2_ref[...] = jnp.broadcast_to(wanted, rest2_ref.shape)
        sends = [
            pltpu.make_async_copy(source, target.at[index - LATE_TILES], sent.at[slot])
            for slot, (source, target) in enumerate(
                (
                    (rest0_ref, pre0_hbm),
                    (rest1_ref, pre1_hbm),
                    (rest2_ref, wanted_hbm),
                    (rest3_ref.at[0], deliver_hbm),
                )
            )
        ]
        for send in sends:
            send.start()
        for send in sends:
            send.wait()

    @pl.loop(late_tiles, jnp.maximum(used_tiles, late_tiles))
    def _(index):
        pre0, pre1, deliver, _ = arrange(index)
        w_out = w_out_ref[...]
        sum0_ref[...] += dot(deliver, dot(silu(pre0).astype(BF16), w_out).astype(BF16))
        sum1_ref[...] += dot(deliver, dot(silu(pre1).astype(BF16), w_out).astype(BF16))


def edge_kernel(
    tiles_ref,
    late_wanted_ref,
    late_pre0_hbm,
    late_pre1_hbm,
    late_deliver_hbm,
    own_hbm,
    sum0_hbm,
    sum1_hbm,
    pre0_hbm,
    pre1_hbm,
    wanted_hbm,
    deliver_hbm,
    w_in_ref,
    w_out_ref,
    node_w_in_ref,
    node_bias_ref,
    node_w_out_ref,
    node_gain_ref,
    attention_gain_ref,
    remote_ref,
    state_ref,
    out0_ref,
    out1_ref,
    out2_ref,
    out3_ref,
    normed_ref,
    pre0_ref,
    pre1_ref,
    late_deliver_ref,
    own_ref,
    total0_ref,
    total1_ref,
    rest0_ref,
    rest1_ref,
    rest2_ref,
    rest3_ref,
    early_arrived,
    arrived,
):
    width = w_out_ref.shape[0]
    early = [
        pltpu.make_async_copy(source, target, early_arrived.at[slot])
        for slot, (source, target) in enumerate(
            (
                (late_pre0_hbm, pre0_ref),
                (late_pre1_hbm, pre1_ref),
                (late_deliver_hbm, late_deliver_ref),
                (sum0_hbm, total0_ref),
                (sum1_hbm, total1_ref),
                (own_hbm, own_ref),
            )
        )
    ]
    for fetch in early:
        fetch.start()
    w_send = w_in_ref[0:width, :]

    def gather(wanted):
        lanes = lax.broadcasted_iota(jnp.int32, wanted.shape, 1).astype(F32)
        pick = jnp.concatenate(
            [
                jnp.where(wanted == lanes + float(first), 1.0, 0.0).astype(BF16)
                for first in range(0, remote_ref.shape[0], 128)
            ],
            axis=1,
        )
        return level_pair(dot(pick, remote_ref[...]).astype(BF16), w_send)

    def messages(pre, sent):
        return dot(silu(pre + sent).astype(BF16), w_out_ref[...]).astype(BF16)

    sent0, sent1 = gather(late_wanted_ref[...])
    early[0].wait()
    message0 = messages(pre0_ref[...], sent0)
    early[1].wait()
    message1 = messages(pre1_ref[...], sent1)
    for fetch in early[2:]:
        fetch.wait()
    deliver = jnp.concatenate([late_deliver_ref[i] for i in range(LATE_TILES)], axis=1)
    total0_ref[...] += dot(deliver, message0)
    total1_ref[...] += dot(deliver, message1)

    @pl.loop(LATE_TILES, tiles_ref[0])
    def _(index):
        fetches = [
            pltpu.make_async_copy(source.at[index - LATE_TILES], target, arrived.at[slot])
            for slot, (source, target) in enumerate(
                (
                    (pre0_hbm, rest0_ref),
                    (pre1_hbm, rest1_ref),
                    (wanted_hbm, rest2_ref),
                    (deliver_hbm, rest3_ref.at[0]),
                )
            )
        ]
        for fetch in fetches:
            fetch.start()
        for fetch in fetches:
            fetch.wait()
        sent0, sent1 = gather(rest2_ref[...])
        total0_ref[...] += dot(rest3_ref[0], messages(rest0_ref[...], sent0))
        total1_ref[...] += dot(rest3_ref[0], messages(rest1_ref[...], sent1))

    own = own_ref[...]
    own_pair = level_pair(own, node_w_in_ref[0:width, :])
    own_values = (own[:, :width], own[:, width:])
    states = []
    normed = []
    for level, total_ref in enumerate((total0_ref, total1_ref)):
        summed = total_ref[...].astype(BF16)
        node_pre = (
            own_pair[level] + dot(summed, node_w_in_ref[width : 2 * width, :]) + node_bias_ref[...]
        )
        update = dot(silu(node_pre).astype(BF16), node_w_out_ref[...])
        state = (
            own_values[level].astype(F32) + node_gain_ref[...] * normalize(update)
        ).astype(BF16)
        states.append(state)
        normed.append(
            (attention_gain_ref[...] * normalize(state.astype(F32))).astype(BF16)
        )
    state_ref[...] = merge_levels(*states)
    normed_ref[...] = merge_levels(*normed)
    share = out0_ref.shape[0]
    for shift, out_ref in enumerate((out0_ref, out1_ref, out2_ref, out3_ref)):
        block = lax.rem(tiles_ref[1] + shift, CHIPS)
        out_ref[...] = normed_ref[pl.ds(pl.multiple_of(block * share, share), share), :]


def attention_kernel(*refs):
    block_refs, refs = refs[: CHIPS * CORES], refs[CHIPS * CORES :]
    bias_ref, query_ref, key_ref, value_ref, *out_refs, mix_ref = refs
    block_count = len(block_refs)
    item_count, merged = block_refs[0].shape
    width = merged // 2
    head_width = width // HEADS
    scale = 1.0 / math.sqrt(head_width)
    key_total = 2 * block_count * CHUNK
    query_total = 2 * CHIPS * CHUNK
    head_of = lax.broadcasted_iota(jnp.int32, (1, width), 1) // head_width
    same_node = (
        lax.broadcasted_iota(jnp.int32, (query_total, key_total), 0) % CHUNK
        == lax.broadcasted_iota(jnp.int32, (query_total, key_total), 1) % CHUNK
    )
    blocks = jnp.concatenate([ref[...] for ref in block_refs], axis=0)

    def project(count, weight_ref):
        return [
            p.reshape(count, item_count, width)
            for p in level_pair(blocks[: count * item_count], weight_ref[...])
        ]

    def rows_of(pair, part):
        items = slice(part * CHUNK, (part + 1) * CHUNK)
        return jnp.concatenate([p[:, items, :].reshape(-1, width) for p in pair], axis=0)

    def per_head(rows):
        return jnp.concatenate(
            [jnp.where(head_of == head, rows, 0.0).astype(BF16) for head in range(HEADS)], axis=0
        )

    queries = project(CHIPS, query_ref)
    keys, values = project(block_count, key_ref), project(block_count, value_ref)
    ones = per_head(jnp.ones((key_total, width), F32))
    for part in range(item_count // CHUNK):
        bias = jnp.where(same_node, bias_ref[part], -1e30)
        scores = dot_lanes(rows_of(queries, part).astype(BF16), per_head(rows_of(keys, part)))
        powers = []
        for head in range(HEADS):
            own_scores = scores[:, head * key_total : (head + 1) * key_total] * scale + bias
            top = jnp.max(own_scores, axis=-1, keepdims=True)
            powers.append(jnp.exp(own_scores - top).astype(BF16))
        powers = jnp.concatenate(powers, axis=1)
        attended = dot(powers, per_head(rows_of(values, part))) / dot(powers, ones)
        mix_ref[:, :, part * CHUNK : (part + 1) * CHUNK, :] = attended.reshape(
            2, CHIPS, CHUNK, width
        )
    for chip, out_ref in enumerate(out_refs):
        out_ref[...] = merge_levels(mix_ref[0, chip].astype(BF16), mix_ref[1, chip].astype(BF16))


def output_kernel(
    place_ref, state_ref, part0_ref, part1_ref, part2_ref, part3_ref, live_ref, weight_ref, out_ref,
    attended_ref,
):
    width = weight_ref.shape[0]
    share = part0_ref.shape[0]
    for shift, part_ref in enumerate((part0_ref, part1_ref, part2_ref, part3_ref)):
        block = lax.rem(place_ref[1] + shift, CHIPS)
        attended_ref[pl.ds(pl.multiple_of(block * share, share), share), :] = part_ref[...]
    mixed = level_pair(attended_ref[...], weight_ref[...])
    state = state_ref[...].astype(F32)
    for level in range(2):
        live_part = mixed[level] * live_ref[:, level : level + 1]
        result = state[:, level * width : (level + 1) * width] + live_part
        out_ref[level] = result.T.astype(BF16)


def call(kernel, out_shape, *operands, scratch=(), **specs):
    return pl.pallas_call(
        kernel,
        out_shape=out_shape,
        **specs,
        scratch_shapes=list(scratch),
        compiler_params=pltpu.CompilerParams(vmem_limit_bytes=VMEM_BYTES),
    )(*operands)


def shape(dims, dtype=BF16):
    return jax.ShapeDtypeStruct(dims, dtype)


def kept(array):
    return pltpu.with_memory_space_constraint(array, pltpu.VMEM)


def in_hbm(array):
    return pltpu.with_memory_space_constraint(array, pltpu.HBM)


IN_SMEM = pl.BlockSpec(memory_space=pltpu.SMEM)
IN_VMEM = pl.BlockSpec(memory_space=pltpu.VMEM)
ANYWHERE = pl.BlockSpec(memory_space=pl.ANY)


def per_device(
    node_state,
    edge_attr,
    edge_sender,
    edge_receiver,
    tile_block,
    halo_rows,
    valid_levels,
    edge_w_in,
    edge_bias,
    edge_w_out,
    node_w_in,
    node_bias,
    node_w_out,
    node_gain,
    attention_gain,
    query_weight,
    key_weight,
    value_weight,
    output_weight,
):
    group_count = lax.axis_size("lev")
    node_dev, lev_dev, width = node_state.shape
    tile_count = tile_block.shape[0]
    patch_count, slot_count = halo_rows.shape
    merged = lev_dev * width
    remote_count = patch_count * slot_count
    edge_count = edge_attr.shape[0]
    own = node_state.transpose(1, 2, 0).reshape(merged, node_dev)
    outgoing = call(
        halo_kernel,
        shape((remote_count, merged)),
        in_hbm(halo_rows),
        in_hbm(own),
        in_specs=[ANYWHERE] * 2,
        out_specs=ANYWHERE,
        scratch=[
            pltpu.VMEM((patch_count, slot_count), jnp.int32),
            pltpu.VMEM((merged, node_dev), BF16),
            pltpu.VMEM((remote_count, merged), BF16),
            pltpu.SemaphoreType.DMA((2,)),
            pltpu.SemaphoreType.DMA((4,)),
        ],
    )
    incoming = lax.all_to_all(
        outgoing.reshape(patch_count, slot_count, merged),
        "patch",
        split_axis=0,
        concat_axis=0,
        tiled=True,
    ).reshape(remote_count, merged)

    senders = edge_sender.reshape(tile_count, 128)
    in_block = edge_receiver.reshape(tile_count, 128)
    receivers = jnp.where(in_block >= 0, tile_block[:, None] * 128 + in_block, -1)
    share = node_dev // CHIPS
    me = lax.axis_index("lev")
    chip, core = me // CORES, me % CORES
    mine = lax.dynamic_slice_in_dim(valid_levels, chip * share, share)
    block = jnp.arange(CHIPS * CORES, dtype=jnp.int32)
    from_chip = (chip - block % CHIPS) % CHIPS
    from_core = jnp.where(block < CHIPS, core, 1 - core)
    level_of = (
        ((from_chip * CORES + from_core) * lev_dev)[None, :, None]
        + jnp.arange(lev_dev, dtype=jnp.int32)[:, None, None]
    )
    key_bias = jnp.where(
        level_of[None] < mine.reshape(share // CHUNK, 1, 1, CHUNK), 0.0, -1e30
    ).reshape(share // CHUNK, 1, lev_dev * group_count * CHUNK)
    levels = me * lev_dev + jnp.arange(lev_dev, dtype=jnp.int32)
    live = (levels[None, :] < valid_levels[:, None]).astype(F32)

    rest = edge_count // WIDE - LATE_TILES
    late = LATE_TILES * WIDE
    rest_shapes = [
        ((WIDE, width), F32),
        ((WIDE, width), F32),
        ((WIDE, 128), F32),
        ((1, node_dev, WIDE), BF16),
    ]
    tiles, wanted, *tail = call(
        local_kernel,
        (
            shape((2,), jnp.int32),
            pltpu.VMEM((late, 128), F32),
            pltpu.HBM((late, width), F32),
            pltpu.HBM((late, width), F32),
            pltpu.HBM((LATE_TILES, node_dev, WIDE), BF16),
            pltpu.HBM((node_dev, merged), BF16),
            pltpu.HBM((node_dev, width), F32),
            pltpu.HBM((node_dev, width), F32),
            pltpu.HBM((rest, WIDE, width), F32),
            pltpu.HBM((rest, WIDE, width), F32),
            pltpu.HBM((rest, WIDE, 128), F32),
            pltpu.HBM((rest, node_dev, WIDE), BF16),
        ),
        chip.reshape(1),
        senders,
        receivers,
        in_hbm(edge_attr.T),
        in_hbm(own),
        edge_w_in,
        edge_bias[None, :],
        edge_w_out,
        scratch=[
            pltpu.VMEM((merged, node_dev), BF16),
            pltpu.VMEM((tile_count, 128), F32),
            pltpu.VMEM((width + 16, edge_count), BF16),
            *(pltpu.VMEM(*entry) for entry in rest_shapes),
            pltpu.SemaphoreType.DMA((4,)),
            pltpu.SemaphoreType.DMA((2,)),
        ],
        in_specs=[IN_SMEM] + [IN_VMEM] * 2 + [ANYWHERE] * 2 + [IN_VMEM] * 3,
        out_specs=[IN_SMEM] + [IN_VMEM] * 7 + [ANYWHERE] * 4,
    )
    state, *blocks = call(
        edge_kernel,
        (pltpu.VMEM((node_dev, merged), BF16), *[shape((share, merged))] * CHIPS),
        tiles,
        kept(wanted),
        *(in_hbm(array) for array in tail),
        edge_w_in,
        edge_w_out,
        node_w_in,
        node_bias[None, :],
        node_w_out,
        node_gain[None, :],
        attention_gain[None, :],
        incoming,
        scratch=[
            pltpu.VMEM((node_dev, merged), BF16),
            pltpu.VMEM((late, width), F32),
            pltpu.VMEM((late, width), F32),
            pltpu.VMEM((LATE_TILES, node_dev, WIDE), BF16),
            pltpu.VMEM((node_dev, merged), BF16),
            pltpu.VMEM((node_dev, width), F32),
            pltpu.VMEM((node_dev, width), F32),
            *(pltpu.VMEM(*entry) for entry in rest_shapes),
            pltpu.SemaphoreType.DMA((6,)),
            pltpu.SemaphoreType.DMA((4,)),
        ],
        in_specs=[IN_SMEM, IN_VMEM] + [ANYWHERE] * 10 + [IN_VMEM] * 8,
    )

    def to_chip(array, shift):
        return lax.ppermute(
            array,
            "lev",
            [
                (a * CORES + b, (a + shift) % CHIPS * CORES + b)
                for a in range(CHIPS)
                for b in range(CORES)
            ],
        )

    def to_core(array):
        return lax.ppermute(array, "lev", [(a, a ^ 1) for a in range(CHIPS * CORES)])

    blocks = blocks[:1] + [to_chip(blocks[shift], shift) for shift in range(1, CHIPS)]
    blocks = blocks + [to_core(array) for array in blocks]
    attended = call(
        attention_kernel,
        [shape((share, merged))] * CHIPS,
        *blocks,
        key_bias,
        query_weight,
        key_weight,
        value_weight,
        scratch=[pltpu.VMEM((lev_dev, CHIPS, share, width), F32)],
    )
    returned = [attended[0]] + [to_chip(attended[shift], -shift) for shift in range(1, CHIPS)]
    out = call(
        output_kernel,
        shape((lev_dev, width, node_dev)),
        tiles,
        kept(state),
        *returned,
        live,
        output_weight,
        scratch=[pltpu.VMEM((node_dev, merged), BF16)],
        in_specs=[IN_SMEM] + [IN_VMEM] * 7,
    )
    return out.transpose(2, 0, 1)


def solution(mesh):
    in_specs = (
        P("patch", "lev", None),
        P("patch", None),
        P("patch"),
        P("patch"),
        P("patch"),
        P("patch", None),
        P("patch"),
    ) + (P(),) * 12
    out_specs = P("patch", "lev", None)
    return jax.shard_map(
        per_device, mesh=mesh, in_specs=in_specs, out_specs=out_specs, check_vma=False
    )
```

```python
import math

import jax
import jax.numpy as jnp
from jax import lax
from jax.experimental import pallas as pl
from jax.experimental.pallas import tpu as pltpu
from jax.sharding import PartitionSpec as P

HEADS = 4
BF16 = jnp.bfloat16
F32 = jnp.float32
VMEM_BYTES = 20 * 1024 * 1024
WIDE = 256
LATE_TILES = 3
CHUNK = 8
CHIPS = 4
CORES = 2


def dot(a, b):
    return jnp.dot(a, b, preferred_element_type=F32)


def dot_lanes(a, b):
    return lax.dot_general(a, b, (((1,), (1,)), ((), ())), preferred_element_type=F32)


def silu(v):
    return v / (1.0 + jnp.exp(-v))


def normalize(values):
    centered = values - jnp.mean(values, axis=-1, keepdims=True)
    spread = jnp.mean(centered * centered, axis=-1, keepdims=True)
    return centered * lax.rsqrt(spread + 1e-05)


def onehot(column, width):
    lanes = lax.broadcasted_iota(jnp.int32, (column.shape[0], width), 1).astype(F32)
    return jnp.where(column == lanes, 1.0, 0.0).astype(BF16)


def level_pair(merged, weight):
    depth, width = weight.shape
    half = merged.shape[1] // 2
    cut = half // 128 * 128
    filler = jnp.zeros((half - cut, width), weight.dtype)
    first = jnp.concatenate([weight, filler], axis=0)
    second = jnp.concatenate([filler, weight], axis=0)
    return (
        dot(merged[:, : half + half - cut], first),
        dot(merged[:, cut:], second),
    )


def merge_levels(first, second):
    return jnp.concatenate([first, second], axis=1)


def halo_kernel(halo_hbm, own_hbm, out_hbm, halo_ref, own_ref, rows_ref, arrived, sent):
    patch_count, slot_count = halo_ref.shape
    fetches = [
        pltpu.make_async_copy(halo_hbm, halo_ref, arrived.at[0]),
        pltpu.make_async_copy(own_hbm, own_ref, arrived.at[1]),
    ]
    for fetch in fetches:
        fetch.start()
    fetches[0].wait()
    columns = halo_ref[...].astype(F32).T
    sends = []
    step = patch_count // 4
    for part in range(4):
        pick = jnp.concatenate(
            [
                onehot(columns[:, patch : patch + 1], own_ref.shape[1])
                for patch in range(part * step, (part + 1) * step)
            ],
            axis=0,
        )
        if part == 0:
            fetches[1].wait()
        rows = slice(part * step * slot_count, (part + 1) * step * slot_count)
        rows_ref[rows, :] = dot_lanes(pick, own_ref[...]).astype(BF16)
        sends.append(
            pltpu.make_async_copy(rows_ref.at[rows], out_hbm.at[rows], sent.at[part])
        )
        sends[-1].start()
    for send in sends:
        send.wait()


def running_count(flags):
    tile_count, tile = flags.shape
    flags = flags.astype(BF16)
    before = lax.broadcasted_iota(jnp.int32, (tile, tile), 0) < lax.broadcasted_iota(
        jnp.int32, (tile, tile), 1
    )
    above = lax.broadcasted_iota(jnp.int32, (tile_count, tile_count), 1) < lax.broadcasted_iota(
        jnp.int32, (tile_count, tile_count), 0
    )
    inside = dot(flags, jnp.where(before, 1.0, 0.0).astype(BF16))
    totals = dot(flags, jnp.ones((tile, tile), BF16)).astype(BF16)
    return (
        inside + dot(jnp.where(above, 1.0, 0.0).astype(BF16), totals),
        dot(jnp.ones((tile_count, tile_count), BF16), totals),
    )


def local_kernel(
    place_ref,
    sender_ref,
    receiver_ref,
    attr_hbm,
    own_hbm,
    w_in_ref,
    bias_ref,
    w_out_ref,
    node_w_in_ref,
    node_bias_ref,
    tiles_ref,
    late_wanted_ref,
    pre0_ref,
    pre1_ref,
    receivers_ref,
    own_rows_ref,
    node_pre0_ref,
    node_pre1_ref,
    sum0_ref,
    sum1_ref,
    pre0_hbm,
    pre1_hbm,
    wanted_hbm,
    deliver_hbm,
    own_ref,
    position_ref,
    table_ref,
    rest0_ref,
    rest1_ref,
    rest2_ref,
    rest3_ref,
    sent,
    arrived,
):
    fetches = [
        pltpu.make_async_copy(own_hbm, own_ref, arrived.at[0]),
        pltpu.make_async_copy(attr_hbm, table_ref.at[0 : attr_hbm.shape[0]], arrived.at[1]),
    ]
    for fetch in fetches:
        fetch.start()
    tile_count, tile = sender_ref.shape
    width, edge_count = attr_hbm.shape
    merged, node_dev = own_ref.shape
    eye = jnp.where(
        lax.broadcasted_iota(jnp.int32, (node_dev, node_dev), 0)
        == lax.broadcasted_iota(jnp.int32, (node_dev, node_dev), 1),
        1.0,
        0.0,
    ).astype(BF16)
    senders = sender_ref[...]
    receivers = receiver_ref[...]
    used = receivers >= 0
    is_remote = jnp.where(used & (senders >= node_dev), 1.0, 0.0)
    is_local = jnp.where(used & (senders < node_dev), 1.0, 0.0)
    is_empty = jnp.where(used, 0.0, 1.0)
    remote_rank, remote_total = running_count(is_remote)
    local_rank, local_total = running_count(is_local)
    empty_rank, _ = running_count(is_empty)
    position_ref[...] = jnp.where(
        is_remote > 0.0,
        remote_rank,
        jnp.where(
            is_local > 0.0, remote_total + local_rank, remote_total + local_total + empty_rank
        ),
    )
    remote_tiles = (jnp.sum(is_remote).astype(jnp.int32) + WIDE - 1) // WIDE
    used_tiles = (jnp.sum(1.0 - is_empty).astype(jnp.int32) + WIDE - 1) // WIDE
    late_tiles = jnp.maximum(remote_tiles, LATE_TILES)
    slot = lax.broadcasted_iota(jnp.int32, tiles_ref.shape, 1)
    tiles_ref[...] = jnp.where(slot == 0, late_tiles, place_ref[0])
    for fetch in fetches:
        fetch.wait()
    own_rows_ref[...] = dot_lanes(eye, own_ref[...]).astype(BF16)
    own_pair = level_pair(own_rows_ref[...], node_w_in_ref[0:width, :])
    node_pre0_ref[:, 0:width] = own_pair[0] + node_bias_ref[...]
    node_pre1_ref[:, 0:width] = own_pair[1] + node_bias_ref[...]
    table_ref[width:, :] = jnp.zeros((table_ref.shape[0] - width, edge_count), BF16)
    for index in range(tile_count):
        lanes = slice(index * tile, (index + 1) * tile)
        row = senders[index : index + 1, :]
        table_ref[width : width + 16, lanes] = jnp.concatenate(
            [
                (row // tile).astype(F32),
                (row % tile).astype(F32),
                receivers[index : index + 1, :].astype(F32),
                jnp.zeros((13, tile), F32),
            ],
            axis=0,
        ).astype(BF16)
    w_send = w_in_ref[0:width, :]
    w_recv = w_in_ref[width : 2 * width, :]
    w_attr = w_in_ref[2 * width : 3 * width, :]
    sum0_ref[...] = jnp.zeros_like(sum0_ref)
    sum1_ref[...] = jnp.zeros_like(sum1_ref)

    def arrange(index):
        wanted = lax.broadcasted_iota(jnp.int32, (WIDE, tile), 0).astype(F32) + (
            index * WIDE
        ).astype(F32)
        order = jnp.concatenate(
            [
                jnp.where(position_ref[t : t + 1, :] == wanted, 1.0, 0.0).astype(BF16)
                for t in range(tile_count)
            ],
            axis=1,
        )
        moved = dot_lanes(order, table_ref[...])
        receiver_row = dot_lanes(table_ref[width : width + 16, :], order)[2:3, :]
        sender_column = moved[:, width : width + 1] * tile + moved[:, width + 1 : width + 2]
        receiver_column = moved[:, width + 2 : width + 3]
        own = own_rows_ref[...]
        send_rows = dot(onehot(sender_column, node_dev), own).astype(BF16)
        recv_rows = dot(onehot(receiver_column, node_dev), own).astype(BF16)
        base = dot(moved[:, :width].astype(BF16), w_attr) + bias_ref[...]
        send0, send1 = level_pair(send_rows, w_send)
        recv0, recv1 = level_pair(recv_rows, w_recv)
        nodes = lax.broadcasted_iota(jnp.int32, (node_dev, WIDE), 0).astype(F32)
        deliver = jnp.where(nodes == receiver_row, 1.0, 0.0).astype(BF16)
        return (
            base + send0 + recv0,
            base + send1 + recv1,
            deliver,
            sender_column - node_dev,
            receiver_row,
        )

    @pl.loop(0, LATE_TILES)
    def _(index):
        pre0, pre1, _, wanted, receiver_row = arrange(index)
        rows = pl.ds(pl.multiple_of(index * WIDE, WIDE), WIDE)
        pre0_ref[rows, 0:width] = pre0
        pre1_ref[rows, 0:width] = pre1
        receivers_ref[index] = jnp.broadcast_to(receiver_row, receivers_ref.shape[1:])
        late_wanted_ref[rows, :] = jnp.broadcast_to(wanted, (WIDE, 128))

    @pl.loop(LATE_TILES, late_tiles)
    def _(index):
        rest0_ref[...], rest1_ref[...], rest3_ref[0], wanted, _ = arrange(index)
        rest2_ref[...] = jnp.broadcast_to(wanted, rest2_ref.shape)
        sends = [
            pltpu.make_async_copy(source, target.at[index - LATE_TILES], sent.at[slot])
            for slot, (source, target) in enumerate(
                (
                    (rest0_ref, pre0_hbm),
                    (rest1_ref, pre1_hbm),
                    (rest2_ref, wanted_hbm),
                    (rest3_ref.at[0], deliver_hbm),
                )
            )
        ]
        for send in sends:
            send.start()
        for send in sends:
            send.wait()

    @pl.loop(late_tiles, jnp.maximum(used_tiles, late_tiles))
    def _(index):
        pre0, pre1, deliver, _, _ = arrange(index)
        w_out = w_out_ref[...]
        sum0_ref[:, 0:width] += dot(deliver, dot(silu(pre0).astype(BF16), w_out).astype(BF16))
        sum1_ref[:, 0:width] += dot(deliver, dot(silu(pre1).astype(BF16), w_out).astype(BF16))


def edge_kernel(
    tiles_ref,
    late_wanted_ref,
    receivers_ref,
    late_pre0_hbm,
    late_pre1_hbm,
    own_hbm,
    node_pre0_hbm,
    node_pre1_hbm,
    sum0_hbm,
    sum1_hbm,
    pre0_hbm,
    pre1_hbm,
    wanted_hbm,
    deliver_hbm,
    w_in_ref,
    w_out_ref,
    node_w_in_ref,
    node_w_out_ref,
    node_gain_ref,
    attention_gain_ref,
    remote_ref,
    state_ref,
    out0_ref,
    out1_ref,
    out2_ref,
    out3_ref,
    normed_ref,
    late_pre0_ref,
    late_pre1_ref,
    node_pre0_ref,
    node_pre1_ref,
    own_ref,
    total0_ref,
    total1_ref,
    rest0_ref,
    rest1_ref,
    rest2_ref,
    rest3_ref,
    early_arrived,
    arrived,
):
    width = w_out_ref.shape[0]
    early = [
        pltpu.make_async_copy(source, target, early_arrived.at[slot])
        for slot, (source, target) in enumerate(
            (
                (late_pre0_hbm, late_pre0_ref),
                (late_pre1_hbm, late_pre1_ref),
                (sum0_hbm, total0_ref),
                (sum1_hbm, total1_ref),
                (node_pre0_hbm, node_pre0_ref),
                (node_pre1_hbm, node_pre1_ref),
                (own_hbm, own_ref),
            )
        )
    ]
    for fetch in early:
        fetch.start()
    w_send = w_in_ref[0:width, :]

    def gather(wanted):
        lanes = lax.broadcasted_iota(jnp.int32, wanted.shape, 1).astype(F32)
        pick = jnp.concatenate(
            [
                jnp.where(wanted == lanes + float(first), 1.0, 0.0).astype(BF16)
                for first in range(0, remote_ref.shape[0], 128)
            ],
            axis=1,
        )
        return level_pair(dot(pick, remote_ref[...]).astype(BF16), w_send)

    def messages(pre, sent):
        return dot(silu(pre + sent).astype(BF16), w_out_ref[...]).astype(BF16)

    sent0, sent1 = gather(late_wanted_ref[...])
    early[0].wait()
    message0 = messages(late_pre0_ref[:, 0:width], sent0)
    early[1].wait()
    message1 = messages(late_pre1_ref[:, 0:width], sent1)
    nodes = lax.broadcasted_iota(jnp.int32, (state_ref.shape[0], WIDE), 0).astype(F32)
    deliver = jnp.concatenate(
        [
            jnp.where(nodes == receivers_ref[block][0:1, :], 1.0, 0.0).astype(BF16)
            for block in range(LATE_TILES)
        ],
        axis=1,
    )
    arrived0, arrived1 = dot(deliver, message0), dot(deliver, message1)
    for fetch in early[2:]:
        fetch.wait()
    total0_ref[:, 0:width] += arrived0
    total1_ref[:, 0:width] += arrived1

    @pl.loop(LATE_TILES, tiles_ref[0, 0])
    def _(index):
        fetches = [
            pltpu.make_async_copy(source.at[index - LATE_TILES], target, arrived.at[slot])
            for slot, (source, target) in enumerate(
                (
                    (pre0_hbm, rest0_ref),
                    (pre1_hbm, rest1_ref),
                    (wanted_hbm, rest2_ref),
                    (deliver_hbm, rest3_ref.at[0]),
                )
            )
        ]
        for fetch in fetches:
            fetch.start()
        for fetch in fetches:
            fetch.wait()
        sent0, sent1 = gather(rest2_ref[...])
        total0_ref[:, 0:width] += dot(rest3_ref[0], messages(rest0_ref[...], sent0))
        total1_ref[:, 0:width] += dot(rest3_ref[0], messages(rest1_ref[...], sent1))

    own = own_ref[...]
    own_pair = (node_pre0_ref[:, 0:width], node_pre1_ref[:, 0:width])
    own_values = (own[:, :width], own[:, width:])
    states = []
    normed = []
    for level, total_ref in enumerate((total0_ref, total1_ref)):
        summed = total_ref[:, 0:width].astype(BF16)
        node_pre = own_pair[level] + dot(summed, node_w_in_ref[width : 2 * width, :])
        update = dot(silu(node_pre).astype(BF16), node_w_out_ref[...])
        state = (
            own_values[level].astype(F32) + node_gain_ref[...] * normalize(update)
        ).astype(BF16)
        states.append(state)
        normed.append(
            (attention_gain_ref[...] * normalize(state.astype(F32))).astype(BF16)
        )
    state_ref[...] = merge_levels(*states)
    normed_ref[...] = merge_levels(*normed)
    share = out0_ref.shape[0]
    place = tiles_ref[0, 1]
    for shift, out_ref in enumerate((out0_ref, out1_ref, out2_ref, out3_ref)):
        block = lax.rem(place + shift, CHIPS)
        out_ref[...] = normed_ref[pl.ds(pl.multiple_of(block * share, share), share), :]


def attention_kernel(*refs):
    block_refs, refs = refs[: CHIPS * CORES], refs[CHIPS * CORES :]
    bias_ref, query_ref, key_ref, value_ref, *out_refs, mix_ref = refs
    block_count = len(block_refs)
    item_count, merged = block_refs[0].shape
    width = merged // 2
    head_width = width // HEADS
    scale = 1.0 / math.sqrt(head_width)
    key_total = 2 * block_count * CHUNK
    query_total = 2 * CHIPS * CHUNK
    head_of = lax.broadcasted_iota(jnp.int32, (1, width), 1) // head_width
    same_node = (
        lax.broadcasted_iota(jnp.int32, (query_total, key_total), 0) % CHUNK
        == lax.broadcasted_iota(jnp.int32, (query_total, key_total), 1) % CHUNK
    )
    blocks = jnp.concatenate([ref[...] for ref in block_refs], axis=0)

    def project(count, weight_ref):
        return [
            p.reshape(count, item_count, width)
            for p in level_pair(blocks[: count * item_count], weight_ref[...])
        ]

    def rows_of(pair, part):
        items = slice(part * CHUNK, (part + 1) * CHUNK)
        return jnp.concatenate([p[:, items, :].reshape(-1, width) for p in pair], axis=0).astype(BF16)

    def per_head(rows):
        return jnp.concatenate(
            [rows * jnp.where(head_of == head, 1.0, 0.0).astype(BF16) for head in range(HEADS)],
            axis=0,
        )

    queries = project(CHIPS, query_ref)
    keys, values = project(block_count, key_ref), project(block_count, value_ref)
    ones = per_head(jnp.ones((key_total, width), BF16))
    all_powers, mixes = [], []
    for part in range(item_count // CHUNK):
        bias = jnp.where(same_node, bias_ref[part], -1e30)
        scores = dot_lanes(rows_of(queries, part), per_head(rows_of(keys, part)))
        powers = []
        for head in range(HEADS):
            own_scores = scores[:, head * key_total : (head + 1) * key_total] * scale + bias
            top = jnp.max(own_scores, axis=-1, keepdims=True)
            powers.append(jnp.exp(own_scores - top).astype(BF16))
        powers = jnp.concatenate(powers, axis=1)
        all_powers.append(powers)
        mixes.append(dot(powers, per_head(rows_of(values, part))))
    sums = dot(jnp.concatenate(all_powers, axis=0), ones)
    for part, mix in enumerate(mixes):
        attended = mix / sums[part * query_total : (part + 1) * query_total]
        mix_ref[:, :, part * CHUNK : (part + 1) * CHUNK, :] = attended.reshape(
            2, CHIPS, CHUNK, width
        )
    for chip, out_ref in enumerate(out_refs):
        out_ref[...] = merge_levels(mix_ref[0, chip].astype(BF16), mix_ref[1, chip].astype(BF16))


def output_kernel(
    place_ref, state_ref, part0_ref, part1_ref, part2_ref, part3_ref, live_ref, weight_ref, out_ref,
    attended_ref,
):
    width = weight_ref.shape[0]
    share = part0_ref.shape[0]
    place = place_ref[0, 1]
    for shift, part_ref in enumerate((part0_ref, part1_ref, part2_ref, part3_ref)):
        block = lax.rem(place + shift, CHIPS)
        attended_ref[pl.ds(pl.multiple_of(block * share, share), share), :] = part_ref[...]
    mixed = level_pair(attended_ref[...], weight_ref[...])
    state = state_ref[...].astype(F32)
    for level in range(2):
        live_part = mixed[level] * live_ref[:, level : level + 1]
        result = state[:, level * width : (level + 1) * width] + live_part
        out_ref[level] = result.T.astype(BF16)


def call(kernel, out_shape, *operands, scratch=(), **specs):
    return pl.pallas_call(
        kernel,
        out_shape=out_shape,
        **specs,
        scratch_shapes=list(scratch),
        compiler_params=pltpu.CompilerParams(vmem_limit_bytes=VMEM_BYTES),
    )(*operands)


def shape(dims, dtype=BF16):
    return jax.ShapeDtypeStruct(dims, dtype)


def kept(array):
    return pltpu.with_memory_space_constraint(array, pltpu.VMEM)


def in_hbm(array):
    return pltpu.with_memory_space_constraint(array, pltpu.HBM)


IN_SMEM = pl.BlockSpec(memory_space=pltpu.SMEM)
IN_VMEM = pl.BlockSpec(memory_space=pltpu.VMEM)
ANYWHERE = pl.BlockSpec(memory_space=pl.ANY)


def per_device(
    node_state,
    edge_attr,
    edge_sender,
    edge_receiver,
    tile_block,
    halo_rows,
    valid_levels,
    edge_w_in,
    edge_bias,
    edge_w_out,
    node_w_in,
    node_bias,
    node_w_out,
    node_gain,
    attention_gain,
    query_weight,
    key_weight,
    value_weight,
    output_weight,
):
    group_count = lax.axis_size("lev")
    node_dev, lev_dev, width = node_state.shape
    tile_count = tile_block.shape[0]
    patch_count, slot_count = halo_rows.shape
    merged = lev_dev * width
    remote_count = patch_count * slot_count
    edge_count = edge_attr.shape[0]
    own = node_state.transpose(1, 2, 0).reshape(merged, node_dev)
    outgoing = call(
        halo_kernel,
        shape((remote_count, merged)),
        in_hbm(halo_rows),
        in_hbm(own),
        in_specs=[ANYWHERE] * 2,
        out_specs=ANYWHERE,
        scratch=[
            pltpu.VMEM((patch_count, slot_count), jnp.int32),
            pltpu.VMEM((merged, node_dev), BF16),
            pltpu.VMEM((remote_count, merged), BF16),
            pltpu.SemaphoreType.DMA((2,)),
            pltpu.SemaphoreType.DMA((4,)),
        ],
    )
    incoming = lax.all_to_all(
        outgoing.reshape(patch_count, slot_count, merged),
        "patch",
        split_axis=0,
        concat_axis=0,
        tiled=True,
    ).reshape(remote_count, merged)

    senders = edge_sender.reshape(tile_count, 128)
    in_block = edge_receiver.reshape(tile_count, 128)
    receivers = jnp.where(in_block >= 0, tile_block[:, None] * 128 + in_block, -1)
    share = node_dev // CHIPS
    me = lax.axis_index("lev")
    chip, core = me // CORES, me % CORES
    mine = lax.dynamic_slice_in_dim(valid_levels, chip * share, share)
    block = jnp.arange(CHIPS * CORES, dtype=jnp.int32)
    from_chip = (chip - block % CHIPS) % CHIPS
    from_core = jnp.where(block < CHIPS, core, 1 - core)
    level_of = (
        ((from_chip * CORES + from_core) * lev_dev)[None, :, None]
        + jnp.arange(lev_dev, dtype=jnp.int32)[:, None, None]
    )
    key_bias = jnp.where(
        level_of[None] < mine.reshape(share // CHUNK, 1, 1, CHUNK), 0.0, -1e30
    ).reshape(share // CHUNK, 1, lev_dev * group_count * CHUNK)
    levels = me * lev_dev + jnp.arange(lev_dev, dtype=jnp.int32)
    live = (levels[None, :] < valid_levels[:, None]).astype(F32)

    rest = edge_count // WIDE - LATE_TILES
    late = LATE_TILES * WIDE
    rest_shapes = [
        ((WIDE, width), F32),
        ((WIDE, width), F32),
        ((WIDE, 128), F32),
        ((1, node_dev, WIDE), BF16),
    ]
    tiles, wanted, pre0, pre1, late_receivers, *tail = call(
        local_kernel,
        (
            pltpu.VMEM((8, 128), jnp.int32),
            pltpu.VMEM((late, 128), F32),
            pltpu.HBM((late, WIDE), F32),
            pltpu.HBM((late, WIDE), F32),
            pltpu.VMEM((LATE_TILES, 8, WIDE), F32),
            pltpu.HBM((node_dev, merged), BF16),
            *[pltpu.HBM((node_dev, WIDE), F32)] * 4,
            pltpu.HBM((rest, WIDE, width), F32),
            pltpu.HBM((rest, WIDE, width), F32),
            pltpu.HBM((rest, WIDE, 128), F32),
            pltpu.HBM((rest, node_dev, WIDE), BF16),
        ),
        chip.reshape(1),
        senders,
        receivers,
        in_hbm(edge_attr.T),
        in_hbm(own),
        edge_w_in,
        edge_bias[None, :],
        edge_w_out,
        node_w_in,
        node_bias[None, :],
        scratch=[
            pltpu.VMEM((merged, node_dev), BF16),
            pltpu.VMEM((tile_count, 128), F32),
            pltpu.VMEM((width + 16, edge_count), BF16),
            *(pltpu.VMEM(*entry) for entry in rest_shapes),
            pltpu.SemaphoreType.DMA((4,)),
            pltpu.SemaphoreType.DMA((2,)),
        ],
        in_specs=[IN_SMEM] + [IN_VMEM] * 2 + [ANYWHERE] * 2 + [IN_VMEM] * 5,
        out_specs=[IN_VMEM] * 10 + [ANYWHERE] * 4,
    )
    state, *blocks = call(
        edge_kernel,
        (pltpu.VMEM((node_dev, merged), BF16), *[shape((share, merged))] * CHIPS),
        kept(tiles),
        kept(wanted),
        kept(late_receivers),
        in_hbm(pre0),
        in_hbm(pre1),
        *(in_hbm(array) for array in tail),
        edge_w_in,
        edge_w_out,
        node_w_in,
        node_w_out,
        node_gain[None, :],
        attention_gain[None, :],
        incoming,
        scratch=[
            pltpu.VMEM((node_dev, merged), BF16),
            pltpu.VMEM((late, WIDE), F32),
            pltpu.VMEM((late, WIDE), F32),
            pltpu.VMEM((node_dev, WIDE), F32),
            pltpu.VMEM((node_dev, WIDE), F32),
            pltpu.VMEM((node_dev, merged), BF16),
            pltpu.VMEM((node_dev, WIDE), F32),
            pltpu.VMEM((node_dev, WIDE), F32),
            *(pltpu.VMEM(*entry) for entry in rest_shapes),
            pltpu.SemaphoreType.DMA((7,)),
            pltpu.SemaphoreType.DMA((4,)),
        ],
        in_specs=[IN_VMEM] * 3 + [ANYWHERE] * 11 + [IN_VMEM] * 7,
    )

    def to_chip(array, shift):
        return lax.ppermute(
            array,
            "lev",
            [
                (a * CORES + b, (a + shift) % CHIPS * CORES + b)
                for a in range(CHIPS)
                for b in range(CORES)
            ],
        )

    def to_core(array):
        return lax.ppermute(array, "lev", [(a, a ^ 1) for a in range(CHIPS * CORES)])

    blocks = blocks[:1] + [to_chip(blocks[shift], shift) for shift in range(1, CHIPS)]
    blocks = blocks + [to_core(array) for array in blocks]
    attended = call(
        attention_kernel,
        [shape((share, merged))] * CHIPS,
        *blocks,
        key_bias,
        query_weight,
        key_weight,
        value_weight,
        scratch=[pltpu.VMEM((lev_dev, CHIPS, share, width), F32)],
    )
    returned = [attended[0]] + [to_chip(attended[shift], -shift) for shift in range(1, CHIPS)]
    out = call(
        output_kernel,
        shape((lev_dev, width, node_dev)),
        kept(tiles),
        kept(state),
        *returned,
        live,
        output_weight,
        scratch=[pltpu.VMEM((node_dev, merged), BF16)],
    )
    return out.transpose(2, 0, 1)


def solution(mesh):
    in_specs = (
        P("patch", "lev", None),
        P("patch", None),
        P("patch"),
        P("patch"),
        P("patch"),
        P("patch", None),
        P("patch"),
    ) + (P(),) * 12
    out_specs = P("patch", "lev", None)
    return jax.shard_map(
        per_device, mesh=mesh, in_specs=in_specs, out_specs=out_specs, check_vma=False
    )
```

```python
import math

import jax
import jax.numpy as jnp
from jax import lax
from jax.experimental import pallas as pl
from jax.experimental.pallas import tpu as pltpu
from jax.sharding import PartitionSpec as P

HEADS = 4
BF16 = jnp.bfloat16
F32 = jnp.float32
VMEM_BYTES = 20 * 1024 * 1024
WIDE = 256
LATE_TILES = 3
CHUNK = 8
CHIPS = 4
CORES = 2


def dot(a, b):
    return jnp.dot(a, b, preferred_element_type=F32)


def dot_lanes(a, b):
    return lax.dot_general(a, b, (((1,), (1,)), ((), ())), preferred_element_type=F32)


def silu(v):
    return v / (1.0 + jnp.exp(-v))


def normalize_all(arrays):
    means = [jnp.mean(values, axis=-1, keepdims=True) for values in arrays]
    centered = [values - mean for values, mean in zip(arrays, means, strict=True)]
    spreads = [jnp.mean(values * values, axis=-1, keepdims=True) for values in centered]
    return [
        values * lax.rsqrt(spread + 1e-05)
        for values, spread in zip(centered, spreads, strict=True)
    ]


def onehot(column, width):
    lanes = lax.broadcasted_iota(jnp.int32, (column.shape[0], width), 1).astype(F32)
    return jnp.where(column == lanes, 1.0, 0.0).astype(BF16)


def level_pair(merged, weight):
    depth, width = weight.shape
    half = merged.shape[1] // 2
    cut = half // 128 * 128
    filler = jnp.zeros((half - cut, width), weight.dtype)
    first = jnp.concatenate([weight, filler], axis=0)
    second = jnp.concatenate([filler, weight], axis=0)
    return (
        dot(merged[:, : half + half - cut], first),
        dot(merged[:, cut:], second),
    )


def merge_levels(first, second):
    return jnp.concatenate([first, second], axis=1)


def halo_kernel(halo_hbm, own_hbm, out_hbm, halo_ref, own_ref, rows_ref, arrived, sent):
    patch_count, slot_count = halo_ref.shape
    fetches = [
        pltpu.make_async_copy(halo_hbm, halo_ref, arrived.at[0]),
        pltpu.make_async_copy(own_hbm, own_ref, arrived.at[1]),
    ]
    for fetch in fetches:
        fetch.start()
    fetches[0].wait()
    columns = halo_ref[...].astype(F32).T
    sends = []
    step = patch_count // 4
    for part in range(4):
        pick = jnp.concatenate(
            [
                onehot(columns[:, patch : patch + 1], own_ref.shape[1])
                for patch in range(part * step, (part + 1) * step)
            ],
            axis=0,
        )
        if part == 0:
            fetches[1].wait()
        rows = slice(part * step * slot_count, (part + 1) * step * slot_count)
        rows_ref[rows, :] = dot_lanes(pick, own_ref[...]).astype(BF16)
        sends.append(
            pltpu.make_async_copy(rows_ref.at[rows], out_hbm.at[rows], sent.at[part])
        )
        sends[-1].start()
    for send in sends:
        send.wait()


def running_count(flags):
    tile_count, tile = flags.shape
    flags = flags.astype(BF16)
    before = lax.broadcasted_iota(jnp.int32, (tile, tile), 0) < lax.broadcasted_iota(
        jnp.int32, (tile, tile), 1
    )
    above = lax.broadcasted_iota(jnp.int32, (tile_count, tile_count), 1) < lax.broadcasted_iota(
        jnp.int32, (tile_count, tile_count), 0
    )
    inside = dot(flags, jnp.where(before, 1.0, 0.0).astype(BF16))
    totals = dot(flags, jnp.ones((tile, tile), BF16)).astype(BF16)
    return (
        inside + dot(jnp.where(above, 1.0, 0.0).astype(BF16), totals),
        dot(jnp.ones((tile_count, tile_count), BF16), totals),
    )


def local_kernel(
    place_ref,
    sender_ref,
    receiver_ref,
    attr_hbm,
    own_hbm,
    w_in_ref,
    bias_ref,
    w_out_ref,
    node_w_in_ref,
    node_bias_ref,
    tiles_ref,
    late_wanted_ref,
    pre0_ref,
    pre1_ref,
    receivers_ref,
    own_rows_ref,
    node_pre0_ref,
    node_pre1_ref,
    sum0_ref,
    sum1_ref,
    pre0_hbm,
    pre1_hbm,
    wanted_hbm,
    deliver_hbm,
    own_ref,
    position_ref,
    table_ref,
    rest0_ref,
    rest1_ref,
    rest2_ref,
    rest3_ref,
    sent,
    arrived,
):
    fetches = [
        pltpu.make_async_copy(own_hbm, own_ref, arrived.at[0]),
        pltpu.make_async_copy(attr_hbm, table_ref.at[0 : attr_hbm.shape[0]], arrived.at[1]),
    ]
    for fetch in fetches:
        fetch.start()
    tile_count, tile = sender_ref.shape
    width, edge_count = attr_hbm.shape
    merged, node_dev = own_ref.shape
    eye = jnp.where(
        lax.broadcasted_iota(jnp.int32, (node_dev, node_dev), 0)
        == lax.broadcasted_iota(jnp.int32, (node_dev, node_dev), 1),
        1.0,
        0.0,
    ).astype(BF16)
    senders = sender_ref[...]
    receivers = receiver_ref[...]
    used = receivers >= 0
    is_remote = jnp.where(used & (senders >= node_dev), 1.0, 0.0)
    is_local = jnp.where(used & (senders < node_dev), 1.0, 0.0)
    is_empty = jnp.where(used, 0.0, 1.0)
    remote_rank, remote_total = running_count(is_remote)
    local_rank, local_total = running_count(is_local)
    empty_rank, _ = running_count(is_empty)
    position_ref[...] = jnp.where(
        is_remote > 0.0,
        remote_rank,
        jnp.where(
            is_local > 0.0, remote_total + local_rank, remote_total + local_total + empty_rank
        ),
    )
    remote_tiles = (jnp.sum(is_remote).astype(jnp.int32) + WIDE - 1) // WIDE
    used_tiles = (jnp.sum(1.0 - is_empty).astype(jnp.int32) + WIDE - 1) // WIDE
    late_tiles = jnp.maximum(remote_tiles, LATE_TILES)
    slot = lax.broadcasted_iota(jnp.int32, tiles_ref.shape, 1)
    tiles_ref[...] = jnp.where(slot == 0, late_tiles, place_ref[0])
    for fetch in fetches:
        fetch.wait()
    own_rows_ref[...] = dot_lanes(eye, own_ref[...]).astype(BF16)
    own_pair = level_pair(own_rows_ref[...], node_w_in_ref[0:width, :])
    node_pre0_ref[:, 0:width] = own_pair[0] + node_bias_ref[...]
    node_pre1_ref[:, 0:width] = own_pair[1] + node_bias_ref[...]
    table_ref[width:, :] = jnp.zeros((table_ref.shape[0] - width, edge_count), BF16)
    for index in range(tile_count):
        lanes = slice(index * tile, (index + 1) * tile)
        row = senders[index : index + 1, :]
        table_ref[width : width + 16, lanes] = jnp.concatenate(
            [
                (row // tile).astype(F32),
                (row % tile).astype(F32),
                receivers[index : index + 1, :].astype(F32),
                jnp.zeros((13, tile), F32),
            ],
            axis=0,
        ).astype(BF16)
    w_send = w_in_ref[0:width, :]
    w_recv = w_in_ref[width : 2 * width, :]
    w_attr = w_in_ref[2 * width : 3 * width, :]
    sum0_ref[...] = jnp.zeros_like(sum0_ref)
    sum1_ref[...] = jnp.zeros_like(sum1_ref)

    def arrange(index):
        wanted = lax.broadcasted_iota(jnp.int32, (WIDE, tile), 0).astype(F32) + (
            index * WIDE
        ).astype(F32)
        order = jnp.concatenate(
            [
                jnp.where(position_ref[t : t + 1, :] == wanted, 1.0, 0.0).astype(BF16)
                for t in range(tile_count)
            ],
            axis=1,
        )
        moved = dot_lanes(order, table_ref[...])
        receiver_row = dot_lanes(table_ref[width : width + 16, :], order)[2:3, :]
        sender_column = moved[:, width : width + 1] * tile + moved[:, width + 1 : width + 2]
        receiver_column = moved[:, width + 2 : width + 3]
        own = own_rows_ref[...]
        send_rows = dot(onehot(sender_column, node_dev), own).astype(BF16)
        recv_rows = dot(onehot(receiver_column, node_dev), own).astype(BF16)
        base = dot(moved[:, :width].astype(BF16), w_attr) + bias_ref[...]
        send0, send1 = level_pair(send_rows, w_send)
        recv0, recv1 = level_pair(recv_rows, w_recv)
        nodes = lax.broadcasted_iota(jnp.int32, (node_dev, WIDE), 0).astype(F32)
        deliver = jnp.where(nodes == receiver_row, 1.0, 0.0).astype(BF16)
        return (
            base + send0 + recv0,
            base + send1 + recv1,
            deliver,
            sender_column - node_dev,
            receiver_row,
        )

    @pl.loop(0, LATE_TILES)
    def _(index):
        pre0, pre1, _, wanted, receiver_row = arrange(index)
        rows = pl.ds(pl.multiple_of(index * WIDE, WIDE), WIDE)
        pre0_ref[rows, 0:width] = pre0
        pre1_ref[rows, 0:width] = pre1
        receivers_ref[index] = jnp.broadcast_to(receiver_row, receivers_ref.shape[1:])
        late_wanted_ref[rows, :] = jnp.broadcast_to(wanted, (WIDE, 128))

    @pl.loop(LATE_TILES, late_tiles)
    def _(index):
        rest0_ref[...], rest1_ref[...], rest3_ref[0], wanted, _ = arrange(index)
        rest2_ref[...] = jnp.broadcast_to(wanted, rest2_ref.shape)
        sends = [
            pltpu.make_async_copy(source, target.at[index - LATE_TILES], sent.at[slot])
            for slot, (source, target) in enumerate(
                (
                    (rest0_ref, pre0_hbm),
                    (rest1_ref, pre1_hbm),
                    (rest2_ref, wanted_hbm),
                    (rest3_ref.at[0], deliver_hbm),
                )
            )
        ]
        for send in sends:
            send.start()
        for send in sends:
            send.wait()

    @pl.loop(late_tiles, jnp.maximum(used_tiles, late_tiles))
    def _(index):
        pre0, pre1, deliver, _, _ = arrange(index)
        w_out = w_out_ref[...]
        sum0_ref[:, 0:width] += dot(deliver, dot(silu(pre0).astype(BF16), w_out).astype(BF16))
        sum1_ref[:, 0:width] += dot(deliver, dot(silu(pre1).astype(BF16), w_out).astype(BF16))


def edge_kernel(
    tiles_ref,
    late_wanted_ref,
    receivers_ref,
    late_pre0_hbm,
    late_pre1_hbm,
    own_hbm,
    node_pre0_hbm,
    node_pre1_hbm,
    sum0_hbm,
    sum1_hbm,
    pre0_hbm,
    pre1_hbm,
    wanted_hbm,
    deliver_hbm,
    w_in_ref,
    w_out_ref,
    node_w_in_ref,
    node_w_out_ref,
    node_gain_ref,
    attention_gain_ref,
    remote_ref,
    state_ref,
    out0_ref,
    out1_ref,
    out2_ref,
    out3_ref,
    normed_ref,
    late_pre0_ref,
    late_pre1_ref,
    node_pre0_ref,
    node_pre1_ref,
    own_ref,
    total0_ref,
    total1_ref,
    rest0_ref,
    rest1_ref,
    rest2_ref,
    rest3_ref,
    early_arrived,
    arrived,
):
    width = w_out_ref.shape[0]
    early = [
        pltpu.make_async_copy(source, target, early_arrived.at[slot])
        for slot, (source, target) in enumerate(
            (
                (late_pre0_hbm, late_pre0_ref),
                (late_pre1_hbm, late_pre1_ref),
                (sum0_hbm, total0_ref),
                (sum1_hbm, total1_ref),
                (node_pre0_hbm, node_pre0_ref),
                (node_pre1_hbm, node_pre1_ref),
                (own_hbm, own_ref),
            )
        )
    ]
    for fetch in early:
        fetch.start()
    w_send = w_in_ref[0:width, :]

    def gather(wanted):
        lanes = lax.broadcasted_iota(jnp.int32, wanted.shape, 1).astype(F32)
        pick = jnp.concatenate(
            [
                jnp.where(wanted == lanes + float(first), 1.0, 0.0).astype(BF16)
                for first in range(0, remote_ref.shape[0], 128)
            ],
            axis=1,
        )
        return level_pair(dot(pick, remote_ref[...]).astype(BF16), w_send)

    def messages(pre, sent):
        return dot(silu(pre + sent).astype(BF16), w_out_ref[...]).astype(BF16)

    sent0, sent1 = gather(late_wanted_ref[...])
    early[0].wait()
    message0 = messages(late_pre0_ref[:, 0:width], sent0)
    early[1].wait()
    message1 = messages(late_pre1_ref[:, 0:width], sent1)
    nodes = lax.broadcasted_iota(jnp.int32, (state_ref.shape[0], WIDE), 0).astype(F32)
    deliver = jnp.concatenate(
        [
            jnp.where(nodes == receivers_ref[block][0:1, :], 1.0, 0.0).astype(BF16)
            for block in range(LATE_TILES)
        ],
        axis=1,
    )
    arrived0, arrived1 = dot(deliver, message0), dot(deliver, message1)
    for fetch in early[2:]:
        fetch.wait()
    total0_ref[:, 0:width] += arrived0
    total1_ref[:, 0:width] += arrived1

    @pl.loop(LATE_TILES, tiles_ref[0, 0])
    def _(index):
        fetches = [
            pltpu.make_async_copy(source.at[index - LATE_TILES], target, arrived.at[slot])
            for slot, (source, target) in enumerate(
                (
                    (pre0_hbm, rest0_ref),
                    (pre1_hbm, rest1_ref),
                    (wanted_hbm, rest2_ref),
                    (deliver_hbm, rest3_ref.at[0]),
                )
            )
        ]
        for fetch in fetches:
            fetch.start()
        for fetch in fetches:
            fetch.wait()
        sent0, sent1 = gather(rest2_ref[...])
        total0_ref[:, 0:width] += dot(rest3_ref[0], messages(rest0_ref[...], sent0))
        total1_ref[:, 0:width] += dot(rest3_ref[0], messages(rest1_ref[...], sent1))

    own = own_ref[...]
    own_pair = (node_pre0_ref[:, 0:width], node_pre1_ref[:, 0:width])
    own_values = (own[:, :width], own[:, width:])
    levels = range(2)
    summed = [total0_ref[:, 0:width].astype(BF16), total1_ref[:, 0:width].astype(BF16)]
    w_summed = node_w_in_ref[width : 2 * width, :]
    node_pre = [own_pair[level] + dot(summed[level], w_summed) for level in levels]
    hidden = [silu(node_pre[level]).astype(BF16) for level in levels]
    update = [dot(hidden[level], node_w_out_ref[...]) for level in levels]
    update = normalize_all(update)
    states = [
        (own_values[level].astype(F32) + node_gain_ref[...] * update[level]).astype(BF16)
        for level in levels
    ]
    normed = normalize_all([state.astype(F32) for state in states])
    normed = [(attention_gain_ref[...] * rows).astype(BF16) for rows in normed]
    state_ref[...] = merge_levels(*states)
    normed_ref[...] = merge_levels(*normed)
    share = out0_ref.shape[0]
    place = tiles_ref[0, 1]
    for shift, out_ref in enumerate((out0_ref, out1_ref, out2_ref, out3_ref)):
        block = lax.rem(place + shift, CHIPS)
        out_ref[...] = normed_ref[pl.ds(pl.multiple_of(block * share, share), share), :]


def attention_kernel(*refs):
    block_refs, refs = refs[: CHIPS * CORES], refs[CHIPS * CORES :]
    bias_ref, query_ref, key_ref, value_ref, *out_refs, mix_ref = refs
    block_count = len(block_refs)
    item_count, merged = block_refs[0].shape
    width = merged // 2
    head_width = width // HEADS
    scale = 1.0 / math.sqrt(head_width)
    key_total = 2 * block_count * CHUNK
    query_total = 2 * CHIPS * CHUNK
    head_of = lax.broadcasted_iota(jnp.int32, (1, width), 1) // head_width
    in_head = [jnp.where(head_of == head, 1.0, 0.0) for head in range(HEADS)]
    same_node = (
        lax.broadcasted_iota(jnp.int32, (HEADS * query_total, key_total), 0) % CHUNK
        == lax.broadcasted_iota(jnp.int32, (HEADS * query_total, key_total), 1) % CHUNK
    )
    blocks = jnp.concatenate([ref[...] for ref in block_refs], axis=0)

    def project(count, weight):
        return [
            p.reshape(count, item_count, weight.shape[1])
            for p in level_pair(blocks[: count * item_count], weight)
        ]

    def rows_of(pair, part):
        items = slice(part * CHUNK, (part + 1) * CHUNK)
        return jnp.concatenate(
            [p[:, items, :].reshape(-1, p.shape[2]) for p in pair], axis=0
        ).astype(BF16)

    queries = project(CHIPS, query_ref[...])
    keys = project(block_count, key_ref[...])
    wide_value = jnp.concatenate(
        [value_ref[...], jnp.zeros((width, WIDE - width), BF16)], axis=1
    )
    lanes = lax.broadcasted_iota(jnp.int32, (1, 1, WIDE), 2)
    values = [p + jnp.where(lanes < width, 0.0, 1.0) for p in project(block_count, wide_value)]
    parts = range(item_count // CHUNK)
    headed = [rows_of(queries, part) for part in parts]
    headed = [
        jnp.concatenate([rows * mask.astype(BF16) for mask in in_head], axis=0) for rows in headed
    ]
    scores = [dot_lanes(headed[part], rows_of(keys, part)) for part in parts]
    scores = [
        scores[part] * scale + jnp.where(same_node, bias_ref[part], -1e30) for part in parts
    ]
    tops = [jnp.max(part_scores, axis=-1, keepdims=True) for part_scores in scores]
    powers = [jnp.exp(scores[part] - tops[part]).astype(BF16) for part in parts]
    mixes = [dot(powers[part], rows_of(values, part)) for part in parts]
    for part, mix in enumerate(mixes):
        mix = mix[:, :width] * (1.0 / mix[:, width : width + 1])
        attended = sum(
            mix[head * query_total : (head + 1) * query_total] * mask
            for head, mask in enumerate(in_head)
        )
        mix_ref[:, :, part * CHUNK : (part + 1) * CHUNK, :] = attended.reshape(
            2, CHIPS, CHUNK, width
        )
    for chip, out_ref in enumerate(out_refs):
        out_ref[...] = merge_levels(mix_ref[0, chip].astype(BF16), mix_ref[1, chip].astype(BF16))


def output_kernel(
    place_ref, state_ref, part0_ref, part1_ref, part2_ref, part3_ref, live_ref, weight_ref, out_ref,
    attended_ref,
):
    width = weight_ref.shape[0]
    share = part0_ref.shape[0]
    place = place_ref[0, 1]
    for shift, part_ref in enumerate((part0_ref, part1_ref, part2_ref, part3_ref)):
        block = lax.rem(place + shift, CHIPS)
        attended_ref[pl.ds(pl.multiple_of(block * share, share), share), :] = part_ref[...]
    mixed = level_pair(attended_ref[...], weight_ref[...])
    state = state_ref[...].astype(F32)
    for level in range(2):
        live_part = mixed[level] * live_ref[:, level : level + 1]
        result = state[:, level * width : (level + 1) * width] + live_part
        out_ref[level] = result.T.astype(BF16)


def call(kernel, out_shape, *operands, scratch=(), **specs):
    return pl.pallas_call(
        kernel,
        out_shape=out_shape,
        **specs,
        scratch_shapes=list(scratch),
        compiler_params=pltpu.CompilerParams(vmem_limit_bytes=VMEM_BYTES),
    )(*operands)


def shape(dims, dtype=BF16):
    return jax.ShapeDtypeStruct(dims, dtype)


def kept(array):
    return pltpu.with_memory_space_constraint(array, pltpu.VMEM)


def in_hbm(array):
    return pltpu.with_memory_space_constraint(array, pltpu.HBM)


IN_SMEM = pl.BlockSpec(memory_space=pltpu.SMEM)
IN_VMEM = pl.BlockSpec(memory_space=pltpu.VMEM)
ANYWHERE = pl.BlockSpec(memory_space=pl.ANY)


def per_device(
    node_state,
    edge_attr,
    edge_sender,
    edge_receiver,
    tile_block,
    halo_rows,
    valid_levels,
    edge_w_in,
    edge_bias,
    edge_w_out,
    node_w_in,
    node_bias,
    node_w_out,
    node_gain,
    attention_gain,
    query_weight,
    key_weight,
    value_weight,
    output_weight,
):
    group_count = lax.axis_size("lev")
    node_dev, lev_dev, width = node_state.shape
    tile_count = tile_block.shape[0]
    patch_count, slot_count = halo_rows.shape
    merged = lev_dev * width
    remote_count = patch_count * slot_count
    edge_count = edge_attr.shape[0]
    own = node_state.transpose(1, 2, 0).reshape(merged, node_dev)
    outgoing = call(
        halo_kernel,
        shape((remote_count, merged)),
        in_hbm(halo_rows),
        in_hbm(own),
        in_specs=[ANYWHERE] * 2,
        out_specs=ANYWHERE,
        scratch=[
            pltpu.VMEM((patch_count, slot_count), jnp.int32),
            pltpu.VMEM((merged, node_dev), BF16),
            pltpu.VMEM((remote_count, merged), BF16),
            pltpu.SemaphoreType.DMA((2,)),
            pltpu.SemaphoreType.DMA((4,)),
        ],
    )
    incoming = lax.all_to_all(
        outgoing.reshape(patch_count, slot_count, merged),
        "patch",
        split_axis=0,
        concat_axis=0,
        tiled=True,
    ).reshape(remote_count, merged)

    senders = edge_sender.reshape(tile_count, 128)
    in_block = edge_receiver.reshape(tile_count, 128)
    receivers = jnp.where(in_block >= 0, tile_block[:, None] * 128 + in_block, -1)
    share = node_dev // CHIPS
    me = lax.axis_index("lev")
    chip, core = me // CORES, me % CORES
    mine = lax.dynamic_slice_in_dim(valid_levels, chip * share, share)
    block = jnp.arange(CHIPS * CORES, dtype=jnp.int32)
    from_chip = (chip - block % CHIPS) % CHIPS
    from_core = jnp.where(block < CHIPS, core, 1 - core)
    level_of = (
        ((from_chip * CORES + from_core) * lev_dev)[None, :, None]
        + jnp.arange(lev_dev, dtype=jnp.int32)[:, None, None]
    )
    key_bias = jnp.where(
        level_of[None] < mine.reshape(share // CHUNK, 1, 1, CHUNK), 0.0, -1e30
    ).reshape(share // CHUNK, 1, lev_dev * group_count * CHUNK)
    levels = me * lev_dev + jnp.arange(lev_dev, dtype=jnp.int32)
    live = (levels[None, :] < valid_levels[:, None]).astype(F32)

    rest = edge_count // WIDE - LATE_TILES
    late = LATE_TILES * WIDE
    rest_shapes = [
        ((WIDE, width), F32),
        ((WIDE, width), F32),
        ((WIDE, 128), F32),
        ((1, node_dev, WIDE), BF16),
    ]
    tiles, wanted, pre0, pre1, late_receivers, *tail = call(
        local_kernel,
        (
            pltpu.VMEM((8, 128), jnp.int32),
            pltpu.VMEM((late, 128), F32),
            pltpu.HBM((late, WIDE), F32),
            pltpu.HBM((late, WIDE), F32),
            pltpu.VMEM((LATE_TILES, 8, WIDE), F32),
            pltpu.HBM((node_dev, merged), BF16),
            *[pltpu.HBM((node_dev, WIDE), F32)] * 4,
            pltpu.HBM((rest, WIDE, width), F32),
            pltpu.HBM((rest, WIDE, width), F32),
            pltpu.HBM((rest, WIDE, 128), F32),
            pltpu.HBM((rest, node_dev, WIDE), BF16),
        ),
        chip.reshape(1),
        senders,
        receivers,
        in_hbm(edge_attr.T),
        in_hbm(own),
        edge_w_in,
        edge_bias[None, :],
        edge_w_out,
        node_w_in,
        node_bias[None, :],
        scratch=[
            pltpu.VMEM((merged, node_dev), BF16),
            pltpu.VMEM((tile_count, 128), F32),
            pltpu.VMEM((width + 16, edge_count), BF16),
            *(pltpu.VMEM(*entry) for entry in rest_shapes),
            pltpu.SemaphoreType.DMA((4,)),
            pltpu.SemaphoreType.DMA((2,)),
        ],
        in_specs=[IN_SMEM] + [IN_VMEM] * 2 + [ANYWHERE] * 2 + [IN_VMEM] * 5,
        out_specs=[IN_VMEM] * 10 + [ANYWHERE] * 4,
    )
    state, *blocks = call(
        edge_kernel,
        (pltpu.VMEM((node_dev, merged), BF16), *[shape((share, merged))] * CHIPS),
        kept(tiles),
        kept(wanted),
        kept(late_receivers),
        in_hbm(pre0),
        in_hbm(pre1),
        *(in_hbm(array) for array in tail),
        edge_w_in,
        edge_w_out,
        node_w_in,
        node_w_out,
        node_gain[None, :],
        attention_gain[None, :],
        incoming,
        scratch=[
            pltpu.VMEM((node_dev, merged), BF16),
            pltpu.VMEM((late, WIDE), F32),
            pltpu.VMEM((late, WIDE), F32),
            pltpu.VMEM((node_dev, WIDE), F32),
            pltpu.VMEM((node_dev, WIDE), F32),
            pltpu.VMEM((node_dev, merged), BF16),
            pltpu.VMEM((node_dev, WIDE), F32),
            pltpu.VMEM((node_dev, WIDE), F32),
            *(pltpu.VMEM(*entry) for entry in rest_shapes),
            pltpu.SemaphoreType.DMA((7,)),
            pltpu.SemaphoreType.DMA((4,)),
        ],
        in_specs=[IN_VMEM] * 3 + [ANYWHERE] * 11 + [IN_VMEM] * 7,
    )

    def to_chip(array, shift):
        return lax.ppermute(
            array,
            "lev",
            [
                (a * CORES + b, (a + shift) % CHIPS * CORES + b)
                for a in range(CHIPS)
                for b in range(CORES)
            ],
        )

    def to_core(array):
        return lax.ppermute(array, "lev", [(a, a ^ 1) for a in range(CHIPS * CORES)])

    blocks = blocks[:1] + [to_chip(blocks[shift], shift) for shift in range(1, CHIPS)]
    blocks = blocks + [to_core(array) for array in blocks]
    attended = call(
        attention_kernel,
        [shape((share, merged))] * CHIPS,
        *blocks,
        key_bias,
        query_weight,
        key_weight,
        value_weight,
        scratch=[pltpu.VMEM((lev_dev, CHIPS, share, width), F32)],
    )
    returned = [attended[0]] + [to_chip(attended[shift], -shift) for shift in range(1, CHIPS)]
    out = call(
        output_kernel,
        shape((lev_dev, width, node_dev)),
        kept(tiles),
        kept(state),
        *returned,
        live,
        output_weight,
        scratch=[pltpu.VMEM((node_dev, merged), BF16)],
    )
    return out.transpose(2, 0, 1)


def solution(mesh):
    in_specs = (
        P("patch", "lev", None),
        P("patch", None),
        P("patch"),
        P("patch"),
        P("patch"),
        P("patch", None),
        P("patch"),
    ) + (P(),) * 12
    out_specs = P("patch", "lev", None)
    return jax.shard_map(
        per_device, mesh=mesh, in_specs=in_specs, out_specs=out_specs, check_vma=False
    )
```

```python
import math

import jax
import jax.numpy as jnp
from jax import lax
from jax.experimental import pallas as pl
from jax.experimental.pallas import tpu as pltpu
from jax.sharding import PartitionSpec as P

HEADS = 4
BF16 = jnp.bfloat16
F32 = jnp.float32
VMEM_BYTES = 20 * 1024 * 1024
WIDE = 256
LATE_TILES = 3
CHUNK = 8
CHIPS = 4
CORES = 2


def dot(a, b):
    return jnp.dot(a, b, preferred_element_type=F32)


def dot_lanes(a, b):
    return lax.dot_general(a, b, (((1,), (1,)), ((), ())), preferred_element_type=F32)


def silu(v):
    half = 0.5 * v
    return half + half * jnp.tanh(half)


def normalize_all(arrays):
    means = [jnp.mean(values, axis=-1, keepdims=True) for values in arrays]
    centered = [values - mean for values, mean in zip(arrays, means, strict=True)]
    spreads = [jnp.mean(values * values, axis=-1, keepdims=True) for values in centered]
    return [
        values * lax.rsqrt(spread + 1e-05)
        for values, spread in zip(centered, spreads, strict=True)
    ]


def onehot(column, width):
    lanes = lax.broadcasted_iota(jnp.int32, (column.shape[0], width), 1).astype(F32)
    return jnp.where(column == lanes, 1.0, 0.0).astype(BF16)


def level_pair(merged, weight):
    depth, width = weight.shape
    half = merged.shape[1] // 2
    cut = half // 128 * 128
    filler = jnp.zeros((half - cut, width), weight.dtype)
    first = jnp.concatenate([weight, filler], axis=0)
    second = jnp.concatenate([filler, weight], axis=0)
    return (
        dot(merged[:, : half + half - cut], first),
        dot(merged[:, cut:], second),
    )


def put_pair(ref, rows, first, second):
    width = first.shape[1]
    ref[rows, 0:width] = first
    ref[rows, WIDE:] = second[:, : 2 * width - WIDE]
    ref[rows, width:WIDE] = second[:, 2 * width - WIDE :]


def get_pair(ref):
    width = ref.shape[1] // 2
    return (
        ref[:, 0:width],
        jnp.concatenate([ref[:, WIDE:], ref[:, width:WIDE]], axis=1),
    )


def merge_levels(first, second):
    return jnp.concatenate([first, second], axis=1)


def halo_kernel(halo_hbm, own_hbm, out_hbm, halo_ref, own_ref, rows_ref, arrived, sent):
    patch_count, slot_count = halo_ref.shape
    fetches = [
        pltpu.make_async_copy(halo_hbm, halo_ref, arrived.at[0]),
        pltpu.make_async_copy(own_hbm, own_ref, arrived.at[1]),
    ]
    for fetch in fetches:
        fetch.start()
    fetches[0].wait()
    columns = halo_ref[...].astype(F32).T
    sends = []
    step = patch_count // 4
    for part in range(4):
        pick = jnp.concatenate(
            [
                onehot(columns[:, patch : patch + 1], own_ref.shape[1])
                for patch in range(part * step, (part + 1) * step)
            ],
            axis=0,
        )
        if part == 0:
            fetches[1].wait()
        rows = slice(part * step * slot_count, (part + 1) * step * slot_count)
        rows_ref[rows, :] = dot_lanes(pick, own_ref[...]).astype(BF16)
        sends.append(
            pltpu.make_async_copy(rows_ref.at[rows], out_hbm.at[rows], sent.at[part])
        )
        sends[-1].start()
    for send in sends:
        send.wait()


def running_count(flags):
    tile_count, tile = flags.shape
    flags = flags.astype(BF16)
    before = lax.broadcasted_iota(jnp.int32, (tile, tile), 0) < lax.broadcasted_iota(
        jnp.int32, (tile, tile), 1
    )
    above = lax.broadcasted_iota(jnp.int32, (tile_count, tile_count), 1) < lax.broadcasted_iota(
        jnp.int32, (tile_count, tile_count), 0
    )
    inside = dot(flags, jnp.where(before, 1.0, 0.0).astype(BF16))
    totals = dot(flags, jnp.ones((tile, tile), BF16)).astype(BF16)
    return (
        inside + dot(jnp.where(above, 1.0, 0.0).astype(BF16), totals),
        dot(jnp.ones((tile_count, tile_count), BF16), totals),
    )


def local_kernel(
    place_ref,
    sender_ref,
    receiver_ref,
    attr_hbm,
    own_hbm,
    w_in_ref,
    bias_ref,
    w_out_ref,
    tiles_ref,
    late_wanted_ref,
    late_pre_ref,
    receivers_ref,
    own_rows_ref,
    sums_ref,
    pre0_hbm,
    pre1_hbm,
    wanted_hbm,
    deliver_hbm,
    own_ref,
    sum0_ref,
    sum1_ref,
    position_ref,
    table_ref,
    rest0_ref,
    rest1_ref,
    rest2_ref,
    rest3_ref,
    sent,
    arrived,
):
    fetches = [
        pltpu.make_async_copy(own_hbm, own_ref, arrived.at[0]),
        pltpu.make_async_copy(attr_hbm, table_ref.at[0 : attr_hbm.shape[0]], arrived.at[1]),
    ]
    for fetch in fetches:
        fetch.start()
    tile_count, tile = sender_ref.shape
    width, edge_count = attr_hbm.shape
    merged, node_dev = own_ref.shape
    eye = jnp.where(
        lax.broadcasted_iota(jnp.int32, (node_dev, node_dev), 0)
        == lax.broadcasted_iota(jnp.int32, (node_dev, node_dev), 1),
        1.0,
        0.0,
    ).astype(BF16)
    senders = sender_ref[...]
    receivers = receiver_ref[...]
    used = receivers >= 0
    is_remote = jnp.where(used & (senders >= node_dev), 1.0, 0.0)
    is_local = jnp.where(used & (senders < node_dev), 1.0, 0.0)
    is_empty = jnp.where(used, 0.0, 1.0)
    remote_rank, remote_total = running_count(is_remote)
    local_rank, local_total = running_count(is_local)
    empty_rank, _ = running_count(is_empty)
    position_ref[...] = jnp.where(
        is_remote > 0.0,
        remote_rank,
        jnp.where(
            is_local > 0.0, remote_total + local_rank, remote_total + local_total + empty_rank
        ),
    )
    remote_tiles = (jnp.sum(is_remote).astype(jnp.int32) + WIDE - 1) // WIDE
    used_tiles = (jnp.sum(1.0 - is_empty).astype(jnp.int32) + WIDE - 1) // WIDE
    late_tiles = jnp.maximum(remote_tiles, LATE_TILES)
    slot = lax.broadcasted_iota(jnp.int32, tiles_ref.shape, 1)
    tiles_ref[...] = jnp.where(slot == 0, late_tiles, place_ref[0])
    for fetch in fetches:
        fetch.wait()
    own_rows_ref[...] = dot_lanes(eye, own_ref[...]).astype(BF16)
    table_ref[width:, :] = jnp.zeros((table_ref.shape[0] - width, edge_count), BF16)
    for index in range(tile_count):
        lanes = slice(index * tile, (index + 1) * tile)
        row = senders[index : index + 1, :]
        table_ref[width : width + 16, lanes] = jnp.concatenate(
            [
                (row // tile).astype(F32),
                (row % tile).astype(F32),
                receivers[index : index + 1, :].astype(F32),
                jnp.zeros((13, tile), F32),
            ],
            axis=0,
        ).astype(BF16)
    w_send = w_in_ref[0:width, :]
    w_recv = w_in_ref[width : 2 * width, :]
    w_attr = w_in_ref[2 * width : 3 * width, :]
    sum0_ref[...] = jnp.zeros_like(sum0_ref)
    sum1_ref[...] = jnp.zeros_like(sum1_ref)

    def arrange(index):
        wanted = lax.broadcasted_iota(jnp.int32, (WIDE, tile), 0).astype(F32) + (
            index * WIDE
        ).astype(F32)
        order = jnp.concatenate(
            [
                jnp.where(position_ref[t : t + 1, :] == wanted, 1.0, 0.0).astype(BF16)
                for t in range(tile_count)
            ],
            axis=1,
        )
        moved = dot_lanes(order, table_ref[...])
        receiver_row = dot_lanes(table_ref[width : width + 16, :], order)[2:3, :]
        sender_column = moved[:, width : width + 1] * tile + moved[:, width + 1 : width + 2]
        receiver_column = moved[:, width + 2 : width + 3]
        own = own_rows_ref[...]
        send_rows = dot(onehot(sender_column, node_dev), own).astype(BF16)
        recv_rows = dot(onehot(receiver_column, node_dev), own).astype(BF16)
        base = dot(moved[:, :width].astype(BF16), w_attr) + bias_ref[...]
        send0, send1 = level_pair(send_rows, w_send)
        recv0, recv1 = level_pair(recv_rows, w_recv)
        nodes = lax.broadcasted_iota(jnp.int32, (node_dev, WIDE), 0).astype(F32)
        deliver = jnp.where(nodes == receiver_row, 1.0, 0.0).astype(BF16)
        return (
            base + send0 + recv0,
            base + send1 + recv1,
            deliver,
            sender_column - node_dev,
            receiver_row,
        )

    @pl.loop(0, LATE_TILES)
    def _(index):
        pre0, pre1, _, wanted, receiver_row = arrange(index)
        rows = pl.ds(pl.multiple_of(index * WIDE, WIDE), WIDE)
        put_pair(late_pre_ref, rows, pre0, pre1)
        receivers_ref[index] = jnp.broadcast_to(receiver_row, receivers_ref.shape[1:])
        late_wanted_ref[rows, :] = jnp.broadcast_to(wanted, (WIDE, 128))

    @pl.loop(LATE_TILES, late_tiles)
    def _(index):
        rest0_ref[...], rest1_ref[...], rest3_ref[0], wanted, _ = arrange(index)
        rest2_ref[...] = jnp.broadcast_to(wanted, rest2_ref.shape)
        sends = [
            pltpu.make_async_copy(source, target.at[index - LATE_TILES], sent.at[slot])
            for slot, (source, target) in enumerate(
                (
                    (rest0_ref, pre0_hbm),
                    (rest1_ref, pre1_hbm),
                    (rest2_ref, wanted_hbm),
                    (rest3_ref.at[0], deliver_hbm),
                )
            )
        ]
        for send in sends:
            send.start()
        for send in sends:
            send.wait()

    @pl.loop(late_tiles, jnp.maximum(used_tiles, late_tiles))
    def _(index):
        pre0, pre1, deliver, _, _ = arrange(index)
        w_out = w_out_ref[...]
        sum0_ref[...] += dot(deliver, dot(silu(pre0).astype(BF16), w_out).astype(BF16))
        sum1_ref[...] += dot(deliver, dot(silu(pre1).astype(BF16), w_out).astype(BF16))

    put_pair(sums_ref, slice(None), sum0_ref[...], sum1_ref[...])


def edge_kernel(
    tiles_ref,
    late_wanted_ref,
    receivers_ref,
    late_pre_hbm,
    own_hbm,
    sums_hbm,
    pre0_hbm,
    pre1_hbm,
    wanted_hbm,
    deliver_hbm,
    w_in_ref,
    w_out_ref,
    node_w_in_ref,
    node_bias_ref,
    node_w_out_ref,
    node_gain_ref,
    attention_gain_ref,
    remote_ref,
    state_ref,
    out0_ref,
    out1_ref,
    out2_ref,
    out3_ref,
    normed_ref,
    late_pre_ref,
    sums_ref,
    own_ref,
    total0_ref,
    total1_ref,
    rest0_ref,
    rest1_ref,
    rest2_ref,
    rest3_ref,
    early_arrived,
    arrived,
):
    width = w_out_ref.shape[0]
    early = [
        pltpu.make_async_copy(source, target, early_arrived.at[slot])
        for slot, (source, target) in enumerate(
            (
                (late_pre_hbm, late_pre_ref),
                (sums_hbm, sums_ref),
                (own_hbm, own_ref),
            )
        )
    ]
    for fetch in early:
        fetch.start()
    w_send = w_in_ref[0:width, :]

    def gather(wanted):
        lanes = lax.broadcasted_iota(jnp.int32, wanted.shape, 1).astype(F32)
        pick = jnp.concatenate(
            [
                jnp.where(wanted == lanes + float(first), 1.0, 0.0).astype(BF16)
                for first in range(0, remote_ref.shape[0], 128)
            ],
            axis=1,
        )
        return level_pair(dot(pick, remote_ref[...]).astype(BF16), w_send)

    def messages(pre, sent):
        return dot(silu(pre + sent).astype(BF16), w_out_ref[...]).astype(BF16)

    sent0, sent1 = gather(late_wanted_ref[...])
    early[0].wait()
    late_pre0, late_pre1 = get_pair(late_pre_ref)
    message0 = messages(late_pre0, sent0)
    message1 = messages(late_pre1, sent1)
    nodes = lax.broadcasted_iota(jnp.int32, (state_ref.shape[0], WIDE), 0).astype(F32)
    deliver = jnp.concatenate(
        [
            jnp.where(nodes == receivers_ref[block][0:1, :], 1.0, 0.0).astype(BF16)
            for block in range(LATE_TILES)
        ],
        axis=1,
    )
    arrived0, arrived1 = dot(deliver, message0), dot(deliver, message1)
    for fetch in early[1:]:
        fetch.wait()
    sum0, sum1 = get_pair(sums_ref)
    total0_ref[...] = sum0 + arrived0
    total1_ref[...] = sum1 + arrived1

    @pl.loop(LATE_TILES, tiles_ref[0, 0])
    def _(index):
        fetches = [
            pltpu.make_async_copy(source.at[index - LATE_TILES], target, arrived.at[slot])
            for slot, (source, target) in enumerate(
                (
                    (pre0_hbm, rest0_ref),
                    (pre1_hbm, rest1_ref),
                    (wanted_hbm, rest2_ref),
                    (deliver_hbm, rest3_ref.at[0]),
                )
            )
        ]
        for fetch in fetches:
            fetch.start()
        for fetch in fetches:
            fetch.wait()
        sent0, sent1 = gather(rest2_ref[...])
        total0_ref[...] += dot(rest3_ref[0], messages(rest0_ref[...], sent0))
        total1_ref[...] += dot(rest3_ref[0], messages(rest1_ref[...], sent1))

    own = own_ref[...]
    own_pair = [
        rows + node_bias_ref[...] for rows in level_pair(own, node_w_in_ref[0:width, :])
    ]
    own_values = (own[:, :width], own[:, width:])
    levels = range(2)
    summed = [total0_ref[...].astype(BF16), total1_ref[...].astype(BF16)]
    w_summed = node_w_in_ref[width : 2 * width, :]
    node_pre = [own_pair[level] + dot(summed[level], w_summed) for level in levels]
    hidden = [silu(node_pre[level]).astype(BF16) for level in levels]
    update = [dot(hidden[level], node_w_out_ref[...]) for level in levels]
    update = normalize_all(update)
    states = [
        (own_values[level].astype(F32) + node_gain_ref[...] * update[level]).astype(BF16)
        for level in levels
    ]
    normed = normalize_all([state.astype(F32) for state in states])
    normed = [(attention_gain_ref[...] * rows).astype(BF16) for rows in normed]
    state_ref[...] = merge_levels(*states)
    normed_ref[...] = merge_levels(*normed)
    share = out0_ref.shape[0]
    place = tiles_ref[0, 1]
    for shift, out_ref in enumerate((out0_ref, out1_ref, out2_ref, out3_ref)):
        block = lax.rem(place + shift, CHIPS)
        out_ref[...] = normed_ref[pl.ds(pl.multiple_of(block * share, share), share), :]


def attention_kernel(*refs):
    block_refs, refs = refs[: CHIPS * CORES], refs[CHIPS * CORES :]
    bias_ref, query_ref, key_ref, value_ref, *out_refs, mix_ref = refs
    block_count = len(block_refs)
    item_count, merged = block_refs[0].shape
    width = merged // 2
    head_width = width // HEADS
    scale = 1.0 / math.sqrt(head_width)
    key_total = 2 * block_count * CHUNK
    query_total = 2 * CHIPS * CHUNK
    head_of = lax.broadcasted_iota(jnp.int32, (1, width), 1) // head_width
    in_head = [jnp.where(head_of == head, 1.0, 0.0) for head in range(HEADS)]
    same_node = (
        lax.broadcasted_iota(jnp.int32, (HEADS * query_total, key_total), 0) % CHUNK
        == lax.broadcasted_iota(jnp.int32, (HEADS * query_total, key_total), 1) % CHUNK
    )
    blocks = jnp.concatenate([ref[...] for ref in block_refs], axis=0)

    def project(count, weight):
        return [
            p.reshape(count, item_count, weight.shape[1])
            for p in level_pair(blocks[: count * item_count], weight)
        ]

    def rows_of(pair, part):
        items = slice(part * CHUNK, (part + 1) * CHUNK)
        return jnp.concatenate(
            [p[:, items, :].reshape(-1, p.shape[2]) for p in pair], axis=0
        ).astype(BF16)

    queries = project(CHIPS, query_ref[...])
    keys = project(block_count, key_ref[...])
    wide_value = jnp.concatenate(
        [value_ref[...], jnp.zeros((width, WIDE - width), BF16)], axis=1
    )
    lanes = lax.broadcasted_iota(jnp.int32, (1, 1, WIDE), 2)
    values = [p + jnp.where(lanes < width, 0.0, 1.0) for p in project(block_count, wide_value)]
    parts = range(item_count // CHUNK)
    headed = [rows_of(queries, part) for part in parts]
    headed = [
        jnp.concatenate([rows * mask.astype(BF16) for mask in in_head], axis=0) for rows in headed
    ]
    scores = [dot_lanes(headed[part], rows_of(keys, part)) for part in parts]
    scores = [
        scores[part] * scale + jnp.where(same_node, bias_ref[part], -1e30) for part in parts
    ]
    tops = [jnp.max(part_scores, axis=-1, keepdims=True) for part_scores in scores]
    powers = [jnp.exp(scores[part] - tops[part]).astype(BF16) for part in parts]
    mixes = [dot(powers[part], rows_of(values, part)) for part in parts]
    for part, mix in enumerate(mixes):
        mix = mix[:, :width] * (1.0 / mix[:, width : width + 1])
        attended = sum(
            mix[head * query_total : (head + 1) * query_total] * mask
            for head, mask in enumerate(in_head)
        )
        mix_ref[:, :, part * CHUNK : (part + 1) * CHUNK, :] = attended.reshape(
            2, CHIPS, CHUNK, width
        )
    for chip, out_ref in enumerate(out_refs):
        out_ref[...] = merge_levels(mix_ref[0, chip].astype(BF16), mix_ref[1, chip].astype(BF16))


def output_kernel(
    place_ref, state_ref, part0_ref, part1_ref, part2_ref, part3_ref, live_ref, weight_ref, out_hbm,
    attended_ref, out_ref, sent,
):
    width = weight_ref.shape[0]
    share = part0_ref.shape[0]
    place = place_ref[0, 1]
    for shift, part_ref in enumerate((part0_ref, part1_ref, part2_ref, part3_ref)):
        block = lax.rem(place + shift, CHIPS)
        attended_ref[pl.ds(pl.multiple_of(block * share, share), share), :] = part_ref[...]
    mixed = level_pair(attended_ref[...], weight_ref[...])
    state = state_ref[...].astype(F32)
    sends = []
    for level in range(2):
        live_part = mixed[level] * live_ref[:, level : level + 1]
        result = state[:, level * width : (level + 1) * width] + live_part
        out_ref[level] = result.T.astype(BF16)
        sends.append(pltpu.make_async_copy(out_ref.at[level], out_hbm.at[level], sent.at[level]))
        sends[-1].start()
    for send in sends:
        send.wait()


def call(kernel, out_shape, *operands, scratch=(), **specs):
    return pl.pallas_call(
        kernel,
        out_shape=out_shape,
        **specs,
        scratch_shapes=list(scratch),
        compiler_params=pltpu.CompilerParams(vmem_limit_bytes=VMEM_BYTES),
    )(*operands)


def shape(dims, dtype=BF16):
    return jax.ShapeDtypeStruct(dims, dtype)


def kept(array):
    return pltpu.with_memory_space_constraint(array, pltpu.VMEM)


def in_hbm(array):
    return pltpu.with_memory_space_constraint(array, pltpu.HBM)


IN_SMEM = pl.BlockSpec(memory_space=pltpu.SMEM)
IN_VMEM = pl.BlockSpec(memory_space=pltpu.VMEM)
ANYWHERE = pl.BlockSpec(memory_space=pl.ANY)


def per_device(
    node_state,
    edge_attr,
    edge_sender,
    edge_receiver,
    tile_block,
    halo_rows,
    valid_levels,
    edge_w_in,
    edge_bias,
    edge_w_out,
    node_w_in,
    node_bias,
    node_w_out,
    node_gain,
    attention_gain,
    query_weight,
    key_weight,
    value_weight,
    output_weight,
):
    group_count = lax.axis_size("lev")
    node_dev, lev_dev, width = node_state.shape
    tile_count = tile_block.shape[0]
    patch_count, slot_count = halo_rows.shape
    merged = lev_dev * width
    remote_count = patch_count * slot_count
    edge_count = edge_attr.shape[0]
    own = node_state.transpose(1, 2, 0).reshape(merged, node_dev)
    outgoing = call(
        halo_kernel,
        shape((remote_count, merged)),
        in_hbm(halo_rows),
        in_hbm(own),
        in_specs=[ANYWHERE] * 2,
        out_specs=ANYWHERE,
        scratch=[
            pltpu.VMEM((patch_count, slot_count), jnp.int32),
            pltpu.VMEM((merged, node_dev), BF16),
            pltpu.VMEM((remote_count, merged), BF16),
            pltpu.SemaphoreType.DMA((2,)),
            pltpu.SemaphoreType.DMA((4,)),
        ],
    )
    incoming = lax.all_to_all(
        outgoing.reshape(patch_count, slot_count, merged),
        "patch",
        split_axis=0,
        concat_axis=0,
        tiled=True,
    ).reshape(remote_count, merged)

    senders = edge_sender.reshape(tile_count, 128)
    in_block = edge_receiver.reshape(tile_count, 128)
    receivers = jnp.where(in_block >= 0, tile_block[:, None] * 128 + in_block, -1)
    share = node_dev // CHIPS
    me = lax.axis_index("lev")
    chip, core = me // CORES, me % CORES
    mine = lax.dynamic_slice_in_dim(valid_levels, chip * share, share)
    block = jnp.arange(CHIPS * CORES, dtype=jnp.int32)
    from_chip = (chip - block % CHIPS) % CHIPS
    from_core = jnp.where(block < CHIPS, core, 1 - core)
    level_of = (
        ((from_chip * CORES + from_core) * lev_dev)[None, :, None]
        + jnp.arange(lev_dev, dtype=jnp.int32)[:, None, None]
    )
    key_bias = jnp.where(
        level_of[None] < mine.reshape(share // CHUNK, 1, 1, CHUNK), 0.0, -1e30
    ).reshape(share // CHUNK, 1, lev_dev * group_count * CHUNK)
    levels = me * lev_dev + jnp.arange(lev_dev, dtype=jnp.int32)
    live = (levels[None, :] < valid_levels[:, None]).astype(F32)

    rest = edge_count // WIDE - LATE_TILES
    late = LATE_TILES * WIDE
    rest_shapes = [
        ((WIDE, width), F32),
        ((WIDE, width), F32),
        ((WIDE, 128), F32),
        ((1, node_dev, WIDE), BF16),
    ]
    tiles, wanted, late_pre, late_receivers, *tail = call(
        local_kernel,
        (
            pltpu.VMEM((8, 128), jnp.int32),
            pltpu.VMEM((late, 128), F32),
            pltpu.HBM((late, merged), F32),
            pltpu.VMEM((LATE_TILES, 8, WIDE), F32),
            pltpu.HBM((node_dev, merged), BF16),
            pltpu.HBM((node_dev, merged), F32),
            pltpu.HBM((rest, WIDE, width), F32),
            pltpu.HBM((rest, WIDE, width), F32),
            pltpu.HBM((rest, WIDE, 128), F32),
            pltpu.HBM((rest, node_dev, WIDE), BF16),
        ),
        chip.reshape(1),
        senders,
        receivers,
        in_hbm(edge_attr.T),
        in_hbm(own),
        edge_w_in,
        edge_bias[None, :],
        edge_w_out,
        scratch=[
            pltpu.VMEM((merged, node_dev), BF16),
            pltpu.VMEM((node_dev, width), F32),
            pltpu.VMEM((node_dev, width), F32),
            pltpu.VMEM((tile_count, 128), F32),
            pltpu.VMEM((width + 16, edge_count), BF16),
            *(pltpu.VMEM(*entry) for entry in rest_shapes),
            pltpu.SemaphoreType.DMA((4,)),
            pltpu.SemaphoreType.DMA((2,)),
        ],
        in_specs=[IN_SMEM] + [IN_VMEM] * 2 + [ANYWHERE] * 2 + [IN_VMEM] * 3,
        out_specs=[IN_VMEM] * 6 + [ANYWHERE] * 4,
    )
    state, *blocks = call(
        edge_kernel,
        (pltpu.VMEM((node_dev, merged), BF16), *[shape((share, merged))] * CHIPS),
        kept(tiles),
        kept(wanted),
        kept(late_receivers),
        in_hbm(late_pre),
        *(in_hbm(array) for array in tail),
        edge_w_in,
        edge_w_out,
        node_w_in,
        node_bias[None, :],
        node_w_out,
        node_gain[None, :],
        attention_gain[None, :],
        incoming,
        scratch=[
            pltpu.VMEM((node_dev, merged), BF16),
            pltpu.VMEM((late, merged), F32),
            pltpu.VMEM((node_dev, merged), F32),
            pltpu.VMEM((node_dev, merged), BF16),
            pltpu.VMEM((node_dev, width), F32),
            pltpu.VMEM((node_dev, width), F32),
            *(pltpu.VMEM(*entry) for entry in rest_shapes),
            pltpu.SemaphoreType.DMA((3,)),
            pltpu.SemaphoreType.DMA((4,)),
        ],
        in_specs=[IN_VMEM] * 3 + [ANYWHERE] * 7 + [IN_VMEM] * 8,
    )

    def to_chip(array, shift):
        return lax.ppermute(
            array,
            "lev",
            [
                (a * CORES + b, (a + shift) % CHIPS * CORES + b)
                for a in range(CHIPS)
                for b in range(CORES)
            ],
        )

    def to_core(array):
        return lax.ppermute(array, "lev", [(a, a ^ 1) for a in range(CHIPS * CORES)])

    blocks = blocks[:1] + [to_chip(blocks[shift], shift) for shift in range(1, CHIPS)]
    blocks = blocks + [to_core(array) for array in blocks]
    attended = call(
        attention_kernel,
        [shape((share, merged))] * CHIPS,
        *blocks,
        key_bias,
        query_weight,
        key_weight,
        value_weight,
        scratch=[pltpu.VMEM((lev_dev, CHIPS, share, width), F32)],
    )
    returned = [attended[0]] + [to_chip(attended[shift], -shift) for shift in range(1, CHIPS)]
    out = call(
        output_kernel,
        shape((lev_dev, width, node_dev)),
        kept(tiles),
        kept(state),
        *returned,
        live,
        output_weight,
        scratch=[
            pltpu.VMEM((node_dev, merged), BF16),
            pltpu.VMEM((lev_dev, width, node_dev), BF16),
            pltpu.SemaphoreType.DMA((lev_dev,)),
        ],
        out_specs=ANYWHERE,
    )
    return out.transpose(2, 0, 1)


def solution(mesh):
    in_specs = (
        P("patch", "lev", None),
        P("patch", None),
        P("patch"),
        P("patch"),
        P("patch"),
        P("patch", None),
        P("patch"),
    ) + (P(),) * 12
    out_specs = P("patch", "lev", None)
    return jax.shard_map(
        per_device, mesh=mesh, in_specs=in_specs, out_specs=out_specs, check_vma=False
    )
```

```python
import math

import jax
import jax.numpy as jnp
from jax import lax
from jax.experimental import pallas as pl
from jax.experimental.pallas import tpu as pltpu
from jax.sharding import PartitionSpec as P

HEADS = 4
BF16 = jnp.bfloat16
F32 = jnp.float32
VMEM_BYTES = 20 * 1024 * 1024
WIDE = 256
LATE_TILES = 3
CHUNK = 8
CHIPS = 4
CORES = 2


def dot(a, b):
    return jnp.dot(a, b, preferred_element_type=F32)


def dot_lanes(a, b):
    return lax.dot_general(a, b, (((1,), (1,)), ((), ())), preferred_element_type=F32)


def silu(v):
    half = 0.5 * v
    return half + half * jnp.tanh(half)


def normalize_all(arrays):
    means = [jnp.mean(values, axis=-1, keepdims=True) for values in arrays]
    centered = [values - mean for values, mean in zip(arrays, means, strict=True)]
    spreads = [jnp.mean(values * values, axis=-1, keepdims=True) for values in centered]
    return [
        values * lax.rsqrt(spread + 1e-05)
        for values, spread in zip(centered, spreads, strict=True)
    ]


def onehot(column, width):
    lanes = lax.broadcasted_iota(jnp.int32, (column.shape[0], width), 1).astype(F32)
    return jnp.where(column == lanes, 1.0, 0.0).astype(BF16)


def level_pair(merged, weight):
    depth, width = weight.shape
    half = merged.shape[1] // 2
    cut = half // 128 * 128
    filler = jnp.zeros((half - cut, width), weight.dtype)
    first = jnp.concatenate([weight, filler], axis=0)
    second = jnp.concatenate([filler, weight], axis=0)
    return (
        dot(merged[:, : half + half - cut], first),
        dot(merged[:, cut:], second),
    )


def put_pair(ref, rows, first, second):
    width = first.shape[1]
    ref[rows, 0:width] = first
    ref[rows, WIDE:] = second[:, : 2 * width - WIDE]
    ref[rows, width:WIDE] = second[:, 2 * width - WIDE :]


def get_pair(ref):
    width = ref.shape[1] // 2
    return (
        ref[:, 0:width],
        jnp.concatenate([ref[:, WIDE:], ref[:, width:WIDE]], axis=1),
    )


def merge_levels(first, second):
    return jnp.concatenate([first, second], axis=1)


def halo_kernel(halo_hbm, own_hbm, out_hbm, halo_ref, own_ref, rows_ref, arrived, sent):
    patch_count, slot_count = halo_ref.shape
    fetches = [
        pltpu.make_async_copy(halo_hbm, halo_ref, arrived.at[0]),
        pltpu.make_async_copy(own_hbm, own_ref, arrived.at[1]),
    ]
    for fetch in fetches:
        fetch.start()
    fetches[0].wait()
    columns = halo_ref[...].astype(F32).T
    sends = []
    step = patch_count // 4
    for part in range(4):
        pick = jnp.concatenate(
            [
                onehot(columns[:, patch : patch + 1], own_ref.shape[1])
                for patch in range(part * step, (part + 1) * step)
            ],
            axis=0,
        )
        if part == 0:
            fetches[1].wait()
        rows = slice(part * step * slot_count, (part + 1) * step * slot_count)
        rows_ref[rows, :] = dot_lanes(pick, own_ref[...]).astype(BF16)
        sends.append(
            pltpu.make_async_copy(rows_ref.at[rows], out_hbm.at[rows], sent.at[part])
        )
        sends[-1].start()
    for send in sends:
        send.wait()


def running_count(flags):
    tile_count, tile = flags.shape
    flags = flags.astype(BF16)
    before = lax.broadcasted_iota(jnp.int32, (tile, tile), 0) < lax.broadcasted_iota(
        jnp.int32, (tile, tile), 1
    )
    above = lax.broadcasted_iota(jnp.int32, (tile_count, tile_count), 1) < lax.broadcasted_iota(
        jnp.int32, (tile_count, tile_count), 0
    )
    inside = dot(flags, jnp.where(before, 1.0, 0.0).astype(BF16))
    totals = dot(flags, jnp.ones((tile, tile), BF16)).astype(BF16)
    return (
        inside + dot(jnp.where(above, 1.0, 0.0).astype(BF16), totals),
        dot(jnp.ones((tile_count, tile_count), BF16), totals),
    )


def local_kernel(
    place_ref,
    sender_ref,
    receiver_ref,
    attr_hbm,
    own_hbm,
    w_in_ref,
    bias_ref,
    w_out_ref,
    tiles_ref,
    late_wanted_ref,
    late_pre_ref,
    receivers_ref,
    own_rows_ref,
    sums_ref,
    pre0_hbm,
    pre1_hbm,
    wanted_hbm,
    deliver_hbm,
    own_ref,
    sum0_ref,
    sum1_ref,
    position_ref,
    table_ref,
    rest0_ref,
    rest1_ref,
    rest2_ref,
    rest3_ref,
    sent,
    arrived,
):
    fetches = [
        pltpu.make_async_copy(own_hbm, own_ref, arrived.at[0]),
        pltpu.make_async_copy(attr_hbm, table_ref.at[0 : attr_hbm.shape[0]], arrived.at[1]),
    ]
    for fetch in fetches:
        fetch.start()
    tile_count, tile = sender_ref.shape
    width, edge_count = attr_hbm.shape
    merged, node_dev = own_ref.shape
    eye = jnp.where(
        lax.broadcasted_iota(jnp.int32, (node_dev, node_dev), 0)
        == lax.broadcasted_iota(jnp.int32, (node_dev, node_dev), 1),
        1.0,
        0.0,
    ).astype(BF16)
    senders = sender_ref[...]
    receivers = receiver_ref[...]
    used = receivers >= 0
    is_remote = jnp.where(used & (senders >= node_dev), 1.0, 0.0)
    is_local = jnp.where(used & (senders < node_dev), 1.0, 0.0)
    is_empty = jnp.where(used, 0.0, 1.0)
    remote_rank, remote_total = running_count(is_remote)
    local_rank, local_total = running_count(is_local)
    empty_rank, _ = running_count(is_empty)
    position_ref[...] = jnp.where(
        is_remote > 0.0,
        remote_rank,
        jnp.where(
            is_local > 0.0, remote_total + local_rank, remote_total + local_total + empty_rank
        ),
    )
    remote_tiles = (jnp.sum(is_remote).astype(jnp.int32) + WIDE - 1) // WIDE
    used_tiles = (jnp.sum(1.0 - is_empty).astype(jnp.int32) + WIDE - 1) // WIDE
    late_tiles = jnp.maximum(remote_tiles, LATE_TILES)
    slot = lax.broadcasted_iota(jnp.int32, tiles_ref.shape, 1)
    tiles_ref[...] = jnp.where(slot == 0, late_tiles, place_ref[0])
    for fetch in fetches:
        fetch.wait()
    own_rows_ref[...] = dot_lanes(eye, own_ref[...]).astype(BF16)
    table_ref[width:, :] = jnp.zeros((table_ref.shape[0] - width, edge_count), BF16)
    for index in range(tile_count):
        lanes = slice(index * tile, (index + 1) * tile)
        row = senders[index : index + 1, :]
        table_ref[width : width + 16, lanes] = jnp.concatenate(
            [
                (row // tile).astype(F32),
                (row % tile).astype(F32),
                receivers[index : index + 1, :].astype(F32),
                jnp.zeros((13, tile), F32),
            ],
            axis=0,
        ).astype(BF16)
    w_send = w_in_ref[0:width, :]
    w_recv = w_in_ref[width : 2 * width, :]
    w_attr = w_in_ref[2 * width : 3 * width, :]
    sum0_ref[...] = jnp.zeros_like(sum0_ref)
    sum1_ref[...] = jnp.zeros_like(sum1_ref)

    def arrange(index):
        wanted = lax.broadcasted_iota(jnp.int32, (WIDE, tile), 0).astype(F32) + (
            index * WIDE
        ).astype(F32)
        order = jnp.concatenate(
            [
                jnp.where(position_ref[t : t + 1, :] == wanted, 1.0, 0.0).astype(BF16)
                for t in range(tile_count)
            ],
            axis=1,
        )
        moved = dot_lanes(order, table_ref[...])
        receiver_row = dot_lanes(table_ref[width : width + 16, :], order)[2:3, :]
        sender_column = moved[:, width : width + 1] * tile + moved[:, width + 1 : width + 2]
        receiver_column = moved[:, width + 2 : width + 3]
        own = own_rows_ref[...]
        send_rows = dot(onehot(sender_column, node_dev), own).astype(BF16)
        recv_rows = dot(onehot(receiver_column, node_dev), own).astype(BF16)
        base = dot(moved[:, :width].astype(BF16), w_attr) + bias_ref[...]
        send0, send1 = level_pair(send_rows, w_send)
        recv0, recv1 = level_pair(recv_rows, w_recv)
        nodes = lax.broadcasted_iota(jnp.int32, (node_dev, WIDE), 0).astype(F32)
        deliver = jnp.where(nodes == receiver_row, 1.0, 0.0).astype(BF16)
        return (
            base + send0 + recv0,
            base + send1 + recv1,
            deliver,
            sender_column - node_dev,
            receiver_row,
        )

    @pl.loop(0, LATE_TILES)
    def _(index):
        pre0, pre1, _, wanted, receiver_row = arrange(index)
        rows = pl.ds(pl.multiple_of(index * WIDE, WIDE), WIDE)
        put_pair(late_pre_ref, rows, pre0, pre1)
        receivers_ref[index] = jnp.broadcast_to(receiver_row, receivers_ref.shape[1:])
        late_wanted_ref[rows, :] = jnp.broadcast_to(wanted, (WIDE, 128))

    @pl.loop(LATE_TILES, late_tiles)
    def _(index):
        rest0_ref[...], rest1_ref[...], rest3_ref[0], wanted, _ = arrange(index)
        rest2_ref[...] = jnp.broadcast_to(wanted, rest2_ref.shape)
        sends = [
            pltpu.make_async_copy(source, target.at[index - LATE_TILES], sent.at[slot])
            for slot, (source, target) in enumerate(
                (
                    (rest0_ref, pre0_hbm),
                    (rest1_ref, pre1_hbm),
                    (rest2_ref, wanted_hbm),
                    (rest3_ref.at[0], deliver_hbm),
                )
            )
        ]
        for send in sends:
            send.start()
        for send in sends:
            send.wait()

    @pl.loop(late_tiles, jnp.maximum(used_tiles, late_tiles))
    def _(index):
        pre0, pre1, deliver, _, _ = arrange(index)
        w_out = w_out_ref[...]
        sum0_ref[...] += dot(deliver, dot(silu(pre0).astype(BF16), w_out).astype(BF16))
        sum1_ref[...] += dot(deliver, dot(silu(pre1).astype(BF16), w_out).astype(BF16))

    put_pair(sums_ref, slice(None), sum0_ref[...], sum1_ref[...])


def edge_kernel(
    tiles_ref,
    late_wanted_ref,
    receivers_ref,
    late_pre_hbm,
    own_hbm,
    sums_hbm,
    pre0_hbm,
    pre1_hbm,
    wanted_hbm,
    deliver_hbm,
    w_in_ref,
    w_out_ref,
    node_w_in_ref,
    node_bias_ref,
    node_w_out_ref,
    node_gain_ref,
    attention_gain_ref,
    remote_ref,
    state_ref,
    out0_ref,
    out1_ref,
    out2_ref,
    out3_ref,
    normed_ref,
    late_pre_ref,
    sums_ref,
    own_ref,
    total0_ref,
    total1_ref,
    rest0_ref,
    rest1_ref,
    rest2_ref,
    rest3_ref,
    early_arrived,
    arrived,
):
    width = w_out_ref.shape[0]
    early = [
        pltpu.make_async_copy(source, target, early_arrived.at[slot])
        for slot, (source, target) in enumerate(
            (
                (late_pre_hbm, late_pre_ref),
                (sums_hbm, sums_ref),
                (own_hbm, own_ref),
            )
        )
    ]
    for fetch in early:
        fetch.start()
    w_send = w_in_ref[0:width, :]

    def gather(wanted):
        lanes = lax.broadcasted_iota(jnp.int32, wanted.shape, 1).astype(F32)
        pick = jnp.concatenate(
            [
                jnp.where(wanted == lanes + float(first), 1.0, 0.0).astype(BF16)
                for first in range(0, remote_ref.shape[0], 128)
            ],
            axis=1,
        )
        return level_pair(dot(pick, remote_ref[...]).astype(BF16), w_send)

    def messages(pre, sent):
        return dot(silu(pre + sent).astype(BF16), w_out_ref[...]).astype(BF16)

    sent0, sent1 = gather(late_wanted_ref[...])
    nodes = lax.broadcasted_iota(jnp.int32, (state_ref.shape[0], WIDE), 0).astype(F32)
    deliver = jnp.concatenate(
        [
            jnp.where(nodes == receivers_ref[block][0:1, :], 1.0, 0.0).astype(BF16)
            for block in range(LATE_TILES)
        ],
        axis=1,
    )
    early[0].wait()
    late_pre0, late_pre1 = get_pair(late_pre_ref)
    message0 = messages(late_pre0, sent0)
    message1 = messages(late_pre1, sent1)
    arrived0, arrived1 = dot(deliver, message0), dot(deliver, message1)
    for fetch in early[1:]:
        fetch.wait()
    sum0, sum1 = get_pair(sums_ref)
    total0_ref[...] = sum0 + arrived0
    total1_ref[...] = sum1 + arrived1

    @pl.loop(LATE_TILES, tiles_ref[0, 0])
    def _(index):
        fetches = [
            pltpu.make_async_copy(source.at[index - LATE_TILES], target, arrived.at[slot])
            for slot, (source, target) in enumerate(
                (
                    (pre0_hbm, rest0_ref),
                    (pre1_hbm, rest1_ref),
                    (wanted_hbm, rest2_ref),
                    (deliver_hbm, rest3_ref.at[0]),
                )
            )
        ]
        for fetch in fetches:
            fetch.start()
        for fetch in fetches:
            fetch.wait()
        sent0, sent1 = gather(rest2_ref[...])
        total0_ref[...] += dot(rest3_ref[0], messages(rest0_ref[...], sent0))
        total1_ref[...] += dot(rest3_ref[0], messages(rest1_ref[...], sent1))

    own = own_ref[...]
    own_pair = [
        rows + node_bias_ref[...] for rows in level_pair(own, node_w_in_ref[0:width, :])
    ]
    own_values = (own[:, :width], own[:, width:])
    levels = range(2)
    summed = [total0_ref[...].astype(BF16), total1_ref[...].astype(BF16)]
    w_summed = node_w_in_ref[width : 2 * width, :]
    node_pre = [own_pair[level] + dot(summed[level], w_summed) for level in levels]
    hidden = [silu(node_pre[level]).astype(BF16) for level in levels]
    update = [dot(hidden[level], node_w_out_ref[...]) for level in levels]
    update = normalize_all(update)
    states = [
        (own_values[level].astype(F32) + node_gain_ref[...] * update[level]).astype(BF16)
        for level in levels
    ]
    normed = normalize_all([state.astype(F32) for state in states])
    normed = [(attention_gain_ref[...] * rows).astype(BF16) for rows in normed]
    state_ref[...] = merge_levels(*states)
    normed_ref[...] = merge_levels(*normed)
    share = out0_ref.shape[0]
    place = tiles_ref[0, 1]
    for shift, out_ref in enumerate((out0_ref, out1_ref, out2_ref, out3_ref)):
        block = lax.rem(place + shift, CHIPS)
        out_ref[...] = normed_ref[pl.ds(pl.multiple_of(block * share, share), share), :]


def attention_kernel(*refs):
    block_refs, refs = refs[: CHIPS * CORES], refs[CHIPS * CORES :]
    bias_ref, query_ref, key_ref, value_ref, *out_refs, mix_ref = refs
    block_count = len(block_refs)
    item_count, merged = block_refs[0].shape
    width = merged // 2
    head_width = width // HEADS
    scale = 1.0 / math.sqrt(head_width)
    key_total = 2 * block_count * CHUNK
    query_total = 2 * CHIPS * CHUNK
    head_of = lax.broadcasted_iota(jnp.int32, (1, width), 1) // head_width
    in_head = [jnp.where(head_of == head, 1.0, 0.0) for head in range(HEADS)]
    same_node = (
        lax.broadcasted_iota(jnp.int32, (HEADS * query_total, key_total), 0) % CHUNK
        == lax.broadcasted_iota(jnp.int32, (HEADS * query_total, key_total), 1) % CHUNK
    )
    blocks = jnp.concatenate([ref[...] for ref in block_refs], axis=0)

    def project(count, weight):
        return [
            p.reshape(count, item_count, weight.shape[1])
            for p in level_pair(blocks[: count * item_count], weight)
        ]

    def rows_of(pair, part):
        items = slice(part * CHUNK, (part + 1) * CHUNK)
        return jnp.concatenate(
            [p[:, items, :].reshape(-1, p.shape[2]) for p in pair], axis=0
        ).astype(BF16)

    queries = project(CHIPS, query_ref[...])
    keys = project(block_count, key_ref[...])
    wide_value = jnp.concatenate(
        [value_ref[...], jnp.zeros((width, WIDE - width), BF16)], axis=1
    )
    lanes = lax.broadcasted_iota(jnp.int32, (1, 1, WIDE), 2)
    values = [p + jnp.where(lanes < width, 0.0, 1.0) for p in project(block_count, wide_value)]
    parts = range(item_count // CHUNK)
    headed = [rows_of(queries, part) for part in parts]
    headed = [
        jnp.concatenate([rows * mask.astype(BF16) for mask in in_head], axis=0) for rows in headed
    ]
    scores = [dot_lanes(headed[part], rows_of(keys, part)) for part in parts]
    scores = [
        scores[part] * scale + jnp.where(same_node, bias_ref[part], -1e30) for part in parts
    ]
    tops = [jnp.max(part_scores, axis=-1, keepdims=True) for part_scores in scores]
    powers = [jnp.exp(scores[part] - tops[part]).astype(BF16) for part in parts]
    mixes = [dot(powers[part], rows_of(values, part)) for part in parts]
    for part, mix in enumerate(mixes):
        mix = mix[:, :width] * (1.0 / mix[:, width : width + 1])
        attended = sum(
            mix[head * query_total : (head + 1) * query_total] * mask
            for head, mask in enumerate(in_head)
        )
        mix_ref[:, :, part * CHUNK : (part + 1) * CHUNK, :] = attended.reshape(
            2, CHIPS, CHUNK, width
        )
    for chip, out_ref in enumerate(out_refs):
        out_ref[...] = merge_levels(mix_ref[0, chip].astype(BF16), mix_ref[1, chip].astype(BF16))


def output_kernel(
    place_ref, state_ref, part0_ref, part1_ref, part2_ref, part3_ref, live_ref, weight_ref, out_hbm,
    attended_ref, out_ref, sent,
):
    width = weight_ref.shape[0]
    share = part0_ref.shape[0]
    place = place_ref[0, 1]
    for shift, part_ref in enumerate((part0_ref, part1_ref, part2_ref, part3_ref)):
        block = lax.rem(place + shift, CHIPS)
        attended_ref[pl.ds(pl.multiple_of(block * share, share), share), :] = part_ref[...]
    mixed = level_pair(attended_ref[...], weight_ref[...])
    state = state_ref[...].astype(F32)
    sends = []
    for level in range(2):
        live_part = mixed[level] * live_ref[:, level : level + 1]
        result = state[:, level * width : (level + 1) * width] + live_part
        out_ref[level] = result.T.astype(BF16)
        sends.append(pltpu.make_async_copy(out_ref.at[level], out_hbm.at[level], sent.at[level]))
        sends[-1].start()
    for send in sends:
        send.wait()


def call(kernel, out_shape, *operands, scratch=(), **specs):
    return pl.pallas_call(
        kernel,
        out_shape=out_shape,
        **specs,
        scratch_shapes=list(scratch),
        compiler_params=pltpu.CompilerParams(vmem_limit_bytes=VMEM_BYTES),
    )(*operands)


def shape(dims, dtype=BF16):
    return jax.ShapeDtypeStruct(dims, dtype)


def kept(array):
    return pltpu.with_memory_space_constraint(array, pltpu.VMEM)


def in_hbm(array):
    return pltpu.with_memory_space_constraint(array, pltpu.HBM)


IN_SMEM = pl.BlockSpec(memory_space=pltpu.SMEM)
IN_VMEM = pl.BlockSpec(memory_space=pltpu.VMEM)
ANYWHERE = pl.BlockSpec(memory_space=pl.ANY)


def per_device(
    node_state,
    edge_attr,
    edge_sender,
    edge_receiver,
    tile_block,
    halo_rows,
    valid_levels,
    edge_w_in,
    edge_bias,
    edge_w_out,
    node_w_in,
    node_bias,
    node_w_out,
    node_gain,
    attention_gain,
    query_weight,
    key_weight,
    value_weight,
    output_weight,
):
    group_count = lax.axis_size("lev")
    node_dev, lev_dev, width = node_state.shape
    tile_count = tile_block.shape[0]
    patch_count, slot_count = halo_rows.shape
    merged = lev_dev * width
    remote_count = patch_count * slot_count
    edge_count = edge_attr.shape[0]
    own = node_state.transpose(1, 2, 0).reshape(merged, node_dev)
    outgoing = call(
        halo_kernel,
        shape((remote_count, merged)),
        in_hbm(halo_rows),
        in_hbm(own),
        in_specs=[ANYWHERE] * 2,
        out_specs=ANYWHERE,
        scratch=[
            pltpu.VMEM((patch_count, slot_count), jnp.int32),
            pltpu.VMEM((merged, node_dev), BF16),
            pltpu.VMEM((remote_count, merged), BF16),
            pltpu.SemaphoreType.DMA((2,)),
            pltpu.SemaphoreType.DMA((4,)),
        ],
    )
    incoming = lax.all_to_all(
        outgoing.reshape(patch_count, slot_count, merged),
        "patch",
        split_axis=0,
        concat_axis=0,
        tiled=True,
    ).reshape(remote_count, merged)

    senders = edge_sender.reshape(tile_count, 128)
    in_block = edge_receiver.reshape(tile_count, 128)
    receivers = jnp.where(in_block >= 0, tile_block[:, None] * 128 + in_block, -1)
    share = node_dev // CHIPS
    me = lax.axis_index("lev")
    chip, core = me // CORES, me % CORES
    mine = lax.dynamic_slice_in_dim(valid_levels, chip * share, share)
    block = jnp.arange(CHIPS * CORES, dtype=jnp.int32)
    from_chip = (chip - block % CHIPS) % CHIPS
    from_core = jnp.where(block < CHIPS, core, 1 - core)
    level_of = (
        ((from_chip * CORES + from_core) * lev_dev)[None, :, None]
        + jnp.arange(lev_dev, dtype=jnp.int32)[:, None, None]
    )
    key_bias = jnp.where(
        level_of[None] < mine.reshape(share // CHUNK, 1, 1, CHUNK), 0.0, -1e30
    ).reshape(share // CHUNK, 1, lev_dev * group_count * CHUNK)
    levels = me * lev_dev + jnp.arange(lev_dev, dtype=jnp.int32)
    live = (levels[None, :] < valid_levels[:, None]).astype(F32)

    rest = edge_count // WIDE - LATE_TILES
    late = LATE_TILES * WIDE
    rest_shapes = [
        ((WIDE, width), F32),
        ((WIDE, width), F32),
        ((WIDE, 128), F32),
        ((1, node_dev, WIDE), BF16),
    ]
    tiles, wanted, late_pre, late_receivers, *tail = call(
        local_kernel,
        (
            pltpu.VMEM((8, 128), jnp.int32),
            pltpu.VMEM((late, 128), F32),
            pltpu.HBM((late, merged), F32),
            pltpu.VMEM((LATE_TILES, 8, WIDE), F32),
            pltpu.HBM((node_dev, merged), BF16),
            pltpu.HBM((node_dev, merged), F32),
            pltpu.HBM((rest, WIDE, width), F32),
            pltpu.HBM((rest, WIDE, width), F32),
            pltpu.HBM((rest, WIDE, 128), F32),
            pltpu.HBM((rest, node_dev, WIDE), BF16),
        ),
        chip.reshape(1),
        senders,
        receivers,
        in_hbm(edge_attr.T),
        in_hbm(own),
        edge_w_in,
        edge_bias[None, :],
        edge_w_out,
        scratch=[
            pltpu.VMEM((merged, node_dev), BF16),
            pltpu.VMEM((node_dev, width), F32),
            pltpu.VMEM((node_dev, width), F32),
            pltpu.VMEM((tile_count, 128), F32),
            pltpu.VMEM((width + 16, edge_count), BF16),
            *(pltpu.VMEM(*entry) for entry in rest_shapes),
            pltpu.SemaphoreType.DMA((4,)),
            pltpu.SemaphoreType.DMA((2,)),
        ],
        in_specs=[IN_SMEM] + [IN_VMEM] * 2 + [ANYWHERE] * 2 + [IN_VMEM] * 3,
        out_specs=[IN_VMEM] * 6 + [ANYWHERE] * 4,
    )
    state, *blocks = call(
        edge_kernel,
        (pltpu.VMEM((node_dev, merged), BF16), *[shape((share, merged))] * CHIPS),
        kept(tiles),
        kept(wanted),
        kept(late_receivers),
        in_hbm(late_pre),
        *(in_hbm(array) for array in tail),
        edge_w_in,
        edge_w_out,
        node_w_in,
        node_bias[None, :],
        node_w_out,
        node_gain[None, :],
        attention_gain[None, :],
        incoming,
        scratch=[
            pltpu.VMEM((node_dev, merged), BF16),
            pltpu.VMEM((late, merged), F32),
            pltpu.VMEM((node_dev, merged), F32),
            pltpu.VMEM((node_dev, merged), BF16),
            pltpu.VMEM((node_dev, width), F32),
            pltpu.VMEM((node_dev, width), F32),
            *(pltpu.VMEM(*entry) for entry in rest_shapes),
            pltpu.SemaphoreType.DMA((3,)),
            pltpu.SemaphoreType.DMA((4,)),
        ],
        in_specs=[IN_VMEM] * 3 + [ANYWHERE] * 7 + [IN_VMEM] * 8,
    )

    def to_chip(array, shift):
        return lax.ppermute(
            array,
            "lev",
            [
                (a * CORES + b, (a + shift) % CHIPS * CORES + b)
                for a in range(CHIPS)
                for b in range(CORES)
            ],
        )

    def to_core(array):
        return lax.ppermute(array, "lev", [(a, a ^ 1) for a in range(CHIPS * CORES)])

    blocks = blocks[:1] + [to_chip(blocks[shift], shift) for shift in range(1, CHIPS)]
    blocks = blocks + [to_core(array) for array in blocks]
    attended = call(
        attention_kernel,
        [shape((share, merged))] * CHIPS,
        *blocks,
        key_bias,
        query_weight,
        key_weight,
        value_weight,
        scratch=[pltpu.VMEM((lev_dev, CHIPS, share, width), F32)],
    )
    returned = [attended[0]] + [to_chip(attended[shift], -shift) for shift in range(1, CHIPS)]
    out = call(
        output_kernel,
        shape((lev_dev, width, node_dev)),
        kept(tiles),
        kept(state),
        *returned,
        live,
        output_weight,
        scratch=[
            pltpu.VMEM((node_dev, merged), BF16),
            pltpu.VMEM((lev_dev, width, node_dev), BF16),
            pltpu.SemaphoreType.DMA((lev_dev,)),
        ],
        out_specs=ANYWHERE,
    )
    return out.transpose(2, 0, 1)


def solution(mesh):
    in_specs = (
        P("patch", "lev", None),
        P("patch", None),
        P("patch"),
        P("patch"),
        P("patch"),
        P("patch", None),
        P("patch"),
    ) + (P(),) * 12
    out_specs = P("patch", "lev", None)
    return jax.shard_map(
        per_device, mesh=mesh, in_specs=in_specs, out_specs=out_specs, check_vma=False
    )
```
